256 devices in a mesh: role: 4 (over x_lo, core), shard: 64 (over y, z, x_hi).
Axes of the slice: x: 4 (x_hi: 2, x_lo: 2; x = x_hi * 2 + x_lo), y: 4, z: 8, core: 2. Of those that a mesh axis runs over, the one named last changes fastest.
Arguments:
- cls_states: bfloat16 [32768, 768], P(('role', 'shard')), may hold values from -6 to 6
- trainer_in: bfloat16 [4, 3072, 768], P('role', 'shard'), may hold values from -0.21875 to 0.21875
- trainer_out: bfloat16 [4, 3072, 768], P('role', 'shard'), may hold values from -0.109375 to 0.109375
- stale_cache: bfloat16 [65536, 768], P(('role', 'shard')), may hold values from -6 to 6
- block_owner: int32 [16384, 1], P(('role', 'shard')), may hold values from 0 to 63; in each aligned block of 64 rows (0 to 63, 64 to 127, ...) at most 2 rows name the same one
- queries: bfloat16 [256, 768], P(('role', 'shard')), may hold values from -0.4296875 to 0.4296875
- neg_ids: int32 [256, 4096], P('role', 'shard'), may hold values from 0 to 255
- grades: int32 [256, 4096], P('role', 'shard'), may hold values from 0 to 4
Outputs:
- refreshed_cache: bfloat16 [65536, 768], P(('role', 'shard'))
- query_grad: float32 [256, 768], P(('role', 'shard'))
- list_loss: float32 [256], P(('role', 'shard'))
The draws below stay inside these ranges and needn't reach their ends.
Inputs may be any that keep to these rules, and one draw needn't show every extreme that they name: `block_owner`: among the 64 rows of one device at most 2 name the same owner; in every draw some device names some owner exactly 2 times.
All inputs are finite; a program needn't handle non-finite values.
Results may differ from the reference program's by a relative error of at most 0.013.
Values may be sent and summed in bfloat16 or wider, within the bound.
No kernel may reach another device: no remote copies, remote signals or barrier semaphores. Data moves between devices by JAX's collectives and lax.ppermute only.
A program may use at most 64 MiB of HBM per device.

```python
import math
import jax
import jax.numpy as jnp
import numpy as np
from jax import lax

D = 768
FF = 3072
PASS_DEV = 128
NEG = 4096
CAP = 2
NB = 64
BLK = 2
CACHE_DEV = 256
NEG_OWN = 64
Q = 64
PASSAGES = 32768
N_ROLE = 4
N_SHARD = 64
DEVICES = 256


def with_ends(result, stream_key, least, high):
    spot = [jax.random.randint(jax.random.fold_in(stream_key, axis), (), 0, length) for axis, length in enumerate(result.shape)]
    longest = result.shape.index(max(result.shape))
    neighbour = spot[:longest] + [(spot[longest] + 1) % result.shape[longest]] + spot[longest + 1:]
    return result.at[tuple(spot)].set(least).at[tuple(neighbour)].set(high)


def block_levels(stream_key, dims, pieces, smallest, high):
    loudness = 1.0
    for axis_at, shards_of in pieces:
        draws = jax.random.uniform(jax.random.fold_in(jax.random.fold_in(stream_key, 6), axis_at), (shards_of,), jnp.float32, smallest / len(pieces), high / len(pieces))
        loudness = loudness * jnp.repeat(jnp.exp(draws), dims[axis_at] // shards_of).reshape((-1,) + (1,) * (len(dims) - 1 - axis_at))
    return loudness


def deal_out(stream_key, own, number, rows, count, top, reach, skew):
    sequence = jax.random.permutation(stream_key, count)
    crowded, common = load_shares(count, rows * top, reach, skew, True), load_shares(count, rows * top, reach, skew, False)
    places = jnp.arange(count)

    def named(sizes, rotation):
        used = int((sizes > 0).sum())
        fixed = max(1, used // 4)
        moved = fixed + (places - fixed + rotation * (used - fixed)) % max(1, count - fixed)
        return jnp.zeros((count,), jnp.int32).at[sequence[jnp.where(places < fixed, places, moved)]].set(jnp.asarray(sizes, jnp.int32))

    sizes = jnp.where(number % 4 == 0, named(crowded, number // 4), named(common, number - number // 4 - 1))
    mixed = jax.random.permutation(jax.random.fold_in(own, 3), count)
    giver, receiver = mixed[0:count // 2 * 2:2], mixed[1:count // 2 * 2:2]
    margin = jnp.minimum(sizes[giver] - 1, reach - sizes[receiver]) // 2
    margin = jnp.where((giver == sequence[0]) | (receiver == sequence[0]) | (sizes[receiver] == 0), 0, jnp.maximum(margin, 0))
    moved = jax.random.randint(jax.random.fold_in(own, 4), (count // 2,), 0, 1 << 20) % (margin + 1)
    sizes = sizes.at[giver].add(-moved).at[receiver].add(moved)
    labels = jnp.searchsorted(jnp.cumsum(sizes), jnp.arange(rows * top), side="right").astype(jnp.int32)
    grid = labels.reshape(top, rows).T
    grid = grid[jax.random.permutation(jax.random.fold_in(own, 1), rows)]
    rotation = jax.random.randint(jax.random.fold_in(own, 2), (rows, 1), 0, top)
    return jnp.take_along_axis(grid, (jnp.arange(top)[None, :] + rotation) % top, axis=1)


def load_shares(count, total, reach, skew, full):
    weights = [(1 << 20) // math.isqrt(standing ** skew) + 1 for standing in range(1, count + 1)]
    largest = reach if full else min(reach, max(-(-total // count), total * weights[0] // sum(weights)))
    least = 1 if total - largest >= count - 1 else 0
    given, spare = [largest] + [least] * (count - 1), total - largest - least * (count - 1)
    while spare > 0:
        candidates = [i for i in range(1, count) if given[i] < largest] or [i for i in range(1, count) if given[i] < reach]
        mass, remaining = sum([weights[i] for i in candidates]), spare
        for i in candidates:
            extra = min(reach - given[i], max(1, remaining * weights[i] // mass), spare)
            given[i] = given[i] + extra
            spare = spare - extra
    return np.array(given)


def normal_values(own_key, extent, scale, most, split=(), kind=jnp.bfloat16):
    entries = scale * jax.random.normal(own_key, extent, jnp.float32)
    if split:
        entries = entries * block_levels(own_key, extent, split, -0.22, 0.18)
    return jnp.clip(entries, -most, most).astype(kind)


def setup_inputs(seed: int = 0) -> dict:
    keys = jax.random.split(jax.random.key(seed), 9)
    cls_states = normal_values(keys[0], (PASSAGES, D), 1.0, 6.0, ((0, 256),))
    trainer_in = normal_values(keys[1], (N_ROLE, FF, D), D ** -0.5, 0.21875, ((0, 4), (1, 64)))
    trainer_out = normal_values(keys[2], (N_ROLE, FF, D), FF ** -0.5, 0.109375, ((0, 4), (1, 64)))
    stale_cache = normal_values(keys[3], (DEVICES * CACHE_DEV, D), 1.0, 6.0, ((0, 256),))
    block_owner_keys = jax.random.split(jax.random.fold_in(keys[4], 1), (DEVICES * NB) // NB)
    block_owner_turns = jax.random.permutation(jax.random.fold_in(keys[4], 3), (DEVICES * NB) // NB)
    block_owner = jax.vmap(lambda own, number: deal_out(jax.random.fold_in(keys[4], 2), own, number, NB, N_SHARD, 1, CAP, 2))(block_owner_keys, block_owner_turns).reshape((DEVICES * NB, 1))
    queries = normal_values(keys[5], (N_ROLE * Q, D), 0.072, 0.4296875, ((0, 256),))
    neg_ids = with_ends(jax.random.randint(keys[6], (N_ROLE * Q, NEG), 0, CACHE_DEV), jax.random.fold_in(keys[6], 1), 0, CACHE_DEV - 1).astype(jnp.int32)
    grades = with_ends(jax.random.randint(keys[7], (N_ROLE * Q, NEG), 0, 5), jax.random.fold_in(keys[7], 1), 0, 4).astype(jnp.int32)
    return dict(cls_states=cls_states, trainer_in=trainer_in, trainer_out=trainer_out, stale_cache=stale_cache, block_owner=block_owner, queries=queries, neg_ids=neg_ids, grades=grades)


EPSILON = 1e-05
LOG_TWO = math.log(2.0)

def encode(states, weight_in, weight_out):
    inner = jnp.dot(states, weight_in.T, preferred_element_type=jnp.float32)
    hidden = jax.nn.gelu(inner, approximate=False).astype(jnp.bfloat16)
    ffn = jnp.dot(hidden, weight_out, preferred_element_type=jnp.float32)
    resid = states.astype(jnp.float32) + ffn
    average = lax.optimization_barrier(jnp.mean(resid, -1, keepdims=True))
    centred = resid - average
    variance = lax.optimization_barrier(jnp.mean(centred * centred, -1, keepdims=True))
    return (centred * lax.rsqrt(variance + EPSILON)).astype(jnp.bfloat16)

def reference(cls_states, trainer_in, trainer_out, stale_cache, block_owner, queries, neg_ids, grades):
    weight_in = trainer_in[N_ROLE - 1]
    weight_out = trainer_out[N_ROLE - 1]
    groups = N_ROLE * N_SHARD
    fresh = lax.map(lambda states: encode(states, weight_in, weight_out), cls_states.reshape(groups, PASS_DEV, D))
    blocks = fresh.reshape(N_ROLE, N_SHARD, NB, BLK, D)
    owner = block_owner.reshape(N_ROLE, N_SHARD, NB)
    onehot = (owner[..., None] == jnp.arange(N_SHARD, dtype=jnp.int32)).astype(jnp.int32)
    earlier = jnp.cumsum(onehot, axis=2) - onehot
    slot = lax.optimization_barrier(jnp.sum(earlier * onehot, -1)).astype(jnp.int32)
    cache = stale_cache.reshape(N_ROLE, N_SHARD, N_SHARD, CAP, BLK, D)
    role_index = jnp.arange(N_ROLE, dtype=jnp.int32)[:, None, None]
    source = jnp.arange(N_SHARD, dtype=jnp.int32)[None, :, None]
    cache = cache.at[role_index, owner, source, slot].set(blocks)
    refreshed = cache.reshape(N_ROLE * N_SHARD * CACHE_DEV, D)
    position = jnp.arange(1, NEG + 1).astype(jnp.float32)
    discount = 1.0 / jnp.log2(1.0 + position)
    column_owner = (jnp.arange(NEG, dtype=jnp.int32) // NEG_OWN).astype(jnp.int32)
    list_role = (jnp.arange(N_ROLE * Q, dtype=jnp.int32) // Q).astype(jnp.int32)

    def one_list(packed):
        query, ids, grade, role_of = packed
        rows = (role_of * N_SHARD + column_owner) * CACHE_DEV + ids
        embedded = refreshed[rows]
        score = jnp.dot(embedded, query, preferred_element_type=jnp.float32)
        gains = jnp.exp2(grade.astype(jnp.float32))
        ideal = jnp.sum(-jnp.sort(-gains) * discount)
        spread = score[None, :] - score[:, None]
        sigma = jax.nn.sigmoid(spread)
        rank = 0.5 + lax.optimization_barrier(jnp.sum(sigma, 1))
        slope_terms = sigma * (1.0 - sigma)
        slope = lax.optimization_barrier(jnp.sum(slope_terms, 1))
        logged = jnp.log2(1.0 + rank)
        weight = gains / (ideal * LOG_TWO * (1.0 + rank) * logged * logged)
        cross = lax.optimization_barrier(jnp.sum(slope_terms * weight[None, :], 1))
        score_grad = (cross - weight * slope).astype(jnp.bfloat16)
        grad = jnp.dot(score_grad, embedded, preferred_element_type=jnp.float32)
        loss = 1.0 - jnp.sum(gains / logged) / ideal
        return (grad, loss)
    grads, losses = lax.map(one_list, (queries, neg_ids, grades, list_role))
    return (refreshed, grads, losses)
```

```python
import math

import jax
import jax.numpy as jnp
import numpy as np
from jax import lax
from jax.experimental import pallas as pl
from jax.experimental.pallas import tpu as pltpu
from jax.sharding import PartitionSpec as P

CAP = 2
EPSILON = 1e-05
LOG_TWO = math.log(2.0)
EMPTY = 1024.0

f32 = jnp.float32
bf16 = jnp.bfloat16
LANES = 128


def params():
    return pltpu.CompilerParams(vmem_limit_bytes=48 * 1024 * 1024)


def contract_last(a, b):
    return lax.dot_general(a, b, (((1,), (1,)), ((), ())), preferred_element_type=f32)


def encode_kernel(x_ref, win_ref, wout_ref, own_ref, far_ref, near_ref):
    rows = own_ref.shape[0]
    for k in (1, 3, 2, 0):
        inner = contract_last(x_ref[pl.ds(k * rows, rows), :], win_ref[...])
        hidden = 0.5 * inner * (1.0 + lax.erf(inner * math.sqrt(0.5)))
        part = jnp.dot(hidden.astype(bf16), wout_ref[...], preferred_element_type=f32)
        if k == 0:
            own_ref[...] = part
        elif k == 2:
            far_ref[...] = part
        else:
            near_ref[pl.ds(k // 2 * rows, rows), :] = part.astype(bf16)


def encode(x4, w_in, w_out, rows):
    width = x4.shape[1]
    return pl.pallas_call(
        encode_kernel,
        out_shape=(
            jax.ShapeDtypeStruct((rows, width), f32),
            jax.ShapeDtypeStruct((rows, width), f32),
            jax.ShapeDtypeStruct((2 * rows, width), bf16),
        ),
        compiler_params=params(),
        name="encode",
    )(x4, w_in, w_out)


def place_kernel(cls_ref, own_ref, near_ref, far_ref, owner_ref, query_ref, out_ref):
    rows, width = cls_ref.shape
    blocks = owner_ref.shape[1]
    shards = out_ref.shape[0] // (2 * CAP + 1)
    resid = (
        cls_ref[...].astype(f32)
        + own_ref[...]
        + near_ref[:rows, :].astype(f32)
        + far_ref[...].astype(f32)
    )
    centred = resid - jnp.mean(resid, -1, keepdims=True)
    variance = jnp.mean(centred * centred, -1, keepdims=True)
    fresh = (centred * lax.rsqrt(variance + EPSILON)).astype(bf16)

    owner = owner_ref[...]
    shard_of = lax.broadcasted_iota(jnp.int32, (shards, blocks), 0)
    onehot = (shard_of == owner).astype(f32)
    before = lax.broadcasted_iota(jnp.int32, (blocks, blocks), 0) < lax.broadcasted_iota(
        jnp.int32, (blocks, blocks), 1
    )
    earlier = jnp.dot(onehot.astype(bf16), before.astype(bf16), preferred_element_type=f32)
    slot = jnp.sum(earlier * onehot, 0, keepdims=True)
    first = owner.astype(f32) * 5.0 + slot * 2.0

    stride = 2 * CAP + 1
    total = out_ref.shape[0]
    row = lax.broadcasted_iota(jnp.int32, (total, blocks), 0).astype(f32)
    even = row == first
    odd = row == first + 1.0
    picks = lax.broadcasted_iota(jnp.int32, (blocks, rows), 1)
    base = lax.broadcasted_iota(jnp.int32, (blocks, rows), 0) * 2
    even_rows = (picks == base).astype(bf16)
    odd_rows = (picks == base + 1).astype(bf16)
    placing = jnp.dot(even.astype(bf16), even_rows, preferred_element_type=f32) + jnp.dot(
        odd.astype(bf16), odd_rows, preferred_element_type=f32
    )
    placed = jnp.dot(placing.astype(bf16), fresh, preferred_element_type=f32)
    filled = jnp.sum(placing, 1, keepdims=True) > 0.5
    place = lax.broadcasted_iota(jnp.int32, (total, 1), 0)
    is_query = lax.rem(place, stride) == stride - 1
    query = query_ref[...].astype(f32)
    out = jnp.where(filled, placed, jnp.where(is_query, query, EMPTY))
    out_ref[...] = out.astype(bf16)


def place(cls_states, own, near, far, owner, query, shards):
    width = cls_states.shape[1]
    return pl.pallas_call(
        place_kernel,
        out_shape=jax.ShapeDtypeStruct((shards * (2 * CAP + 1), width), bf16),
        compiler_params=params(),
        name="place",
    )(cls_states, own, near, far, owner, query)


def score_kernel(recv_ref, stale_ref, idsg_ref, refreshed_ref, packed_ref):
    cache_rows, width = stale_ref.shape
    total = recv_ref.shape[0]
    stride = 2 * CAP + 1
    shards = total // stride
    recv = recv_ref[...]
    at = lax.broadcasted_iota(jnp.int32, (cache_rows, total), 0)
    source = lax.broadcasted_iota(jnp.int32, (cache_rows, total), 1)
    wanted = (at // (2 * CAP)) * stride + lax.rem(at, 2 * CAP)
    arrived = jnp.dot((source == wanted).astype(bf16), recv, preferred_element_type=f32)
    lists = lax.broadcasted_iota(jnp.int32, (shards, total), 0)
    origin = lax.broadcasted_iota(jnp.int32, (shards, total), 1)
    queries = jnp.dot(
        (origin == lists * stride + stride - 1).astype(bf16), recv, preferred_element_type=f32
    ).astype(bf16)
    refreshed = jnp.where(arrived > 0.5 * EMPTY, stale_ref[...].astype(f32), arrived).astype(bf16)
    refreshed_ref[...] = refreshed
    scores = contract_last(queries, refreshed)
    ids = idsg_ref[...]
    lane = lax.broadcasted_iota(jnp.int32, ids.shape, 1)
    low = ids & (LANES - 1)
    picked = jnp.zeros(ids.shape, f32)
    for part in range(cache_rows // LANES):
        here = jnp.take_along_axis(scores[:, part * LANES : (part + 1) * LANES], low, axis=1)
        picked = jnp.where(ids // LANES == part, here, picked)
    packed_ref[...] = jnp.where(lane < LANES // 2, picked, ids.astype(f32))


def score(recv, stale, idsg):
    return pl.pallas_call(
        score_kernel,
        out_shape=(
            jax.ShapeDtypeStruct(stale.shape, bf16),
            jax.ShapeDtypeStruct(idsg.shape, f32),
        ),
        compiler_params=params(),
        name="score",
    )(recv, stale, idsg)


HALF = LANES // 2


def spread_down(row):
    return jnp.broadcast_to(row, (LANES, LANES)).T


def pair_kernel(x_ref, discount_ref, grad_ref, loss_ref, half_s, wide_w, columns, down_s, rank_ref):
    x = x_ref[...]
    n_blocks = x.shape[0] // 2
    count = n_blocks * LANES
    top, low = x[:n_blocks], x[n_blocks:]
    lane = lax.broadcasted_iota(jnp.int32, (n_blocks, LANES), 1)
    left = lane < HALF
    scores = jnp.where(left, top, pltpu.roll(low, HALF, 1))
    gains = jnp.exp2(jnp.where(left, pltpu.roll(top, HALF, 1), low))
    position = lax.broadcasted_iota(jnp.int32, (n_blocks, LANES), 0) * LANES + lane

    ordered = jnp.ones((n_blocks, LANES), f32)
    for level in range(1, 5):
        above = jnp.sum((gains > float(2**level) - 0.5).astype(f32))
        ordered = jnp.where(position.astype(f32) < above, float(2**level), ordered)
    ideal = jnp.sum(ordered * discount_ref[...])

    half_s[:n_blocks] = 0.5 * scores
    half_s[n_blocks:] = 0.5 * scores
    span = n_blocks // 2
    groups = LANES // 8

    def sweep(rows_of, term):
        columns[...] = jnp.zeros_like(columns)

        def block(i, _):
            s_i, w_i = rows_of(i)
            acc = [jnp.zeros((8, LANES), f32) for _ in range(groups)]

            def step(k, both, acc):
                s_k = jnp.broadcast_to(half_s[pl.ds(k, 1), :], (8, LANES))
                w_k = None
                if w_i is not None:
                    w_k = jnp.broadcast_to(wide_w[pl.ds(k, 1), :], (8, LANES))
                column = [jnp.zeros((8, LANES), f32) for _ in range(4)]
                out = []
                for g in range(groups):
                    part = slice(8 * g, 8 * g + 8)
                    value = term(s_i[part], s_k, None if w_i is None else w_i[part], w_k)
                    out.append(acc[g] + value)
                    column[g % 4] = column[g % 4] + value
                if both:
                    whole = (column[0] + column[1]) + (column[2] + column[3])
                    columns[k] = columns[k] + whole
                return out

            acc = step(i, False, acc)
            for d in range(1, span):
                acc = step(i + d, True, acc)
            rank_ref[pl.ds(i, 1), :] = jnp.sum(jnp.concatenate(acc, 0).T, 0, keepdims=True)
            return 0

        lax.fori_loop(0, n_blocks, block, 0)

        def opposite(i, _):
            s_i, w_i = rows_of(i)
            k = i + span
            s_k = jnp.broadcast_to(half_s[pl.ds(k, 1), :], (8, LANES))
            w_k = None
            if w_i is not None:
                w_k = jnp.broadcast_to(wide_w[pl.ds(k, 1), :], (8, LANES))
            values = [
                term(
                    s_i[8 * g : 8 * g + 8],
                    s_k,
                    None if w_i is None else w_i[8 * g : 8 * g + 8],
                    w_k,
                )
                for g in range(groups)
            ]
            columns[k] = columns[k] + sum(values)
            across = jnp.sum(jnp.concatenate(values, 0).T, 0, keepdims=True)
            rank_ref[pl.ds(i, 1), :] = rank_ref[pl.ds(i, 1), :] + across
            return 0

        lax.fori_loop(0, span, opposite, 0)
        folded = jnp.sum(columns[...], 1)
        wrapped = jnp.concatenate((folded[n_blocks:], jnp.zeros((span, LANES), f32)), 0)
        return rank_ref[...] - folded[:n_blocks] - wrapped

    def first_rows(i):
        s_i = spread_down(half_s[pl.ds(i, 1), :])
        down_s[i] = s_i
        return s_i, None

    def rank_term(s_i, s_k, w_i, w_k):
        return jnp.tanh(s_k - s_i)

    def first_or_again(i):
        return first_rows(i)

    tanhs = sweep(first_or_again, rank_term)
    rank = 0.5 + 0.5 * count + 0.5 * tanhs
    logged = jnp.log2(1.0 + rank)
    weight = gains / (ideal * LOG_TWO * (1.0 + rank) * logged * logged)
    loss_ref[...] = jnp.full((1, LANES), 1.0 - jnp.sum(gains / logged) / ideal, f32)
    wide_w[:n_blocks] = 0.25 * weight
    wide_w[n_blocks:] = 0.25 * weight

    def second_rows(i):
        return down_s[i], spread_down(wide_w[pl.ds(i, 1), :])

    def cross_term(s_i, s_k, w_i, w_k):
        t = jnp.tanh(s_k - s_i)
        return (w_k - w_i) * (1.0 - t * t)

    grad = sweep(second_rows, cross_term).astype(bf16).astype(f32)
    grad_ref[:n_blocks] = grad
    grad_ref[n_blocks:] = pltpu.roll(grad, HALF, 1)


def pair(x, discount):
    n_blocks = x.shape[0] // 2
    wide = n_blocks + n_blocks // 2
    return pl.pallas_call(
        pair_kernel,
        out_shape=(
            jax.ShapeDtypeStruct(x.shape, f32),
            jax.ShapeDtypeStruct((1, LANES), f32),
        ),
        scratch_shapes=[
            pltpu.VMEM((2 * n_blocks, LANES), f32),
            pltpu.VMEM((2 * n_blocks, LANES), f32),
            pltpu.VMEM((wide, 8, LANES), f32),
            pltpu.VMEM((n_blocks, LANES, LANES), f32),
            pltpu.VMEM((n_blocks, LANES), f32),
        ],
        compiler_params=params(),
        name="pair",
    )(x, discount)


def share_kernel(grad_ref, idsg_ref, refreshed_ref, out_ref, rows_w):
    lists, cache_rows = rows_w.shape
    for g in range(lists // 8):
        part = slice(8 * g, 8 * g + 8)
        grads = grad_ref[part, :]
        ids = idsg_ref[part, :]
        spots = [
            lax.broadcasted_iota(jnp.int32, (8, LANES), 1) + LANES * p
            for p in range(cache_rows // LANES)
        ]
        acc = [jnp.zeros((8, LANES), f32) for _ in spots]
        for j in range(HALF):
            id_j = jnp.broadcast_to(ids[:, j : j + 1], (8, LANES))
            grad_j = jnp.broadcast_to(grads[:, j : j + 1], (8, LANES))
            acc = [a + jnp.where(id_j == spot, grad_j, 0.0) for a, spot in zip(acc, spots)]
        for p, a in enumerate(acc):
            rows_w[part, p * LANES : (p + 1) * LANES] = a
    weights = rows_w[...]
    high = weights.astype(bf16)
    rest = (weights - high.astype(f32)).astype(bf16)
    refreshed = refreshed_ref[...]
    out_ref[...] = jnp.dot(high, refreshed, preferred_element_type=f32) + jnp.dot(
        rest, refreshed, preferred_element_type=f32
    )


def share(grads, idsg, refreshed):
    return pl.pallas_call(
        share_kernel,
        out_shape=jax.ShapeDtypeStruct((grads.shape[0], refreshed.shape[1]), f32),
        scratch_shapes=[pltpu.VMEM((grads.shape[0], refreshed.shape[0]), f32)],
        compiler_params=params(),
        name="share",
    )(grads, idsg, refreshed)


def turned(places, axis, by):
    pairs = []
    for start in range(math.prod(places)):
        coords = list(np.unravel_index(start, places))
        coords[axis] = (coords[axis] + by) % places[axis]
        pairs.append((start, int(np.ravel_multi_index(coords, places))))
    return pairs


SHARD_GRID = (4, 8, 2)


def collect(block, axis):
    return [block] + [
        lax.ppermute(block, "shard", turned(SHARD_GRID, axis, by))
        for by in range(1, SHARD_GRID[axis])
    ]


def current_projections(trainer_in, trainer_out):
    roles = lax.axis_size("role")
    units = trainer_in.shape[1]
    share_units = units // roles
    role = lax.axis_index("role")
    both = jnp.stack((trainer_in[0], trainer_out[0]), 0)
    parts = [both[:, k * share_units : (k + 1) * share_units] for k in range(roles)]
    mine = parts[roles - 1]
    arrived = [lax.ppermute(parts[k], "role", [(roles - 1, k)]) for k in range(roles - 1)]
    for k in range(roles - 1):
        mine = jnp.where(role == k, arrived[k], mine)
    pair_ = jnp.concatenate(collect(mine, 2), 1)
    half_in, half_out = pair_[0], pair_[1]
    in_y = jnp.concatenate(collect(half_in, 0), 0)
    out_z = jnp.stack(collect(half_out, 1), 0)
    in_zy = jnp.stack(collect(in_y, 1), 0)
    out_yz = jnp.stack(collect(out_z, 0), 0)
    width = in_zy.shape[-1]
    out_zy = out_yz.transpose(1, 0, 2, 3)
    return in_zy.reshape(-1, width), out_zy.reshape(-1, width)


def per_device(
    cls_states, trainer_in, trainer_out, stale_cache, block_owner, queries, neg_ids, grades
):
    shards = lax.axis_size("shard")
    passages, width = cls_states.shape
    near = [(0, 1), (1, 0), (2, 3), (3, 2)]
    across = [(0, 2), (1, 3), (2, 0), (3, 1)]
    diagonal = [(0, 3), (1, 2), (2, 1), (3, 0)]
    x4 = jnp.concatenate(
        [cls_states] + [lax.ppermute(cls_states, "role", p) for p in (near, across, diagonal)], 0
    )
    w_in, w_out = current_projections(trainer_in, trainer_out)
    own, far, to_near = encode(x4, w_in, w_out, passages)
    from_near = lax.ppermute(to_near, "role", near)
    to_far = (far + from_near[passages:].astype(f32)).astype(bf16)
    from_far = lax.ppermute(to_far, "role", across)
    outgoing = place(
        cls_states, own, from_near, from_far, block_owner.reshape(1, -1), queries, shards
    )
    rows = outgoing.shape[0] // shards
    arrived = lax.all_to_all(
        outgoing.reshape(shards, rows, width), "shard", split_axis=0, concat_axis=0, tiled=True
    )
    idsg = jnp.concatenate((neg_ids, grades), 1)
    refreshed, packed = score(arrived.reshape(-1, width), stale_cache, idsg)
    packed = lax.all_to_all(packed, "shard", split_axis=0, concat_axis=0, tiled=True)
    count = shards * neg_ids.shape[1]
    position = np.arange(1, count + 1, dtype=np.float64)
    discount = (1.0 / np.log2(1.0 + position)).astype(np.float32).reshape(-1, LANES)
    grads, loss = pair(packed, jnp.asarray(discount))
    grads = lax.all_to_all(grads, "shard", split_axis=0, concat_axis=0, tiled=True)
    shares = share(grads, idsg, refreshed)
    shares = lax.all_to_all(shares, "shard", split_axis=0, concat_axis=0, tiled=True)
    return refreshed, jnp.sum(shares, 0, keepdims=True), loss[0, :1]


def solution(mesh):
    return jax.shard_map(
        per_device,
        mesh=mesh,
        in_specs=(
            P(("role", "shard"), None),
            P("role", "shard", None),
            P("role", "shard", None),
            P(("role", "shard"), None),
            P(("role", "shard"), None),
            P(("role", "shard"), None),
            P("role", "shard"),
            P("role", "shard"),
        ),
        out_specs=(P(("role", "shard"), None), P(("role", "shard"), None), P(("role", "shard"))),
        check_vma=False,
    )
```

```python
import math

import jax
import jax.numpy as jnp
import numpy as np
from jax import lax
from jax.experimental import pallas as pl
from jax.experimental.pallas import tpu as pltpu
from jax.sharding import PartitionSpec as P

CAP = 2
EPSILON = 1e-05
LOG_TWO = math.log(2.0)
EMPTY = 1024.0

f32 = jnp.float32
bf16 = jnp.bfloat16
LANES = 128


def params():
    return pltpu.CompilerParams(vmem_limit_bytes=48 * 1024 * 1024)


def contract_last(a, b):
    return lax.dot_general(a, b, (((1,), (1,)), ((), ())), preferred_element_type=f32)


def encode_kernel(x_ref, w_ref, own_ref, far_ref, near_ref):
    rows, width = own_ref.shape
    for k in (1, 3, 2, 0):
        inner = contract_last(x_ref[pl.ds(k * rows, rows), :], w_ref[:, :width])
        hidden = 0.5 * inner * (1.0 + lax.erf(inner * math.sqrt(0.5)))
        part = jnp.dot(hidden.astype(bf16), w_ref[:, width:], preferred_element_type=f32)
        if k == 0:
            own_ref[...] = part
        elif k == 2:
            far_ref[...] = part
        else:
            near_ref[pl.ds(k // 2 * rows, rows), :] = part.astype(bf16)


def encode(x4, projections, rows):
    width = x4.shape[1]
    return pl.pallas_call(
        encode_kernel,
        out_shape=(
            jax.ShapeDtypeStruct((rows, width), f32),
            jax.ShapeDtypeStruct((rows, width), f32),
            jax.ShapeDtypeStruct((2 * rows, width), bf16),
        ),
        compiler_params=params(),
        name="encode",
    )(x4, projections)


ROWS = 32


def place_kernel(cls_ref, own_ref, near_ref, far_ref, owner_ref, query_ref, out_ref):
    rows, width = cls_ref.shape
    blocks = owner_ref.shape[1]
    total = out_ref.shape[0]
    shards = total // ROWS
    chunks = width // LANES
    resid = (
        cls_ref[...].astype(f32)
        + own_ref[...]
        + near_ref[:rows, :].astype(f32)
        + far_ref[...].astype(f32)
    )
    centred = resid - jnp.mean(resid, -1, keepdims=True)
    variance = jnp.mean(centred * centred, -1, keepdims=True)
    fresh = (centred * lax.rsqrt(variance + EPSILON)).astype(bf16)

    owner = owner_ref[...]
    shard_of = lax.broadcasted_iota(jnp.int32, (shards, blocks), 0)
    onehot = (shard_of == owner).astype(f32)
    before = lax.broadcasted_iota(jnp.int32, (blocks, blocks), 0) < lax.broadcasted_iota(
        jnp.int32, (blocks, blocks), 1
    )
    earlier = jnp.dot(onehot.astype(bf16), before.astype(bf16), preferred_element_type=f32)
    slot = jnp.sum(earlier * onehot, 0, keepdims=True)
    passage = lax.broadcasted_iota(jnp.int32, (blocks, rows), 1)
    block = lax.broadcasted_iota(jnp.int32, (blocks, rows), 0)
    widen = (passage // 2 == block).astype(bf16)
    both = jnp.concatenate(
        (jnp.broadcast_to(owner.astype(f32), (8, blocks)), jnp.broadcast_to(slot, (8, blocks))), 0
    )
    both = jnp.dot(both.astype(bf16), widen, preferred_element_type=f32)
    parity = lax.broadcasted_iota(jnp.int32, (1, rows), 1) & 1
    target = both[0:1] * ROWS + (both[8:9] * 2.0 + parity.astype(f32)) * chunks

    row = lax.broadcasted_iota(jnp.int32, (total, rows), 0).astype(f32)
    placed = jnp.zeros((total, LANES), f32)
    taken = jnp.zeros((total, rows), f32)
    for j in range(chunks):
        onto = (row == target + float(j)).astype(f32)
        taken = taken + onto
        placed = placed + jnp.dot(
            onto.astype(bf16), fresh[:, j * LANES : (j + 1) * LANES], preferred_element_type=f32
        )
    filled = jnp.dot(taken.astype(bf16), jnp.ones((rows, LANES), bf16), preferred_element_type=f32)
    rest = jnp.broadcast_to(query_ref[...].astype(f32)[None], (shards, ROWS, LANES))
    out_ref[...] = jnp.where(filled > 0.5, placed, rest.reshape(total, LANES)).astype(bf16)


def place(cls_states, own, near, far, owner, query, shards):
    return pl.pallas_call(
        place_kernel,
        out_shape=jax.ShapeDtypeStruct((shards * ROWS, LANES), bf16),
        compiler_params=params(),
        name="place",
    )(cls_states, own, near, far, owner, query)


def score_kernel(recv_ref, stale_ref, idsg_ref, refreshed_ref, packed_ref, recv_s, arrived_s):
    cache_rows, width = stale_ref.shape
    shards = recv_ref.shape[0] // ROWS
    chunks = width // LANES
    per_shard = cache_rows // shards
    recv_s[...] = recv_ref[...].astype(f32)
    queries = []
    for j in range(chunks):
        for c in range(per_shard):
            arrived_s[j, pl.ds(c, shards, stride=per_shard), :] = recv_s[
                pl.ds(c * chunks + j, shards, stride=ROWS), :
            ]
        queries.append(recv_s[pl.ds(per_shard * chunks + j, shards, stride=ROWS), :])
    queries = jnp.concatenate(queries, 1).astype(bf16)
    arrived = jnp.concatenate([arrived_s[j] for j in range(chunks)], 1)
    refreshed = jnp.where(arrived > 0.5 * EMPTY, stale_ref[...].astype(f32), arrived).astype(bf16)
    refreshed_ref[...] = refreshed
    scores = contract_last(queries, refreshed)
    ids = idsg_ref[...]
    lane = lax.broadcasted_iota(jnp.int32, ids.shape, 1)
    low = ids & (LANES - 1)
    picked = jnp.zeros(ids.shape, f32)
    for part in range(cache_rows // LANES):
        here = jnp.take_along_axis(scores[:, part * LANES : (part + 1) * LANES], low, axis=1)
        picked = jnp.where(ids // LANES == part, here, picked)
    packed_ref[...] = jnp.where(lane < LANES // 2, picked, ids.astype(f32))


def score(recv, stale, idsg):
    return pl.pallas_call(
        score_kernel,
        out_shape=(
            jax.ShapeDtypeStruct(stale.shape, bf16),
            jax.ShapeDtypeStruct(idsg.shape, f32),
        ),
        scratch_shapes=[
            pltpu.VMEM(recv.shape, f32),
            pltpu.VMEM((stale.shape[1] // LANES, stale.shape[0], LANES), f32),
        ],
        compiler_params=params(),
        name="score",
    )(recv, stale, idsg)


HALF = LANES // 2


def spread_down(row):
    return jnp.broadcast_to(row, (LANES, LANES)).T


def pair_kernel(
    x_ref, discount_ref, grad_ref, loss_ref, half_s, wide_w, columns, across, near_q, far_q
):
    x = x_ref[...]
    n_blocks = x.shape[0] // 2
    count = n_blocks * LANES
    top, low = x[:n_blocks], x[n_blocks:]
    lane = lax.broadcasted_iota(jnp.int32, (n_blocks, LANES), 1)
    left = lane < HALF
    scores = jnp.where(left, top, pltpu.roll(low, HALF, 1))
    gains = jnp.exp2(jnp.where(left, pltpu.roll(top, HALF, 1), low))
    position = lax.broadcasted_iota(jnp.int32, (n_blocks, LANES), 0) * LANES + lane

    ordered = jnp.ones((n_blocks, LANES), f32)
    for level in range(1, 5):
        above = jnp.sum((gains > float(2**level) - 0.5).astype(f32))
        ordered = jnp.where(position.astype(f32) < above, float(2**level), ordered)
    ideal = jnp.sum(ordered * discount_ref[...])

    span = n_blocks // 2
    groups = LANES // 8

    def sweep(values, load_or_make):
        columns[...] = jnp.zeros_like(columns)
        values[n_blocks:] = values[:n_blocks]

        def met(i, k, kept, first, acc, both):
            v_k = jnp.broadcast_to(values[pl.ds(k, 1), :], (8, LANES))
            column = [jnp.zeros((8, LANES), f32) for _ in range(4)]
            out = []
            for g in range(groups):
                value = load_or_make(first[8 * g : 8 * g + 8], v_k, kept, 8 * g)
                out.append(acc[g] + value)
                column[g % 4] = column[g % 4] + value
            if both:
                columns[k] = columns[k] + ((column[0] + column[1]) + (column[2] + column[3]))
            return out

        def block(i, _):
            first = spread_down(values[pl.ds(i, 1), :])
            acc = [jnp.zeros((8, LANES), f32) for _ in range(groups)]
            for d in range(span):
                acc = met(i, i + d, near_q.at[i, d], first, acc, d > 0)
            across[pl.ds(i, 1), :] = jnp.sum(jnp.concatenate(acc, 0).T, 0, keepdims=True)
            return 0

        lax.fori_loop(0, n_blocks, block, 0)

        def opposite(i, _):
            first = spread_down(values[pl.ds(i, 1), :])
            acc = [jnp.zeros((8, LANES), f32) for _ in range(groups)]
            acc = met(i, i + span, far_q.at[i], first, acc, True)
            here = jnp.sum(jnp.concatenate(acc, 0).T, 0, keepdims=True)
            across[pl.ds(i, 1), :] = across[pl.ds(i, 1), :] + here
            return 0

        lax.fori_loop(0, span, opposite, 0)
        folded = jnp.sum(columns[...], 1)
        wrapped = jnp.concatenate((folded[n_blocks:], jnp.zeros((span, LANES), f32)), 0)
        return across[...] - folded[:n_blocks] - wrapped

    def rank_term(s_i, s_k, kept, at):
        t = jnp.tanh(s_k - s_i)
        kept[pl.ds(at, 8), :] = 1.0 - t * t
        return t

    def cross_term(w_i, w_k, kept, at):
        return (w_k - w_i) * kept[pl.ds(at, 8), :]

    half_s[:n_blocks] = 0.5 * scores
    rank = 0.5 + 0.5 * count + 0.5 * sweep(half_s, rank_term)
    logged = jnp.log2(1.0 + rank)
    weight = gains / (ideal * LOG_TWO * (1.0 + rank) * logged * logged)
    loss_ref[...] = jnp.full((1, LANES), 1.0 - jnp.sum(gains / logged) / ideal, f32)
    wide_w[:n_blocks] = 0.25 * weight
    grad = sweep(wide_w, cross_term).astype(bf16).astype(f32)
    grad_ref[:n_blocks] = grad
    grad_ref[n_blocks:] = pltpu.roll(grad, HALF, 1)


def pair(x, discount):
    n_blocks = x.shape[0] // 2
    span = n_blocks // 2
    return pl.pallas_call(
        pair_kernel,
        out_shape=(
            jax.ShapeDtypeStruct(x.shape, f32),
            jax.ShapeDtypeStruct((1, LANES), f32),
        ),
        scratch_shapes=[
            pltpu.VMEM((2 * n_blocks, LANES), f32),
            pltpu.VMEM((2 * n_blocks, LANES), f32),
            pltpu.VMEM((n_blocks + span, 8, LANES), f32),
            pltpu.VMEM((n_blocks, LANES), f32),
            pltpu.VMEM((n_blocks, span, LANES, LANES), f32),
            pltpu.VMEM((span, LANES, LANES), f32),
        ],
        compiler_params=params(),
        name="pair",
    )(x, discount)


def share_kernel(grad_ref, idsg_ref, refreshed_ref, out_ref, rows_w):
    lists, cache_rows = rows_w.shape
    for g in range(lists // 8):
        part = slice(8 * g, 8 * g + 8)
        grads = grad_ref[part, :]
        ids = idsg_ref[part, :]
        spots = [
            lax.broadcasted_iota(jnp.int32, (8, LANES), 1) + LANES * p
            for p in range(cache_rows // LANES)
        ]
        acc = [jnp.zeros((8, LANES), f32) for _ in spots]
        for j in range(HALF):
            id_j = jnp.broadcast_to(ids[:, j : j + 1], (8, LANES))
            grad_j = jnp.broadcast_to(grads[:, j : j + 1], (8, LANES))
            acc = [a + jnp.where(id_j == spot, grad_j, 0.0) for a, spot in zip(acc, spots)]
        for p, a in enumerate(acc):
            rows_w[part, p * LANES : (p + 1) * LANES] = a
    weights = rows_w[...]
    high = weights.astype(bf16)
    rest = (weights - high.astype(f32)).astype(bf16)
    refreshed = refreshed_ref[...]
    out_ref[...] = jnp.dot(high, refreshed, preferred_element_type=f32) + jnp.dot(
        rest, refreshed, preferred_element_type=f32
    )


def share(grads, idsg, refreshed):
    return pl.pallas_call(
        share_kernel,
        out_shape=jax.ShapeDtypeStruct((grads.shape[0], refreshed.shape[1]), f32),
        scratch_shapes=[pltpu.VMEM((grads.shape[0], refreshed.shape[0]), f32)],
        compiler_params=params(),
        name="share",
    )(grads, idsg, refreshed)


Y, ZZ, ZL, X = 4, 4, 2, 2


def shard_at(y, zz, zl, x):
    return ((y * ZZ + zz) * ZL + zl) * X + x


def everywhere():
    return [
        (y, zz, zl, x) for y in range(Y) for zz in range(ZZ) for zl in range(ZL) for x in range(X)
    ]


def current_projections(trainer_in, trainer_out):
    roles = lax.axis_size("role")
    shards = lax.axis_size("shard")
    axes = ("role", "shard")
    mine = jnp.concatenate((trainer_in[0], trainer_out[0]), 1)
    mine = lax.ppermute(
        mine,
        axes,
        [
            ((roles - 1) * shards + shard_at(y, zz, zl, x), zz * shards + shard_at(y, zz, zl, x))
            for y, zz, zl, x in everywhere()
        ],
    )
    block = mine
    for by in range(1, ZZ):
        block = block + lax.ppermute(
            mine,
            axes,
            [
                (
                    zz * shards + shard_at(y, zz, zl, x),
                    zz * shards + shard_at(y, (zz + by) % ZZ, zl, x),
                )
                for y, zz, zl, x in everywhere()
            ],
        )
    groups = [
        [shard_at(y, zz, zl, x) for zl in range(ZL) for y in range(Y) for x in range(X)]
        for zz in range(ZZ)
    ]
    parts = len(groups[0])
    units, width = block.shape
    gathered = lax.all_to_all(
        jnp.broadcast_to(block[None], (parts, units, width)),
        "shard",
        split_axis=0,
        concat_axis=0,
        tiled=True,
        axis_index_groups=groups,
    )
    return gathered.reshape(parts * units, width)


def per_device(
    cls_states, trainer_in, trainer_out, stale_cache, block_owner, queries, neg_ids, grades
):
    shards = lax.axis_size("shard")
    passages, width = cls_states.shape
    near = [(0, 1), (1, 0), (2, 3), (3, 2)]
    across = [(0, 2), (1, 3), (2, 0), (3, 1)]
    diagonal = [(0, 3), (1, 2), (2, 1), (3, 0)]
    x4 = jnp.concatenate(
        [cls_states] + [lax.ppermute(cls_states, "role", p) for p in (near, across, diagonal)], 0
    )
    projections = current_projections(trainer_in, trainer_out)
    own, far, to_near = encode(x4, projections, passages)
    from_near = lax.ppermute(to_near, "role", near)
    to_far = (far + from_near[passages:].astype(f32)).astype(bf16)
    from_far = lax.ppermute(to_far, "role", across)
    chunks = width // LANES
    rest = jnp.concatenate(
        (
            jnp.full((2 * CAP * chunks, LANES), EMPTY, bf16),
            queries.reshape(chunks, LANES),
            jnp.full((ROWS - (2 * CAP + 1) * chunks, LANES), EMPTY, bf16),
        ),
        0,
    )
    idsg = jnp.concatenate((neg_ids, grades), 1)
    outgoing = place(
        cls_states, own, from_near, from_far, block_owner.reshape(1, -1), rest, shards
    )
    outgoing, idsg = lax.optimization_barrier((outgoing, idsg))
    arrived = lax.all_to_all(
        outgoing.reshape(shards, ROWS, LANES), "shard", split_axis=0, concat_axis=0, tiled=True
    )
    refreshed, packed = score(arrived.reshape(-1, LANES), stale_cache, idsg)
    packed = lax.all_to_all(packed, "shard", split_axis=0, concat_axis=0, tiled=True)
    count = shards * neg_ids.shape[1]
    position = np.arange(1, count + 1, dtype=np.float64)
    discount = (1.0 / np.log2(1.0 + position)).astype(np.float32).reshape(-1, LANES)
    grads, loss = pair(packed, jnp.asarray(discount))
    grads = lax.all_to_all(grads, "shard", split_axis=0, concat_axis=0, tiled=True)
    shares = share(grads, idsg, refreshed)
    shares = lax.all_to_all(shares, "shard", split_axis=0, concat_axis=0, tiled=True)
    return refreshed, jnp.sum(shares, 0, keepdims=True), loss[0, :1]


def solution(mesh):
    return jax.shard_map(
        per_device,
        mesh=mesh,
        in_specs=(
            P(("role", "shard"), None),
            P("role", "shard", None),
            P("role", "shard", None),
            P(("role", "shard"), None),
            P(("role", "shard"), None),
            P(("role", "shard"), None),
            P("role", "shard"),
            P("role", "shard"),
        ),
        out_specs=(P(("role", "shard"), None), P(("role", "shard"), None), P(("role", "shard"))),
        check_vma=False,
    )
```

```python
import math

import jax
import jax.numpy as jnp
import numpy as np
from jax import lax
from jax.experimental import pallas as pl
from jax.experimental.pallas import tpu as pltpu
from jax.sharding import PartitionSpec as P

CAP = 2
EPSILON = 1e-05
LOG_TWO = math.log(2.0)
EMPTY = 1024.0

f32 = jnp.float32
bf16 = jnp.bfloat16
LANES = 128


def params():
    return pltpu.CompilerParams(vmem_limit_bytes=48 * 1024 * 1024)


def contract_last(a, b):
    return lax.dot_general(a, b, (((1,), (1,)), ((), ())), preferred_element_type=f32)


def encode_kernel(kept_x_ref, sent_x_ref, w_ref, kept_ref, sent_ref):
    width = kept_ref.shape[1]
    for x_ref, out_ref in ((sent_x_ref, sent_ref), (kept_x_ref, kept_ref)):
        inner = contract_last(x_ref[...], w_ref[:, :width])
        hidden = 0.5 * inner * (1.0 + lax.erf(inner * math.sqrt(0.5)))
        part = jnp.dot(hidden.astype(bf16), w_ref[:, width:], preferred_element_type=f32)
        out_ref[...] = part.astype(out_ref.dtype)


def encode(kept_x, sent_x, projections):
    return pl.pallas_call(
        encode_kernel,
        out_shape=(
            jax.ShapeDtypeStruct(kept_x.shape, f32),
            jax.ShapeDtypeStruct(sent_x.shape, bf16),
        ),
        compiler_params=params(),
        name="encode",
    )(kept_x, sent_x, projections)


ROWS = 32


def place_kernel(cls_ref, own_ref, near_ref, far_ref, owner_ref, query_ref, out_ref):
    rows, width = cls_ref.shape
    blocks = owner_ref.shape[1]
    total = out_ref.shape[0]
    shards = total // ROWS
    chunks = width // LANES
    resid = (
        cls_ref[...].astype(f32)
        + own_ref[...]
        + near_ref[...].astype(f32)
        + far_ref[...].astype(f32)
    )
    centred = resid - jnp.mean(resid, -1, keepdims=True)
    variance = jnp.mean(centred * centred, -1, keepdims=True)
    fresh = (centred * lax.rsqrt(variance + EPSILON)).astype(bf16)

    owner = owner_ref[...]
    shard_of = lax.broadcasted_iota(jnp.int32, (shards, blocks), 0)
    onehot = (shard_of == owner).astype(f32)
    before = lax.broadcasted_iota(jnp.int32, (blocks, blocks), 0) < lax.broadcasted_iota(
        jnp.int32, (blocks, blocks), 1
    )
    earlier = jnp.dot(onehot.astype(bf16), before.astype(bf16), preferred_element_type=f32)
    slot = jnp.sum(earlier * onehot, 0, keepdims=True)
    passage = lax.broadcasted_iota(jnp.int32, (blocks, rows), 1)
    block = lax.broadcasted_iota(jnp.int32, (blocks, rows), 0)
    widen = (passage // 2 == block).astype(bf16)
    both = jnp.concatenate(
        (jnp.broadcast_to(owner.astype(f32), (8, blocks)), jnp.broadcast_to(slot, (8, blocks))), 0
    )
    both = jnp.dot(both.astype(bf16), widen, preferred_element_type=f32)
    parity = lax.broadcasted_iota(jnp.int32, (1, rows), 1) & 1
    target = both[0:1] * ROWS + (both[8:9] * 2.0 + parity.astype(f32)) * chunks

    row = lax.broadcasted_iota(jnp.int32, (total, rows), 0).astype(f32)
    placed = jnp.zeros((total, LANES), f32)
    taken = jnp.zeros((total, rows), f32)
    for j in range(chunks):
        onto = (row == target + float(j)).astype(f32)
        taken = taken + onto
        placed = placed + jnp.dot(
            onto.astype(bf16), fresh[:, j * LANES : (j + 1) * LANES], preferred_element_type=f32
        )
    filled = jnp.dot(taken.astype(bf16), jnp.ones((rows, LANES), bf16), preferred_element_type=f32)
    rest = jnp.broadcast_to(query_ref[...].astype(f32)[None], (shards, ROWS, LANES))
    out_ref[...] = jnp.where(filled > 0.5, placed, rest.reshape(total, LANES)).astype(bf16)


def place(cls_states, own, near, far, owner, query, shards):
    return pl.pallas_call(
        place_kernel,
        out_shape=jax.ShapeDtypeStruct((shards * ROWS, LANES), bf16),
        compiler_params=params(),
        name="place",
    )(cls_states, own, near, far, owner, query)


def score_kernel(recv_ref, stale_ref, idsg_ref, refreshed_ref, packed_ref, recv_s, arrived_s):
    cache_rows, width = stale_ref.shape
    shards = recv_ref.shape[0] // ROWS
    chunks = width // LANES
    per_shard = cache_rows // shards
    recv_s[...] = recv_ref[...].astype(f32)
    queries = []
    for j in range(chunks):
        for c in range(per_shard):
            arrived_s[j, pl.ds(c, shards, stride=per_shard), :] = recv_s[
                pl.ds(c * chunks + j, shards, stride=ROWS), :
            ]
        queries.append(recv_s[pl.ds(per_shard * chunks + j, shards, stride=ROWS), :])
    queries = jnp.concatenate(queries, 1).astype(bf16)
    arrived = jnp.concatenate([arrived_s[j] for j in range(chunks)], 1)
    refreshed = jnp.where(arrived > 0.5 * EMPTY, stale_ref[...].astype(f32), arrived).astype(bf16)
    refreshed_ref[...] = refreshed
    scores = contract_last(queries, refreshed)
    ids = idsg_ref[...]
    lane = lax.broadcasted_iota(jnp.int32, ids.shape, 1)
    low = ids & (LANES - 1)
    picked = jnp.zeros(ids.shape, f32)
    for part in range(cache_rows // LANES):
        here = jnp.take_along_axis(scores[:, part * LANES : (part + 1) * LANES], low, axis=1)
        picked = jnp.where(ids // LANES == part, here, picked)
    packed_ref[...] = jnp.where(lane < LANES // 2, picked, ids.astype(f32))


def score(recv, stale, idsg):
    return pl.pallas_call(
        score_kernel,
        out_shape=(
            jax.ShapeDtypeStruct(stale.shape, bf16),
            jax.ShapeDtypeStruct(idsg.shape, f32),
        ),
        scratch_shapes=[
            pltpu.VMEM(recv.shape, f32),
            pltpu.VMEM((stale.shape[1] // LANES, stale.shape[0], LANES), f32),
        ],
        compiler_params=params(),
        name="score",
    )(recv, stale, idsg)


HALF = LANES // 2


def pair_kernel(
    x_ref, discount_ref, grad_ref, loss_ref, half_s, wide_w, columns, across, rows_s, near_q, far_q
):
    x = x_ref[...]
    n_blocks = x.shape[0] // 2
    count = n_blocks * LANES
    top, low = x[:n_blocks], x[n_blocks:]
    lane = lax.broadcasted_iota(jnp.int32, (n_blocks, LANES), 1)
    left = lane < HALF
    scores = jnp.where(left, top, pltpu.roll(low, HALF, 1))
    gains = jnp.exp2(jnp.where(left, pltpu.roll(top, HALF, 1), low))
    position = lax.broadcasted_iota(jnp.int32, (n_blocks, LANES), 0) * LANES + lane

    ordered = jnp.ones((n_blocks, LANES), f32)
    for level in range(1, 5):
        above = jnp.sum((gains > float(2**level) - 0.5).astype(f32))
        ordered = jnp.where(position.astype(f32) < above, float(2**level), ordered)
    ideal = jnp.sum(ordered * discount_ref[...])

    span = n_blocks // 2
    groups = LANES // 8

    def sweep(values, load_or_make):
        columns[...] = jnp.zeros_like(columns)
        values[n_blocks:] = values[:n_blocks]

        def spread(i, _):
            rows_s[i] = jnp.broadcast_to(values[pl.ds(i, 1), :], (LANES, LANES)).T
            return 0

        lax.fori_loop(0, n_blocks, spread, 0, unroll=8)

        def block(i, last):
            first = [rows_s[i, pl.ds(8 * g, 8), :] for g in range(groups)]
            acc = [jnp.zeros((8, LANES), f32) for _ in range(groups)]
            for d in range(last + 1):
                k = i + d
                kept = near_q.at[i, d] if d < span else far_q.at[i]
                v_k = jnp.broadcast_to(values[pl.ds(k, 1), :], (8, LANES))
                column = [jnp.zeros((8, LANES), f32) for _ in range(4)]
                for g in range(groups):
                    value = load_or_make(first[g], v_k, kept, 8 * g)
                    acc[g] = acc[g] + value
                    column[g % 4] = column[g % 4] + value
                if d > 0:
                    columns[k] = columns[k] + ((column[0] + column[1]) + (column[2] + column[3]))
            for g in range(groups):
                rows_s[i, pl.ds(8 * g, 8), :] = acc[g]
            return 0

        lax.fori_loop(0, span, lambda i, _: block(i, span), 0)
        lax.fori_loop(span, n_blocks, lambda i, _: block(i, span - 1), 0)

        def collect(i, _):
            across[pl.ds(i, 1), :] = jnp.sum(rows_s[i].T, 0, keepdims=True)
            return 0

        lax.fori_loop(0, n_blocks, collect, 0, unroll=8)
        folded = jnp.sum(columns[...], 1)
        wrapped = jnp.concatenate((folded[n_blocks:], jnp.zeros((span, LANES), f32)), 0)
        return across[...] - folded[:n_blocks] - wrapped

    def rank_term(s_i, s_k, kept, at):
        t = jnp.tanh(s_k - s_i)
        kept[pl.ds(at, 8), :] = 1.0 - t * t
        return t

    def cross_term(w_i, w_k, kept, at):
        return (w_k - w_i) * kept[pl.ds(at, 8), :]

    half_s[:n_blocks] = 0.5 * scores
    rank = 0.5 + 0.5 * count + 0.5 * sweep(half_s, rank_term)
    logged = jnp.log2(1.0 + rank)
    weight = gains / (ideal * LOG_TWO * (1.0 + rank) * logged * logged)
    loss_ref[...] = jnp.full((1, LANES), 1.0 - jnp.sum(gains / logged) / ideal, f32)
    wide_w[:n_blocks] = 0.25 * weight
    grad = sweep(wide_w, cross_term).astype(bf16).astype(f32)
    grad_ref[:n_blocks] = grad
    grad_ref[n_blocks:] = pltpu.roll(grad, HALF, 1)


def pair(x, discount):
    n_blocks = x.shape[0] // 2
    span = n_blocks // 2
    return pl.pallas_call(
        pair_kernel,
        out_shape=(
            jax.ShapeDtypeStruct(x.shape, f32),
            jax.ShapeDtypeStruct((1, LANES), f32),
        ),
        scratch_shapes=[
            pltpu.VMEM((2 * n_blocks, LANES), f32),
            pltpu.VMEM((2 * n_blocks, LANES), f32),
            pltpu.VMEM((n_blocks + span, 8, LANES), f32),
            pltpu.VMEM((n_blocks, LANES), f32),
            pltpu.VMEM((n_blocks, LANES, LANES), f32),
            pltpu.VMEM((n_blocks, span, LANES, LANES), f32),
            pltpu.VMEM((span, LANES, LANES), f32),
        ],
        compiler_params=params(),
        name="pair",
    )(x, discount)


def share_kernel(grad_ref, idsg_ref, refreshed_ref, out_ref, rows_w):
    lists, cache_rows = rows_w.shape
    for g in range(lists // 8):
        part = slice(8 * g, 8 * g + 8)
        grads = grad_ref[part, :]
        ids = idsg_ref[part, :]
        spots = [
            lax.broadcasted_iota(jnp.int32, (8, LANES), 1) + LANES * p
            for p in range(cache_rows // LANES)
        ]
        acc = [jnp.zeros((8, LANES), f32) for _ in spots]
        for j in range(HALF):
            id_j = jnp.broadcast_to(ids[:, j : j + 1], (8, LANES))
            grad_j = jnp.broadcast_to(grads[:, j : j + 1], (8, LANES))
            acc = [a + jnp.where(id_j == spot, grad_j, 0.0) for a, spot in zip(acc, spots)]
        for p, a in enumerate(acc):
            rows_w[part, p * LANES : (p + 1) * LANES] = a
    weights = rows_w[...]
    high = weights.astype(bf16)
    rest = (weights - high.astype(f32)).astype(bf16)
    refreshed = refreshed_ref[...]
    out_ref[...] = jnp.dot(high, refreshed, preferred_element_type=f32) + jnp.dot(
        rest, refreshed, preferred_element_type=f32
    )


def share(grads, idsg, refreshed):
    return pl.pallas_call(
        share_kernel,
        out_shape=jax.ShapeDtypeStruct((grads.shape[0], refreshed.shape[1]), f32),
        scratch_shapes=[pltpu.VMEM((grads.shape[0], refreshed.shape[0]), f32)],
        compiler_params=params(),
        name="share",
    )(grads, idsg, refreshed)


Y, ZZ, ZL, X = 4, 4, 2, 2


def shard_at(y, zz, zl, x):
    return ((y * ZZ + zz) * ZL + zl) * X + x


def everywhere():
    return [
        (y, zz, zl, x) for y in range(Y) for zz in range(ZZ) for zl in range(ZL) for x in range(X)
    ]


def current_projections(trainer_in, trainer_out):
    roles = lax.axis_size("role")
    shards = lax.axis_size("shard")
    axes = ("role", "shard")
    mine = jnp.concatenate((trainer_in[0], trainer_out[0]), 1)
    mine = lax.ppermute(
        mine,
        axes,
        [
            ((roles - 1) * shards + shard_at(y, zz, zl, x), zz * shards + shard_at(y, zz, zl, x))
            for y, zz, zl, x in everywhere()
        ],
    )
    block = mine
    for by in range(1, ZZ):
        block = block + lax.ppermute(
            mine,
            axes,
            [
                (
                    zz * shards + shard_at(y, zz, zl, x),
                    zz * shards + shard_at(y, (zz + by) % ZZ, zl, x),
                )
                for y, zz, zl, x in everywhere()
            ],
        )
    return block


def gather_units(block):
    groups = [
        [shard_at(y, zz, zl, x) for zl in range(ZL) for y in range(Y) for x in range(X)]
        for zz in range(ZZ)
    ]
    parts = len(groups[0])
    units, width = block.shape
    gathered = lax.all_to_all(
        jnp.broadcast_to(block[None], (parts, units, width)),
        "shard",
        split_axis=0,
        concat_axis=0,
        tiled=True,
        axis_index_groups=groups,
    )
    return gathered.reshape(parts * units, width)


def per_device(
    cls_states, trainer_in, trainer_out, stale_cache, block_owner, queries, neg_ids, grades
):
    shards = lax.axis_size("shard")
    passages, width = cls_states.shape
    near = [(0, 1), (1, 0), (2, 3), (3, 2)]
    across = [(0, 2), (1, 3), (2, 0), (3, 1)]
    x_across = lax.ppermute(cls_states, "role", across)
    x_others = lax.ppermute(jnp.concatenate((cls_states, x_across), 0), "role", near)
    block = current_projections(trainer_in, trainer_out)
    block, x_across, x_others = lax.optimization_barrier((block, x_across, x_others))
    projections = gather_units(block)
    far, for_far = encode(x_across, x_others[passages:], projections)
    to_far = (far + lax.ppermute(for_far, "role", near).astype(f32)).astype(bf16)
    from_far = lax.ppermute(to_far, "role", across)
    own, for_near = encode(cls_states, x_others[:passages], projections)
    from_near = lax.ppermute(for_near, "role", near)
    chunks = width // LANES
    rest = jnp.concatenate(
        (
            jnp.full((2 * CAP * chunks, LANES), EMPTY, bf16),
            queries.reshape(chunks, LANES),
            jnp.full((ROWS - (2 * CAP + 1) * chunks, LANES), EMPTY, bf16),
        ),
        0,
    )
    idsg = jnp.concatenate((neg_ids, grades), 1)
    outgoing = place(
        cls_states, own, from_near, from_far, block_owner.reshape(1, -1), rest, shards
    )
    outgoing, idsg = lax.optimization_barrier((outgoing, idsg))
    arrived = lax.all_to_all(
        outgoing.reshape(shards, ROWS, LANES), "shard", split_axis=0, concat_axis=0, tiled=True
    )
    refreshed, packed = score(arrived.reshape(-1, LANES), stale_cache, idsg)
    packed = lax.all_to_all(packed, "shard", split_axis=0, concat_axis=0, tiled=True)
    count = shards * neg_ids.shape[1]
    position = np.arange(1, count + 1, dtype=np.float64)
    discount = (1.0 / np.log2(1.0 + position)).astype(np.float32).reshape(-1, LANES)
    grads, loss = pair(packed, jnp.asarray(discount))
    grads = lax.all_to_all(grads, "shard", split_axis=0, concat_axis=0, tiled=True)
    shares = share(grads, idsg, refreshed)
    shares = lax.all_to_all(shares, "shard", split_axis=0, concat_axis=0, tiled=True)
    return refreshed, jnp.sum(shares, 0, keepdims=True), loss[0, :1]


def solution(mesh):
    return jax.shard_map(
        per_device,
        mesh=mesh,
        in_specs=(
            P(("role", "shard"), None),
            P("role", "shard", None),
            P("role", "shard", None),
            P(("role", "shard"), None),
            P(("role", "shard"), None),
            P(("role", "shard"), None),
            P("role", "shard"),
            P("role", "shard"),
        ),
        out_specs=(P(("role", "shard"), None), P(("role", "shard"), None), P(("role", "shard"))),
        check_vma=False,
    )
```

```python
import math

import jax
import jax.numpy as jnp
import numpy as np
from jax import lax
from jax.experimental import pallas as pl
from jax.experimental.pallas import tpu as pltpu
from jax.sharding import PartitionSpec as P

CAP = 2
EPSILON = 1e-05
LOG_TWO = math.log(2.0)
EMPTY = 1024.0

f32 = jnp.float32
bf16 = jnp.bfloat16
LANES = 128


def params():
    return pltpu.CompilerParams(vmem_limit_bytes=48 * 1024 * 1024)


def contract_last(a, b):
    return lax.dot_general(a, b, (((1,), (1,)), ((), ())), preferred_element_type=f32)


def partial_sums(x, w_ref):
    width = x.shape[1]
    inner = contract_last(x, w_ref[:, :width])
    hidden = 0.5 * inner * (1.0 + lax.erf(inner * math.sqrt(0.5)))
    return jnp.dot(hidden.astype(bf16), w_ref[:, width:], preferred_element_type=f32)


def first_kernel(own_ref, across_ref, along_ref, diagonal_ref, w_ref, out_ref):
    for n, x_ref in enumerate((own_ref, across_ref, along_ref, diagonal_ref)):
        out_ref[n] = partial_sums(x_ref[...], w_ref)


def first_half(xs, units):
    return pl.pallas_call(
        first_kernel,
        out_shape=jax.ShapeDtypeStruct((len(xs),) + xs[0].shape, f32),
        compiler_params=params(),
        name="encode",
    )(*xs, units)


def second_kernel(
    own_ref,
    across_ref,
    along_ref,
    diagonal_ref,
    w_ref,
    so_far_ref,
    kept_ref,
    later_ref,
    send_across_ref,
    send_along_ref,
):
    half = own_ref.shape[0] // 2
    diagonal = so_far_ref[3] + partial_sums(diagonal_ref[...], w_ref)
    across = so_far_ref[1] + partial_sums(across_ref[...], w_ref)
    send_across_ref[:half] = across[:half].astype(bf16)
    send_across_ref[half:] = diagonal[:half].astype(bf16)
    along = so_far_ref[2] + partial_sums(along_ref[...], w_ref)
    send_along_ref[:half] = along[half:].astype(bf16)
    send_along_ref[half:] = diagonal[half:].astype(bf16)
    later_ref[:half] = along[:half]
    later_ref[half:] = across[half:]
    kept_ref[...] = so_far_ref[0] + partial_sums(own_ref[...], w_ref)


def second_half(xs, units, so_far):
    kept = jax.ShapeDtypeStruct(xs[0].shape, f32)
    sent = jax.ShapeDtypeStruct(xs[0].shape, bf16)
    return pl.pallas_call(
        second_kernel,
        out_shape=(kept, kept, sent, sent),
        compiler_params=params(),
        name="encode_rest",
    )(*xs, units, so_far)


ROWS = 32


def place_kernel(
    cls_ref, kept_ref, across_ref, along_ref, last_ref, owner_ref, query_ref, out_ref
):
    rows, width = cls_ref.shape
    half = rows // 2
    blocks = owner_ref.shape[1]
    total = out_ref.shape[0]
    shards = total // ROWS
    chunks = width // LANES
    early = jnp.concatenate((across_ref[:half], along_ref[:half]), 0).astype(f32)
    resid = cls_ref[...].astype(f32) + kept_ref[...] + early + last_ref[...].astype(f32)
    centred = resid - jnp.mean(resid, -1, keepdims=True)
    variance = jnp.mean(centred * centred, -1, keepdims=True)
    fresh = (centred * lax.rsqrt(variance + EPSILON)).astype(bf16)

    owner = owner_ref[...]
    shard_of = lax.broadcasted_iota(jnp.int32, (shards, blocks), 0)
    onehot = (shard_of == owner).astype(f32)
    before = lax.broadcasted_iota(jnp.int32, (blocks, blocks), 0) < lax.broadcasted_iota(
        jnp.int32, (blocks, blocks), 1
    )
    earlier = jnp.dot(onehot.astype(bf16), before.astype(bf16), preferred_element_type=f32)
    slot = jnp.sum(earlier * onehot, 0, keepdims=True)
    passage = lax.broadcasted_iota(jnp.int32, (blocks, rows), 1)
    block = lax.broadcasted_iota(jnp.int32, (blocks, rows), 0)
    widen = (passage // 2 == block).astype(bf16)
    both = jnp.concatenate(
        (jnp.broadcast_to(owner.astype(f32), (8, blocks)), jnp.broadcast_to(slot, (8, blocks))), 0
    )
    both = jnp.dot(both.astype(bf16), widen, preferred_element_type=f32)
    parity = lax.broadcasted_iota(jnp.int32, (1, rows), 1) & 1
    target = both[0:1] * ROWS + (both[8:9] * 2.0 + parity.astype(f32)) * chunks

    row = lax.broadcasted_iota(jnp.int32, (total, rows), 0).astype(f32)
    placed = jnp.zeros((total, LANES), f32)
    taken = jnp.zeros((total, rows), f32)
    for j in range(chunks):
        onto = (row == target + float(j)).astype(f32)
        taken = taken + onto
        placed = placed + jnp.dot(
            onto.astype(bf16), fresh[:, j * LANES : (j + 1) * LANES], preferred_element_type=f32
        )
    filled = jnp.dot(taken.astype(bf16), jnp.ones((rows, LANES), bf16), preferred_element_type=f32)
    rest = jnp.broadcast_to(query_ref[...].astype(f32)[None], (shards, ROWS, LANES))
    out_ref[...] = jnp.where(filled > 0.5, placed, rest.reshape(total, LANES)).astype(bf16)


def place(cls_states, kept, across, along, last, owner, query, shards):
    return pl.pallas_call(
        place_kernel,
        out_shape=jax.ShapeDtypeStruct((shards * ROWS, LANES), bf16),
        compiler_params=params(),
        name="place",
    )(cls_states, kept, across, along, last, owner, query)


def score_kernel(recv_ref, stale_ref, idsg_ref, refreshed_ref, packed_ref, recv_s, arrived_s):
    cache_rows, width = stale_ref.shape
    shards = recv_ref.shape[0] // ROWS
    chunks = width // LANES
    per_shard = cache_rows // shards
    recv_s[...] = recv_ref[...].astype(f32)
    queries = []
    for j in range(chunks):
        for c in range(per_shard):
            arrived_s[j, pl.ds(c, shards, stride=per_shard), :] = recv_s[
                pl.ds(c * chunks + j, shards, stride=ROWS), :
            ]
        queries.append(recv_s[pl.ds(per_shard * chunks + j, shards, stride=ROWS), :])
    queries = jnp.concatenate(queries, 1).astype(bf16)
    arrived = jnp.concatenate([arrived_s[j] for j in range(chunks)], 1)
    refreshed = jnp.where(arrived > 0.5 * EMPTY, stale_ref[...].astype(f32), arrived).astype(bf16)
    refreshed_ref[...] = refreshed
    scores = contract_last(queries, refreshed)
    ids = idsg_ref[...]
    lane = lax.broadcasted_iota(jnp.int32, ids.shape, 1)
    low = ids & (LANES - 1)
    picked = jnp.zeros(ids.shape, f32)
    for part in range(cache_rows // LANES):
        here = jnp.take_along_axis(scores[:, part * LANES : (part + 1) * LANES], low, axis=1)
        picked = jnp.where(ids // LANES == part, here, picked)
    packed_ref[...] = jnp.where(lane < LANES // 2, picked, ids.astype(f32))


def score(recv, stale, idsg):
    return pl.pallas_call(
        score_kernel,
        out_shape=(
            jax.ShapeDtypeStruct(stale.shape, bf16),
            jax.ShapeDtypeStruct(idsg.shape, f32),
        ),
        scratch_shapes=[
            pltpu.VMEM(recv.shape, f32),
            pltpu.VMEM((stale.shape[1] // LANES, stale.shape[0], LANES), f32),
        ],
        compiler_params=params(),
        name="score",
    )(recv, stale, idsg)


HALF = LANES // 2


def pair_kernel(
    x_ref, discount_ref, grad_ref, loss_ref, half_s, wide_w, columns, across, rows_s, near_q, far_q
):
    x = x_ref[...]
    n_blocks = x.shape[0] // 2
    count = n_blocks * LANES
    top, low = x[:n_blocks], x[n_blocks:]
    lane = lax.broadcasted_iota(jnp.int32, (n_blocks, LANES), 1)
    left = lane < HALF
    scores = jnp.where(left, top, pltpu.roll(low, HALF, 1))
    gains = jnp.exp2(jnp.where(left, pltpu.roll(top, HALF, 1), low))
    position = lax.broadcasted_iota(jnp.int32, (n_blocks, LANES), 0) * LANES + lane

    ordered = jnp.ones((n_blocks, LANES), f32)
    for level in range(1, 5):
        above = jnp.sum((gains > float(2**level) - 0.5).astype(f32))
        ordered = jnp.where(position.astype(f32) < above, float(2**level), ordered)
    ideal = jnp.sum(ordered * discount_ref[...])

    span = n_blocks // 2
    groups = LANES // 8

    def sweep(values, load_or_make):
        columns[...] = jnp.zeros_like(columns)
        values[n_blocks:] = values[:n_blocks]

        def spread(i, _):
            rows_s[i] = jnp.broadcast_to(values[pl.ds(i, 1), :], (LANES, LANES)).T
            return 0

        lax.fori_loop(0, n_blocks, spread, 0, unroll=8)

        def block(i, last):
            first = [rows_s[i, pl.ds(8 * g, 8), :] for g in range(groups)]
            acc = [jnp.zeros((8, LANES), f32) for _ in range(groups)]
            for d in range(last + 1):
                k = i + d
                kept = near_q.at[i, d] if d < span else far_q.at[i]
                v_k = jnp.broadcast_to(values[pl.ds(k, 1), :], (8, LANES))
                column = [jnp.zeros((8, LANES), f32) for _ in range(4)]
                for g in range(groups):
                    value = load_or_make(first[g], v_k, kept, 8 * g)
                    acc[g] = acc[g] + value
                    column[g % 4] = column[g % 4] + value
                if d > 0:
                    columns[k] = columns[k] + ((column[0] + column[1]) + (column[2] + column[3]))
            for g in range(groups):
                rows_s[i, pl.ds(8 * g, 8), :] = acc[g]
            return 0

        lax.fori_loop(0, span, lambda i, _: block(i, span), 0)
        lax.fori_loop(span, n_blocks, lambda i, _: block(i, span - 1), 0)

        def collect(i, _):
            across[pl.ds(i, 1), :] = jnp.sum(rows_s[i].T, 0, keepdims=True)
            return 0

        lax.fori_loop(0, n_blocks, collect, 0, unroll=8)
        folded = jnp.sum(columns[...], 1)
        wrapped = jnp.concatenate((folded[n_blocks:], jnp.zeros((span, LANES), f32)), 0)
        return across[...] - folded[:n_blocks] - wrapped

    def rank_term(s_i, s_k, kept, at):
        t = jnp.tanh(s_k - s_i)
        kept[pl.ds(at, 8), :] = 1.0 - t * t
        return t

    def cross_term(w_i, w_k, kept, at):
        return (w_k - w_i) * kept[pl.ds(at, 8), :]

    half_s[:n_blocks] = 0.5 * scores
    rank = 0.5 + 0.5 * count + 0.5 * sweep(half_s, rank_term)
    logged = jnp.log2(1.0 + rank)
    weight = gains / (ideal * LOG_TWO * (1.0 + rank) * logged * logged)
    loss_ref[...] = jnp.full((1, LANES), 1.0 - jnp.sum(gains / logged) / ideal, f32)
    wide_w[:n_blocks] = 0.25 * weight
    grad = sweep(wide_w, cross_term).astype(bf16).astype(f32)
    grad_ref[:n_blocks] = grad
    grad_ref[n_blocks:] = pltpu.roll(grad, HALF, 1)


def pair(x, discount):
    n_blocks = x.shape[0] // 2
    span = n_blocks // 2
    return pl.pallas_call(
        pair_kernel,
        out_shape=(
            jax.ShapeDtypeStruct(x.shape, f32),
            jax.ShapeDtypeStruct((1, LANES), f32),
        ),
        scratch_shapes=[
            pltpu.VMEM((2 * n_blocks, LANES), f32),
            pltpu.VMEM((2 * n_blocks, LANES), f32),
            pltpu.VMEM((n_blocks + span, 8, LANES), f32),
            pltpu.VMEM((n_blocks, LANES), f32),
            pltpu.VMEM((n_blocks, LANES, LANES), f32),
            pltpu.VMEM((n_blocks, span, LANES, LANES), f32),
            pltpu.VMEM((span, LANES, LANES), f32),
        ],
        compiler_params=params(),
        name="pair",
    )(x, discount)


def share_kernel(grad_ref, idsg_ref, refreshed_ref, out_ref, rows_w):
    lists, cache_rows = rows_w.shape
    for g in range(lists // 8):
        part = slice(8 * g, 8 * g + 8)
        grads = grad_ref[part, :]
        ids = idsg_ref[part, :]
        spots = [
            lax.broadcasted_iota(jnp.int32, (8, LANES), 1) + LANES * p
            for p in range(cache_rows // LANES)
        ]
        acc = [jnp.zeros((8, LANES), f32) for _ in spots]
        for j in range(HALF):
            id_j = jnp.broadcast_to(ids[:, j : j + 1], (8, LANES))
            grad_j = jnp.broadcast_to(grads[:, j : j + 1], (8, LANES))
            acc = [a + jnp.where(id_j == spot, grad_j, 0.0) for a, spot in zip(acc, spots)]
        for p, a in enumerate(acc):
            rows_w[part, p * LANES : (p + 1) * LANES] = a
    weights = rows_w[...]
    high = weights.astype(bf16)
    rest = (weights - high.astype(f32)).astype(bf16)
    refreshed = refreshed_ref[...]
    out_ref[...] = jnp.dot(high, refreshed, preferred_element_type=f32) + jnp.dot(
        rest, refreshed, preferred_element_type=f32
    )


def share(grads, idsg, refreshed):
    return pl.pallas_call(
        share_kernel,
        out_shape=jax.ShapeDtypeStruct((grads.shape[0], refreshed.shape[1]), f32),
        scratch_shapes=[pltpu.VMEM((grads.shape[0], refreshed.shape[0]), f32)],
        compiler_params=params(),
        name="share",
    )(grads, idsg, refreshed)


Y, ZZ, ZL, X = 4, 4, 2, 2


def shard_at(y, zz, zl, x):
    return ((y * ZZ + zz) * ZL + zl) * X + x


def everywhere():
    return [
        (y, zz, zl, x) for y in range(Y) for zz in range(ZZ) for zl in range(ZL) for x in range(X)
    ]


def gather_units(block):
    groups = [
        [shard_at(y, zz, zl, x) for y in range(Y) for x in range(X)]
        for zz in range(ZZ)
        for zl in range(ZL)
    ]
    parts = len(groups[0])
    units, width = block.shape
    gathered = lax.all_to_all(
        jnp.broadcast_to(block[None], (parts, units, width)),
        "shard",
        split_axis=0,
        concat_axis=0,
        tiled=True,
        axis_index_groups=groups,
    )
    return gathered.reshape(parts * units, width)


def per_device(
    cls_states, trainer_in, trainer_out, stale_cache, block_owner, queries, neg_ids, grades
):
    shards = lax.axis_size("shard")
    roles = lax.axis_size("role")
    passages, width = cls_states.shape
    half = passages // 2
    barrier = lax.optimization_barrier

    def to_core(v):
        return lax.ppermute(v, "role", [(0, 1), (1, 0), (2, 3), (3, 2)])

    def to_across(v):
        return lax.ppermute(v, "role", [(0, 2), (1, 3), (2, 0), (3, 1)])

    def to_along(v):
        return lax.ppermute(
            v,
            "shard",
            [
                (shard_at(y, zz, zl, x), shard_at(y, zz, 1 - zl, x))
                for y, zz, zl, x in everywhere()
            ],
        )

    axes = ("role", "shard")
    mine = jnp.concatenate((trainer_in[0], trainer_out[0]), 1)
    mine = lax.ppermute(
        mine,
        axes,
        [
            ((roles - 1) * shards + shard_at(y, zz, zl, x), zz * shards + shard_at(y, zz, zl, x))
            for y, zz, zl, x in everywhere()
        ],
    )
    mine, cls_after = barrier((mine, cls_states))
    block = mine
    for by in range(1, ZZ):
        block = block + lax.ppermute(
            mine,
            axes,
            [
                (
                    zz * shards + shard_at(y, zz, zl, x),
                    zz * shards + shard_at(y, (zz + by) % ZZ, zl, x),
                )
                for y, zz, zl, x in everywhere()
            ],
        )
    x_across = to_across(cls_after)
    block, x_across, cls_after = barrier((block, x_across, cls_after))
    units = gather_units(block)
    xs = (cls_states, x_across, to_along(cls_after), to_along(x_across))
    units, xs = barrier((units, xs))
    other_units = to_core(units)
    so_far = first_half(xs, units)
    kept, later, for_across, for_along = second_half(xs, other_units, so_far)
    from_across = to_across(for_across)
    from_along = to_along(for_along)
    then_along = (later[:half] + from_across[half:].astype(f32)).astype(bf16)
    then_across = (later[half:] + from_along[half:].astype(f32)).astype(bf16)
    last = jnp.concatenate((to_along(then_along), to_across(then_across)), 0)
    chunks = width // LANES
    rest = jnp.concatenate(
        (
            jnp.full((2 * CAP * chunks, LANES), EMPTY, bf16),
            queries.reshape(chunks, LANES),
            jnp.full((ROWS - (2 * CAP + 1) * chunks, LANES), EMPTY, bf16),
        ),
        0,
    )
    idsg = jnp.concatenate((neg_ids, grades), 1)
    outgoing = place(
        cls_states, kept, from_across, from_along, last, block_owner.reshape(1, -1), rest, shards
    )
    outgoing, idsg = lax.optimization_barrier((outgoing, idsg))
    arrived = lax.all_to_all(
        outgoing.reshape(shards, ROWS, LANES), "shard", split_axis=0, concat_axis=0, tiled=True
    )
    refreshed, packed = score(arrived.reshape(-1, LANES), stale_cache, idsg)
    packed = lax.all_to_all(packed, "shard", split_axis=0, concat_axis=0, tiled=True)
    count = shards * neg_ids.shape[1]
    position = np.arange(1, count + 1, dtype=np.float64)
    discount = (1.0 / np.log2(1.0 + position)).astype(np.float32).reshape(-1, LANES)
    grads, loss = pair(packed, jnp.asarray(discount))
    grads = lax.all_to_all(grads, "shard", split_axis=0, concat_axis=0, tiled=True)
    shares = share(grads, idsg, refreshed)
    shares = lax.all_to_all(shares, "shard", split_axis=0, concat_axis=0, tiled=True)
    return refreshed, jnp.sum(shares, 0, keepdims=True), loss[0, :1]


def solution(mesh):
    return jax.shard_map(
        per_device,
        mesh=mesh,
        in_specs=(
            P(("role", "shard"), None),
            P("role", "shard", None),
            P("role", "shard", None),
            P(("role", "shard"), None),
            P(("role", "shard"), None),
            P(("role", "shard"), None),
            P("role", "shard"),
            P("role", "shard"),
        ),
        out_specs=(P(("role", "shard"), None), P(("role", "shard"), None), P(("role", "shard"))),
        check_vma=False,
    )
```

```python
import math

import jax
import jax.numpy as jnp
import numpy as np
from jax import lax
from jax.experimental import pallas as pl
from jax.experimental.pallas import tpu as pltpu
from jax.sharding import PartitionSpec as P

CAP = 2
EPSILON = 1e-05
LOG_TWO = math.log(2.0)
EMPTY = 1024.0

f32 = jnp.float32
bf16 = jnp.bfloat16
LANES = 128


def params():
    return pltpu.CompilerParams(vmem_limit_bytes=48 * 1024 * 1024)


def contract_last(a, b):
    return lax.dot_general(a, b, (((1,), (1,)), ((), ())), preferred_element_type=f32)


def partial_sums(x, w_ref):
    width = x.shape[1]
    inner = contract_last(x, w_ref[:, :width])
    hidden = 0.5 * inner * (1.0 + lax.erf(inner * math.sqrt(0.5)))
    return jnp.dot(hidden.astype(bf16), w_ref[:, width:], preferred_element_type=f32)


def first_kernel(own_ref, across_ref, along_ref, diagonal_ref, w_ref, out_ref):
    for n, x_ref in enumerate((own_ref, across_ref, along_ref, diagonal_ref)):
        out_ref[n] = partial_sums(x_ref[...], w_ref)


def first_half(xs, units):
    return pl.pallas_call(
        first_kernel,
        out_shape=jax.ShapeDtypeStruct((len(xs),) + xs[0].shape, f32),
        compiler_params=params(),
        name="encode",
    )(*xs, units)


def second_kernel(
    own_ref,
    across_ref,
    along_ref,
    diagonal_ref,
    w_ref,
    so_far_ref,
    kept_ref,
    later_ref,
    send_across_ref,
    send_along_ref,
):
    half = own_ref.shape[0] // 2
    diagonal = so_far_ref[3] + partial_sums(diagonal_ref[...], w_ref)
    across = so_far_ref[1] + partial_sums(across_ref[...], w_ref)
    send_across_ref[:half] = across[:half].astype(bf16)
    send_across_ref[half:] = diagonal[:half].astype(bf16)
    along = so_far_ref[2] + partial_sums(along_ref[...], w_ref)
    send_along_ref[:half] = along[half:].astype(bf16)
    send_along_ref[half:] = diagonal[half:].astype(bf16)
    later_ref[:half] = along[:half]
    later_ref[half:] = across[half:]
    kept_ref[...] = so_far_ref[0] + partial_sums(own_ref[...], w_ref)


def second_half(xs, units, so_far):
    kept = jax.ShapeDtypeStruct(xs[0].shape, f32)
    sent = jax.ShapeDtypeStruct(xs[0].shape, bf16)
    return pl.pallas_call(
        second_kernel,
        out_shape=(kept, kept, sent, sent),
        compiler_params=params(),
        name="encode_rest",
    )(*xs, units, so_far)


ROWS = 32


def place_kernel(
    cls_ref, kept_ref, across_ref, along_ref, last_ref, owner_ref, query_ref, out_ref
):
    rows, width = cls_ref.shape
    half = rows // 2
    blocks = owner_ref.shape[1]
    total = out_ref.shape[0]
    shards = total // ROWS
    chunks = width // LANES
    early = jnp.concatenate((across_ref[:half], along_ref[:half]), 0).astype(f32)
    resid = cls_ref[...].astype(f32) + kept_ref[...] + early + last_ref[...].astype(f32)
    centred = resid - jnp.mean(resid, -1, keepdims=True)
    variance = jnp.mean(centred * centred, -1, keepdims=True)
    fresh = (centred * lax.rsqrt(variance + EPSILON)).astype(bf16)

    owner = owner_ref[...]
    shard_of = lax.broadcasted_iota(jnp.int32, (shards, blocks), 0)
    onehot = (shard_of == owner).astype(f32)
    before = lax.broadcasted_iota(jnp.int32, (blocks, blocks), 0) < lax.broadcasted_iota(
        jnp.int32, (blocks, blocks), 1
    )
    earlier = jnp.dot(onehot.astype(bf16), before.astype(bf16), preferred_element_type=f32)
    slot = jnp.sum(earlier * onehot, 0, keepdims=True)
    passage = lax.broadcasted_iota(jnp.int32, (blocks, rows), 1)
    block = lax.broadcasted_iota(jnp.int32, (blocks, rows), 0)
    widen = (passage // 2 == block).astype(bf16)
    both = jnp.concatenate(
        (jnp.broadcast_to(owner.astype(f32), (8, blocks)), jnp.broadcast_to(slot, (8, blocks))), 0
    )
    both = jnp.dot(both.astype(bf16), widen, preferred_element_type=f32)
    parity = lax.broadcasted_iota(jnp.int32, (1, rows), 1) & 1
    target = both[0:1] * ROWS + (both[8:9] * 2.0 + parity.astype(f32)) * chunks

    row = lax.broadcasted_iota(jnp.int32, (total, rows), 0).astype(f32)
    placed = jnp.zeros((total, LANES), f32)
    taken = jnp.zeros((total, rows), f32)
    for j in range(chunks):
        onto = (row == target + float(j)).astype(f32)
        taken = taken + onto
        placed = placed + jnp.dot(
            onto.astype(bf16), fresh[:, j * LANES : (j + 1) * LANES], preferred_element_type=f32
        )
    filled = jnp.dot(taken.astype(bf16), jnp.ones((rows, LANES), bf16), preferred_element_type=f32)
    rest = jnp.broadcast_to(query_ref[...].astype(f32)[None], (shards, ROWS, LANES))
    out_ref[...] = jnp.where(filled > 0.5, placed, rest.reshape(total, LANES)).astype(bf16)


def place(cls_states, kept, across, along, last, owner, query, shards):
    return pl.pallas_call(
        place_kernel,
        out_shape=jax.ShapeDtypeStruct((shards * ROWS, LANES), bf16),
        compiler_params=params(),
        name="place",
    )(cls_states, kept, across, along, last, owner, query)


def score_kernel(
    recv_ref, stale_ref, idsg_ref, refreshed_ref, again_ref, packed_ref, recv_s, arrived_s
):
    cache_rows, width = stale_ref.shape
    shards = recv_ref.shape[0] // ROWS
    chunks = width // LANES
    per_shard = cache_rows // shards
    recv_s[...] = recv_ref[...].astype(f32)
    queries = []
    for j in range(chunks):
        for c in range(per_shard):
            arrived_s[j, pl.ds(c, shards, stride=per_shard), :] = recv_s[
                pl.ds(c * chunks + j, shards, stride=ROWS), :
            ]
        queries.append(recv_s[pl.ds(per_shard * chunks + j, shards, stride=ROWS), :])
    queries = jnp.concatenate(queries, 1).astype(bf16)
    arrived = jnp.concatenate([arrived_s[j] for j in range(chunks)], 1)
    refreshed = jnp.where(arrived > 0.5 * EMPTY, stale_ref[...].astype(f32), arrived).astype(bf16)
    refreshed_ref[...] = refreshed
    again_ref[...] = refreshed
    scores = contract_last(queries, refreshed)
    ids = idsg_ref[...]
    lane = lax.broadcasted_iota(jnp.int32, ids.shape, 1)
    low = ids & (LANES - 1)
    picked = jnp.zeros(ids.shape, f32)
    for part in range(cache_rows // LANES):
        here = jnp.take_along_axis(scores[:, part * LANES : (part + 1) * LANES], low, axis=1)
        picked = jnp.where(ids // LANES == part, here, picked)
    packed_ref[...] = jnp.where(lane < LANES // 2, picked, ids.astype(f32))


def score(recv, stale, idsg):
    return pl.pallas_call(
        score_kernel,
        out_shape=(
            jax.ShapeDtypeStruct(stale.shape, bf16),
            jax.ShapeDtypeStruct(stale.shape, bf16),
            jax.ShapeDtypeStruct(idsg.shape, f32),
        ),
        scratch_shapes=[
            pltpu.VMEM(recv.shape, f32),
            pltpu.VMEM((stale.shape[1] // LANES, stale.shape[0], LANES), f32),
        ],
        compiler_params=params(),
        name="score",
    )(recv, stale, idsg)


HALF = LANES // 2


def pair_kernel(
    x_ref, discount_ref, grad_ref, loss_ref, half_s, wide_w, columns, across, rows_s, near_q, far_q
):
    x = x_ref[...]
    n_blocks = x.shape[0] // 2
    count = n_blocks * LANES
    top, low = x[:n_blocks], x[n_blocks:]
    lane = lax.broadcasted_iota(jnp.int32, (n_blocks, LANES), 1)
    left = lane < HALF
    scores = jnp.where(left, top, pltpu.roll(low, HALF, 1))
    gains = jnp.exp2(jnp.where(left, pltpu.roll(top, HALF, 1), low))
    position = lax.broadcasted_iota(jnp.int32, (n_blocks, LANES), 0) * LANES + lane

    ordered = jnp.ones((n_blocks, LANES), f32)
    for level in range(1, 5):
        above = jnp.sum((gains > float(2**level) - 0.5).astype(f32))
        ordered = jnp.where(position.astype(f32) < above, float(2**level), ordered)
    ideal = jnp.sum(ordered * discount_ref[...])

    span = n_blocks // 2
    groups = LANES // 8

    def sweep(values, load_or_make):
        columns[...] = jnp.zeros_like(columns)
        values[n_blocks:] = values[:n_blocks]

        def spread(i, _):
            rows_s[i] = jnp.broadcast_to(values[pl.ds(i, 1), :], (LANES, LANES)).T
            return 0

        lax.fori_loop(0, n_blocks, spread, 0, unroll=8)

        def block(i, last):
            first = [rows_s[i, pl.ds(8 * g, 8), :] for g in range(groups)]
            acc = [jnp.zeros((8, LANES), f32) for _ in range(groups)]
            for d in range(last + 1):
                k = i + d
                kept = near_q.at[i, d] if d < span else far_q.at[i]
                v_k = jnp.broadcast_to(values[pl.ds(k, 1), :], (8, LANES))
                column = [jnp.zeros((8, LANES), f32) for _ in range(4)]
                for g in range(groups):
                    value = load_or_make(first[g], v_k, kept, 8 * g)
                    acc[g] = acc[g] + value
                    column[g % 4] = column[g % 4] + value
                if d > 0:
                    columns[k] = columns[k] + ((column[0] + column[1]) + (column[2] + column[3]))
            for g in range(groups):
                rows_s[i, pl.ds(8 * g, 8), :] = acc[g]
            return 0

        lax.fori_loop(0, span, lambda i, _: block(i, span), 0)
        lax.fori_loop(span, n_blocks, lambda i, _: block(i, span - 1), 0)

        def collect(i, _):
            across[pl.ds(i, 1), :] = jnp.sum(rows_s[i].T, 0, keepdims=True)
            return 0

        lax.fori_loop(0, n_blocks, collect, 0, unroll=8)
        folded = jnp.sum(columns[...], 1)
        wrapped = jnp.concatenate((folded[n_blocks:], jnp.zeros((span, LANES), f32)), 0)
        return across[...] - folded[:n_blocks] - wrapped

    def rank_term(s_i, s_k, kept, at):
        t = jnp.tanh(s_k - s_i)
        kept[pl.ds(at, 8), :] = 1.0 - t * t
        return t

    def cross_term(w_i, w_k, kept, at):
        return (w_k - w_i) * kept[pl.ds(at, 8), :]

    half_s[:n_blocks] = 0.5 * scores
    rank = 0.5 + 0.5 * count + 0.5 * sweep(half_s, rank_term)
    logged = jnp.log2(1.0 + rank)
    weight = gains / (ideal * LOG_TWO * (1.0 + rank) * logged * logged)
    loss_ref[...] = jnp.full((1, LANES), 1.0 - jnp.sum(gains / logged) / ideal, f32)
    wide_w[:n_blocks] = 0.25 * weight
    grad = sweep(wide_w, cross_term).astype(bf16).astype(f32)
    grad_ref[:n_blocks] = grad
    grad_ref[n_blocks:] = pltpu.roll(grad, HALF, 1)


def pair(x, discount):
    n_blocks = x.shape[0] // 2
    span = n_blocks // 2
    return pl.pallas_call(
        pair_kernel,
        out_shape=(
            jax.ShapeDtypeStruct(x.shape, f32),
            jax.ShapeDtypeStruct((1, LANES), f32),
        ),
        scratch_shapes=[
            pltpu.VMEM((2 * n_blocks, LANES), f32),
            pltpu.VMEM((2 * n_blocks, LANES), f32),
            pltpu.VMEM((n_blocks + span, 8, LANES), f32),
            pltpu.VMEM((n_blocks, LANES), f32),
            pltpu.VMEM((n_blocks, LANES, LANES), f32),
            pltpu.VMEM((n_blocks, span, LANES, LANES), f32),
            pltpu.VMEM((span, LANES, LANES), f32),
        ],
        compiler_params=params(),
        name="pair",
    )(x, discount)


def share_kernel(grad_ref, idsg_ref, refreshed_ref, out_ref, rows_w):
    lists, cache_rows = rows_w.shape
    for g in range(lists // 8):
        part = slice(8 * g, 8 * g + 8)
        grads = grad_ref[part, :]
        ids = idsg_ref[part, :]
        spots = [
            lax.broadcasted_iota(jnp.int32, (8, LANES), 1) + LANES * p
            for p in range(cache_rows // LANES)
        ]
        acc = [jnp.zeros((8, LANES), f32) for _ in spots]
        for j in range(HALF):
            id_j = jnp.broadcast_to(ids[:, j : j + 1], (8, LANES))
            grad_j = jnp.broadcast_to(grads[:, j : j + 1], (8, LANES))
            acc = [a + jnp.where(id_j == spot, grad_j, 0.0) for a, spot in zip(acc, spots)]
        for p, a in enumerate(acc):
            rows_w[part, p * LANES : (p + 1) * LANES] = a
    weights = rows_w[...]
    high = weights.astype(bf16)
    rest = (weights - high.astype(f32)).astype(bf16)
    refreshed = refreshed_ref[...]
    out_ref[...] = jnp.dot(high, refreshed, preferred_element_type=f32) + jnp.dot(
        rest, refreshed, preferred_element_type=f32
    )


def share(grads, idsg, refreshed):
    return pl.pallas_call(
        share_kernel,
        out_shape=jax.ShapeDtypeStruct((grads.shape[0], refreshed.shape[1]), f32),
        scratch_shapes=[pltpu.VMEM((grads.shape[0], refreshed.shape[0]), f32)],
        compiler_params=params(),
        name="share",
    )(grads, idsg, refreshed)


Y, ZZ, ZL, X = 4, 4, 2, 2


def shard_at(y, zz, zl, x):
    return ((y * ZZ + zz) * ZL + zl) * X + x


def everywhere():
    return [
        (y, zz, zl, x) for y in range(Y) for zz in range(ZZ) for zl in range(ZL) for x in range(X)
    ]


def gather_units(block):
    groups = [
        [shard_at(y, zz, zl, x) for y in range(Y) for x in range(X)]
        for zz in range(ZZ)
        for zl in range(ZL)
    ]
    parts = len(groups[0])
    units, width = block.shape
    gathered = lax.all_to_all(
        jnp.broadcast_to(block[None], (parts, units, width)),
        "shard",
        split_axis=0,
        concat_axis=0,
        tiled=True,
        axis_index_groups=groups,
    )
    return gathered.reshape(parts * units, width)


def per_device(
    cls_states, trainer_in, trainer_out, stale_cache, block_owner, queries, neg_ids, grades
):
    shards = lax.axis_size("shard")
    roles = lax.axis_size("role")
    passages, width = cls_states.shape
    half = passages // 2
    barrier = lax.optimization_barrier

    def to_core(v):
        return lax.ppermute(v, "role", [(0, 1), (1, 0), (2, 3), (3, 2)])

    def to_across(v):
        return lax.ppermute(v, "role", [(0, 2), (1, 3), (2, 0), (3, 1)])

    def to_along(v):
        return lax.ppermute(
            v,
            "shard",
            [
                (shard_at(y, zz, zl, x), shard_at(y, zz, 1 - zl, x))
                for y, zz, zl, x in everywhere()
            ],
        )

    x_across = to_across(cls_states)
    mine = jnp.concatenate((trainer_in[0], trainer_out[0]), 1)
    mine = lax.all_to_all(
        mine.reshape(roles, -1, 2 * width), "role", split_axis=0, concat_axis=0, tiled=True
    )[roles - 1]
    block = lax.all_to_all(
        jnp.broadcast_to(mine[None], (ZZ,) + mine.shape),
        "shard",
        split_axis=0,
        concat_axis=0,
        tiled=True,
        axis_index_groups=[
            [shard_at(y, zz, zl, x) for zz in range(ZZ)]
            for y in range(Y)
            for zl in range(ZL)
            for x in range(X)
        ],
    ).reshape(-1, 2 * width)
    block, x_across, cls_after = barrier((block, x_across, cls_states))
    units = gather_units(block)
    xs = (cls_states, x_across, to_along(cls_after), to_along(x_across))
    units, xs = barrier((units, xs))
    other_units = to_core(units)
    so_far = first_half(xs, units)
    kept, later, for_across, for_along = second_half(xs, other_units, so_far)
    from_across = to_across(for_across)
    from_along = to_along(for_along)
    then_along = (later[:half] + from_across[half:].astype(f32)).astype(bf16)
    then_across = (later[half:] + from_along[half:].astype(f32)).astype(bf16)
    last = jnp.concatenate((to_along(then_along), to_across(then_across)), 0)
    chunks = width // LANES
    rest = jnp.concatenate(
        (
            jnp.full((2 * CAP * chunks, LANES), EMPTY, bf16),
            queries.reshape(chunks, LANES),
            jnp.full((ROWS - (2 * CAP + 1) * chunks, LANES), EMPTY, bf16),
        ),
        0,
    )
    idsg = jnp.concatenate((neg_ids, grades), 1)
    outgoing = place(
        cls_states, kept, from_across, from_along, last, block_owner.reshape(1, -1), rest, shards
    )
    outgoing, idsg = lax.optimization_barrier((outgoing, idsg))
    arrived = lax.all_to_all(
        outgoing.reshape(shards, ROWS, LANES), "shard", split_axis=0, concat_axis=0, tiled=True
    )
    refreshed, again, packed = score(arrived.reshape(-1, LANES), stale_cache, idsg)
    packed = lax.all_to_all(packed, "shard", split_axis=0, concat_axis=0, tiled=True)
    count = shards * neg_ids.shape[1]
    position = np.arange(1, count + 1, dtype=np.float64)
    discount = (1.0 / np.log2(1.0 + position)).astype(np.float32).reshape(-1, LANES)
    grads, loss = pair(packed, jnp.asarray(discount))
    grads = lax.all_to_all(grads, "shard", split_axis=0, concat_axis=0, tiled=True)
    shares = share(grads, idsg, again)
    shares = lax.all_to_all(shares, "shard", split_axis=0, concat_axis=0, tiled=True)
    return refreshed, jnp.sum(shares, 0, keepdims=True), loss[0, :1]


def solution(mesh):
    return jax.shard_map(
        per_device,
        mesh=mesh,
        in_specs=(
            P(("role", "shard"), None),
            P("role", "shard", None),
            P("role", "shard", None),
            P(("role", "shard"), None),
            P(("role", "shard"), None),
            P(("role", "shard"), None),
            P("role", "shard"),
            P("role", "shard"),
        ),
        out_specs=(P(("role", "shard"), None), P(("role", "shard"), None), P(("role", "shard"))),
        check_vma=False,
    )
```

```python
import functools
import math

import jax
import jax.numpy as jnp
import numpy as np
from jax import lax
from jax.experimental import pallas as pl
from jax.experimental.pallas import tpu as pltpu
from jax.sharding import PartitionSpec as P

CAP = 2
EPSILON = 1e-05
LOG_TWO = math.log(2.0)
EMPTY = 1024.0

f32 = jnp.float32
bf16 = jnp.bfloat16
LANES = 128


def params():
    return pltpu.CompilerParams(vmem_limit_bytes=48 * 1024 * 1024)


def contract_last(a, b):
    return lax.dot_general(a, b, (((1,), (1,)), ((), ())), preferred_element_type=f32)


def partial_sums(x, w_ref):
    width = x.shape[1]
    inner = contract_last(x, w_ref[:, :width])
    hidden = 0.5 * inner * (1.0 + lax.erf(inner * math.sqrt(0.5)))
    return jnp.dot(hidden.astype(bf16), w_ref[:, width:], preferred_element_type=f32)


def first_kernel(own_ref, across_ref, along_ref, diagonal_ref, w_ref, out_ref):
    for n, x_ref in enumerate((own_ref, across_ref, along_ref, diagonal_ref)):
        out_ref[n] = partial_sums(x_ref[...], w_ref)


def first_half(xs, units):
    return pl.pallas_call(
        first_kernel,
        out_shape=jax.ShapeDtypeStruct((len(xs),) + xs[0].shape, f32),
        compiler_params=params(),
        name="encode",
    )(*xs, units)


def second_kernel(at, *refs):
    x_refs, (w_ref, so_far_ref), out_refs = refs[: len(at)], refs[len(at) :][:2], refs[-len(at) :]
    for n, x_ref, out_ref in zip(at, x_refs, out_refs):
        part = so_far_ref[n] + partial_sums(x_ref[...], w_ref)
        out_ref[...] = part.astype(out_ref.dtype)


def second_half(xs, units, so_far, at, dtype):
    return pl.pallas_call(
        functools.partial(second_kernel, at),
        out_shape=tuple(jax.ShapeDtypeStruct(xs[n].shape, dtype) for n in at),
        compiler_params=params(),
        name="encode_rest",
    )(*(xs[n] for n in at), units, so_far)


ROWS = 32


def place_kernel(
    cls_ref, own_ref, across_ref, along_ref, diagonal_ref, owner_ref, query_ref, out_ref
):
    rows, width = cls_ref.shape
    blocks = owner_ref.shape[1]
    total = out_ref.shape[0]
    shards = total // ROWS
    chunks = width // LANES
    resid = cls_ref[...].astype(f32) + own_ref[...]
    for part_ref in (across_ref, along_ref, diagonal_ref):
        resid = resid + part_ref[...].astype(f32)
    centred = resid - jnp.mean(resid, -1, keepdims=True)
    variance = jnp.mean(centred * centred, -1, keepdims=True)
    fresh = (centred * lax.rsqrt(variance + EPSILON)).astype(bf16)

    owner = owner_ref[...]
    shard_of = lax.broadcasted_iota(jnp.int32, (shards, blocks), 0)
    onehot = (shard_of == owner).astype(f32)
    before = lax.broadcasted_iota(jnp.int32, (blocks, blocks), 0) < lax.broadcasted_iota(
        jnp.int32, (blocks, blocks), 1
    )
    earlier = jnp.dot(onehot.astype(bf16), before.astype(bf16), preferred_element_type=f32)
    slot = jnp.sum(earlier * onehot, 0, keepdims=True)
    passage = lax.broadcasted_iota(jnp.int32, (blocks, rows), 1)
    block = lax.broadcasted_iota(jnp.int32, (blocks, rows), 0)
    widen = (passage // 2 == block).astype(bf16)
    both = jnp.concatenate(
        (jnp.broadcast_to(owner.astype(f32), (8, blocks)), jnp.broadcast_to(slot, (8, blocks))), 0
    )
    both = jnp.dot(both.astype(bf16), widen, preferred_element_type=f32)
    parity = lax.broadcasted_iota(jnp.int32, (1, rows), 1) & 1
    target = both[0:1] * ROWS + (both[8:9] * 2.0 + parity.astype(f32)) * chunks

    row = lax.broadcasted_iota(jnp.int32, (total, rows), 0).astype(f32)
    placed = jnp.zeros((total, LANES), f32)
    taken = jnp.zeros((total, rows), f32)
    for j in range(chunks):
        onto = (row == target + float(j)).astype(f32)
        taken = taken + onto
        placed = placed + jnp.dot(
            onto.astype(bf16), fresh[:, j * LANES : (j + 1) * LANES], preferred_element_type=f32
        )
    filled = jnp.dot(taken.astype(bf16), jnp.ones((rows, LANES), bf16), preferred_element_type=f32)
    rest = jnp.broadcast_to(query_ref[...].astype(f32)[None], (shards, ROWS, LANES))
    out_ref[...] = jnp.where(filled > 0.5, placed, rest.reshape(total, LANES)).astype(bf16)


def place(cls_states, own, across, along, diagonal, owner, query, shards):
    return pl.pallas_call(
        place_kernel,
        out_shape=jax.ShapeDtypeStruct((shards * ROWS, LANES), bf16),
        compiler_params=params(),
        name="place",
    )(cls_states, own, across, along, diagonal, owner, query)


def score_kernel(
    recv_ref, stale_ref, idsg_ref, refreshed_ref, again_ref, packed_ref, recv_s, arrived_s
):
    cache_rows, width = stale_ref.shape
    shards = recv_ref.shape[0] // ROWS
    chunks = width // LANES
    per_shard = cache_rows // shards
    recv_s[...] = recv_ref[...].astype(f32)
    queries = []
    for j in range(chunks):
        for c in range(per_shard):
            arrived_s[j, pl.ds(c, shards, stride=per_shard), :] = recv_s[
                pl.ds(c * chunks + j, shards, stride=ROWS), :
            ]
        queries.append(recv_s[pl.ds(per_shard * chunks + j, shards, stride=ROWS), :])
    queries = jnp.concatenate(queries, 1).astype(bf16)
    arrived = jnp.concatenate([arrived_s[j] for j in range(chunks)], 1)
    refreshed = jnp.where(arrived > 0.5 * EMPTY, stale_ref[...].astype(f32), arrived).astype(bf16)
    refreshed_ref[...] = refreshed
    again_ref[...] = refreshed
    scores = contract_last(queries, refreshed)
    ids = idsg_ref[...]
    lane = lax.broadcasted_iota(jnp.int32, ids.shape, 1)
    low = ids & (LANES - 1)
    picked = jnp.zeros(ids.shape, f32)
    for part in range(cache_rows // LANES):
        here = jnp.take_along_axis(scores[:, part * LANES : (part + 1) * LANES], low, axis=1)
        picked = jnp.where(ids // LANES == part, here, picked)
    packed_ref[...] = jnp.where(lane < LANES // 2, picked, ids.astype(f32))


def score(recv, stale, idsg):
    return pl.pallas_call(
        score_kernel,
        out_shape=(
            jax.ShapeDtypeStruct(stale.shape, bf16),
            jax.ShapeDtypeStruct(stale.shape, bf16),
            jax.ShapeDtypeStruct(idsg.shape, f32),
        ),
        scratch_shapes=[
            pltpu.VMEM(recv.shape, f32),
            pltpu.VMEM((stale.shape[1] // LANES, stale.shape[0], LANES), f32),
        ],
        compiler_params=params(),
        name="score",
    )(recv, stale, idsg)


HALF = LANES // 2


def pair_kernel(
    x_ref, discount_ref, grad_ref, loss_ref, half_s, wide_w, columns, across, rows_s, near_q, far_q
):
    x = x_ref[...]
    n_blocks = x.shape[0] // 2
    count = n_blocks * LANES
    top, low = x[:n_blocks], x[n_blocks:]
    lane = lax.broadcasted_iota(jnp.int32, (n_blocks, LANES), 1)
    left = lane < HALF
    scores = jnp.where(left, top, pltpu.roll(low, HALF, 1))
    gains = jnp.exp2(jnp.where(left, pltpu.roll(top, HALF, 1), low))
    position = lax.broadcasted_iota(jnp.int32, (n_blocks, LANES), 0) * LANES + lane

    ordered = jnp.ones((n_blocks, LANES), f32)
    for level in range(1, 5):
        above = jnp.sum((gains > float(2**level) - 0.5).astype(f32))
        ordered = jnp.where(position.astype(f32) < above, float(2**level), ordered)
    ideal = jnp.sum(ordered * discount_ref[...])

    span = n_blocks // 2
    groups = LANES // 8

    def sweep(values, load_or_make):
        columns[...] = jnp.zeros_like(columns)
        values[n_blocks:] = values[:n_blocks]

        def spread(i, _):
            rows_s[i] = jnp.broadcast_to(values[pl.ds(i, 1), :], (LANES, LANES)).T
            return 0

        lax.fori_loop(0, n_blocks, spread, 0, unroll=8)

        def block(i, last):
            first = [rows_s[i, pl.ds(8 * g, 8), :] for g in range(groups)]
            acc = [jnp.zeros((8, LANES), f32) for _ in range(groups)]
            for d in range(last + 1):
                k = i + d
                kept = near_q.at[i, d] if d < span else far_q.at[i]
                v_k = jnp.broadcast_to(values[pl.ds(k, 1), :], (8, LANES))
                column = [jnp.zeros((8, LANES), f32) for _ in range(4)]
                for g in range(groups):
                    value = load_or_make(first[g], v_k, kept, 8 * g)
                    acc[g] = acc[g] + value
                    column[g % 4] = column[g % 4] + value
                if d > 0:
                    columns[k] = columns[k] + ((column[0] + column[1]) + (column[2] + column[3]))
            for g in range(groups):
                rows_s[i, pl.ds(8 * g, 8), :] = acc[g]
            return 0

        lax.fori_loop(0, span, lambda i, _: block(i, span), 0)
        lax.fori_loop(span, n_blocks, lambda i, _: block(i, span - 1), 0)

        def collect(i, _):
            across[pl.ds(i, 1), :] = jnp.sum(rows_s[i].T, 0, keepdims=True)
            return 0

        lax.fori_loop(0, n_blocks, collect, 0, unroll=8)
        folded = jnp.sum(columns[...], 1)
        wrapped = jnp.concatenate((folded[n_blocks:], jnp.zeros((span, LANES), f32)), 0)
        return across[...] - folded[:n_blocks] - wrapped

    def rank_term(s_i, s_k, kept, at):
        t = jnp.tanh(s_k - s_i)
        kept[pl.ds(at, 8), :] = 1.0 - t * t
        return t

    def cross_term(w_i, w_k, kept, at):
        return (w_k - w_i) * kept[pl.ds(at, 8), :]

    half_s[:n_blocks] = 0.5 * scores
    rank = 0.5 + 0.5 * count + 0.5 * sweep(half_s, rank_term)
    logged = jnp.log2(1.0 + rank)
    weight = gains / (ideal * LOG_TWO * (1.0 + rank) * logged * logged)
    loss_ref[...] = jnp.full((1, LANES), 1.0 - jnp.sum(gains / logged) / ideal, f32)
    wide_w[:n_blocks] = 0.25 * weight
    grad = sweep(wide_w, cross_term).astype(bf16).astype(f32)
    grad_ref[:n_blocks] = grad
    grad_ref[n_blocks:] = pltpu.roll(grad, HALF, 1)


def pair(x, discount):
    n_blocks = x.shape[0] // 2
    span = n_blocks // 2
    return pl.pallas_call(
        pair_kernel,
        out_shape=(
            jax.ShapeDtypeStruct(x.shape, f32),
            jax.ShapeDtypeStruct((1, LANES), f32),
        ),
        scratch_shapes=[
            pltpu.VMEM((2 * n_blocks, LANES), f32),
            pltpu.VMEM((2 * n_blocks, LANES), f32),
            pltpu.VMEM((n_blocks + span, 8, LANES), f32),
            pltpu.VMEM((n_blocks, LANES), f32),
            pltpu.VMEM((n_blocks, LANES, LANES), f32),
            pltpu.VMEM((n_blocks, span, LANES, LANES), f32),
            pltpu.VMEM((span, LANES, LANES), f32),
        ],
        compiler_params=params(),
        name="pair",
    )(x, discount)


def share_kernel(grad_ref, idsg_ref, refreshed_ref, out_ref, rows_w):
    lists, cache_rows = rows_w.shape
    for g in range(lists // 8):
        part = slice(8 * g, 8 * g + 8)
        grads = grad_ref[part, :]
        ids = idsg_ref[part, :]
        spots = [
            lax.broadcasted_iota(jnp.int32, (8, LANES), 1) + LANES * p
            for p in range(cache_rows // LANES)
        ]
        acc = [jnp.zeros((8, LANES), f32) for _ in spots]
        for j in range(HALF):
            id_j = jnp.broadcast_to(ids[:, j : j + 1], (8, LANES))
            grad_j = jnp.broadcast_to(grads[:, j : j + 1], (8, LANES))
            acc = [a + jnp.where(id_j == spot, grad_j, 0.0) for a, spot in zip(acc, spots)]
        for p, a in enumerate(acc):
            rows_w[part, p * LANES : (p + 1) * LANES] = a
    weights = rows_w[...]
    high = weights.astype(bf16)
    rest = (weights - high.astype(f32)).astype(bf16)
    refreshed = refreshed_ref[...]
    out_ref[...] = jnp.dot(high, refreshed, preferred_element_type=f32) + jnp.dot(
        rest, refreshed, preferred_element_type=f32
    )


def share(grads, idsg, refreshed):
    return pl.pallas_call(
        share_kernel,
        out_shape=jax.ShapeDtypeStruct((grads.shape[0], refreshed.shape[1]), f32),
        scratch_shapes=[pltpu.VMEM((grads.shape[0], refreshed.shape[0]), f32)],
        compiler_params=params(),
        name="share",
    )(grads, idsg, refreshed)


Y, ZZ, ZL, X = 4, 4, 2, 2


def shard_at(y, zz, zl, x):
    return ((y * ZZ + zz) * ZL + zl) * X + x


def everywhere():
    return [
        (y, zz, zl, x) for y in range(Y) for zz in range(ZZ) for zl in range(ZL) for x in range(X)
    ]


def gather_units(block):
    groups = [
        [shard_at(y, zz, zl, x) for y in range(Y) for x in range(X)]
        for zz in range(ZZ)
        for zl in range(ZL)
    ]
    parts = len(groups[0])
    units, width = block.shape
    gathered = lax.all_to_all(
        jnp.broadcast_to(block[None], (parts, units, width)),
        "shard",
        split_axis=0,
        concat_axis=0,
        tiled=True,
        axis_index_groups=groups,
    )
    return gathered.reshape(parts * units, width)


def per_device(
    cls_states, trainer_in, trainer_out, stale_cache, block_owner, queries, neg_ids, grades
):
    shards = lax.axis_size("shard")
    roles = lax.axis_size("role")
    width = cls_states.shape[1]
    barrier = lax.optimization_barrier

    def to_core(v):
        return lax.ppermute(v, "role", [(0, 1), (1, 0), (2, 3), (3, 2)])

    def to_across(v):
        return lax.ppermute(v, "role", [(0, 2), (1, 3), (2, 0), (3, 1)])

    def to_along(v):
        return lax.ppermute(
            v,
            "shard",
            [
                (shard_at(y, zz, zl, x), shard_at(y, zz, 1 - zl, x))
                for y, zz, zl, x in everywhere()
            ],
        )

    def to_diagonal(v):
        return lax.ppermute(
            v,
            ("role", "shard"),
            [
                (r * shards + shard_at(y, zz, zl, x), (r ^ 2) * shards + shard_at(y, zz, 1 - zl, x))
                for r in range(roles)
                for y, zz, zl, x in everywhere()
            ],
        )

    pieces = jnp.concatenate((trainer_in[0], trainer_out[0]), 1).reshape(roles, -1, 2 * width)
    role = lax.axis_index("role")
    arrived = [lax.ppermute(pieces[k], "role", [(roles - 1, k)]) for k in range(roles - 1)]
    mine = pieces[roles - 1]
    for k in range(roles - 1):
        mine = jnp.where(role == k, arrived[k], mine)
    mine, cls_after = barrier((mine, cls_states))
    block = [mine]
    for by in range(1, ZZ):
        turn = [
            (shard_at(y, zz, zl, x), shard_at(y, (zz + by) % ZZ, zl, x))
            for y, zz, zl, x in everywhere()
        ]
        block.append(lax.ppermute(mine, "shard", turn))
    block = jnp.concatenate(block, 0)
    x_across = to_across(cls_after)
    block, x_across, cls_after = barrier((block, x_across, cls_after))
    units = gather_units(block)
    xs = (cls_states, x_across, to_along(cls_after), to_along(x_across))
    units, xs = barrier((units, xs))
    other_units = to_core(units)
    so_far = first_half(xs, units)
    (diagonal,) = second_half(xs, other_units, so_far, (3,), bf16)
    from_diagonal = to_diagonal(diagonal)
    across, along = second_half(xs, other_units, so_far, (1, 2), bf16)
    from_across = to_across(across)
    from_along = to_along(along)
    (own,) = second_half(xs, other_units, so_far, (0,), f32)
    chunks = width // LANES
    rest = jnp.concatenate(
        (
            jnp.full((2 * CAP * chunks, LANES), EMPTY, bf16),
            queries.reshape(chunks, LANES),
            jnp.full((ROWS - (2 * CAP + 1) * chunks, LANES), EMPTY, bf16),
        ),
        0,
    )
    idsg = jnp.concatenate((neg_ids, grades), 1)
    outgoing = place(
        cls_states,
        own,
        from_across,
        from_along,
        from_diagonal,
        block_owner.reshape(1, -1),
        rest,
        shards,
    )
    outgoing, idsg = lax.optimization_barrier((outgoing, idsg))
    arrived = lax.all_to_all(
        outgoing.reshape(shards, ROWS, LANES), "shard", split_axis=0, concat_axis=0, tiled=True
    )
    refreshed, again, packed = score(arrived.reshape(-1, LANES), stale_cache, idsg)
    packed = lax.all_to_all(packed, "shard", split_axis=0, concat_axis=0, tiled=True)
    count = shards * neg_ids.shape[1]
    position = np.arange(1, count + 1, dtype=np.float64)
    discount = (1.0 / np.log2(1.0 + position)).astype(np.float32).reshape(-1, LANES)
    grads, loss = pair(packed, jnp.asarray(discount))
    grads = lax.all_to_all(grads, "shard", split_axis=0, concat_axis=0, tiled=True)
    shares = share(grads, idsg, again)
    shares = lax.all_to_all(shares, "shard", split_axis=0, concat_axis=0, tiled=True)
    return refreshed, jnp.sum(shares, 0, keepdims=True), loss[0, :1]


def solution(mesh):
    return jax.shard_map(
        per_device,
        mesh=mesh,
        in_specs=(
            P(("role", "shard"), None),
            P("role", "shard", None),
            P("role", "shard", None),
            P(("role", "shard"), None),
            P(("role", "shard"), None),
            P(("role", "shard"), None),
            P("role", "shard"),
            P("role", "shard"),
        ),
        out_specs=(P(("role", "shard"), None), P(("role", "shard"), None), P(("role", "shard"))),
        check_vma=False,
    )
```

```python
import functools
import math

import jax
import jax.numpy as jnp
import numpy as np
from jax import lax
from jax.experimental import pallas as pl
from jax.experimental.pallas import tpu as pltpu
from jax.sharding import PartitionSpec as P

CAP = 2
EPSILON = 1e-05
LOG_TWO = math.log(2.0)
EMPTY = 1024.0

f32 = jnp.float32
bf16 = jnp.bfloat16
LANES = 128


def params():
    return pltpu.CompilerParams(vmem_limit_bytes=48 * 1024 * 1024)


def contract_last(a, b):
    return lax.dot_general(a, b, (((1,), (1,)), ((), ())), preferred_element_type=f32)


def partial_sums(x, w_ref):
    width = x.shape[1]
    inner = contract_last(x, w_ref[:, :width])
    hidden = 0.5 * inner * (1.0 + lax.erf(inner * math.sqrt(0.5)))
    return jnp.dot(hidden.astype(bf16), w_ref[:, width:], preferred_element_type=f32)


def first_kernel(own_ref, across_ref, along_ref, diagonal_ref, w_ref, out_ref):
    for n, x_ref in enumerate((own_ref, across_ref, along_ref, diagonal_ref)):
        out_ref[n] = partial_sums(x_ref[...], w_ref)


def first_half(xs, units):
    return pl.pallas_call(
        first_kernel,
        out_shape=jax.ShapeDtypeStruct((len(xs),) + xs[0].shape, f32),
        compiler_params=params(),
        name="encode",
    )(*xs, units)


def second_kernel(at, *refs):
    x_refs, (w_ref, so_far_ref), out_refs = refs[: len(at)], refs[len(at) :][:2], refs[-len(at) :]
    for n, x_ref, out_ref in zip(at, x_refs, out_refs):
        part = so_far_ref[n] + partial_sums(x_ref[...], w_ref)
        out_ref[...] = part.astype(out_ref.dtype)


def second_half(xs, units, so_far, at, dtype):
    return pl.pallas_call(
        functools.partial(second_kernel, at),
        out_shape=tuple(jax.ShapeDtypeStruct(xs[n].shape, dtype) for n in at),
        compiler_params=params(),
        name="encode_rest",
    )(*(xs[n] for n in at), units, so_far)


ROWS = 32


def place_kernel(
    cls_ref, own_ref, across_ref, along_ref, diagonal_ref, owner_ref, query_ref, out_ref
):
    rows, width = cls_ref.shape
    blocks = owner_ref.shape[1]
    total = out_ref.shape[0]
    shards = total // ROWS
    chunks = width // LANES
    resid = cls_ref[...].astype(f32) + own_ref[...]
    for part_ref in (across_ref, along_ref, diagonal_ref):
        resid = resid + part_ref[...].astype(f32)
    centred = resid - jnp.mean(resid, -1, keepdims=True)
    variance = jnp.mean(centred * centred, -1, keepdims=True)
    fresh = (centred * lax.rsqrt(variance + EPSILON)).astype(bf16)

    owner = owner_ref[...]
    shard_of = lax.broadcasted_iota(jnp.int32, (shards, blocks), 0)
    onehot = (shard_of == owner).astype(f32)
    before = lax.broadcasted_iota(jnp.int32, (blocks, blocks), 0) < lax.broadcasted_iota(
        jnp.int32, (blocks, blocks), 1
    )
    earlier = jnp.dot(onehot.astype(bf16), before.astype(bf16), preferred_element_type=f32)
    slot = jnp.sum(earlier * onehot, 0, keepdims=True)
    passage = lax.broadcasted_iota(jnp.int32, (blocks, rows), 1)
    block = lax.broadcasted_iota(jnp.int32, (blocks, rows), 0)
    widen = (passage // 2 == block).astype(bf16)
    both = jnp.concatenate(
        (jnp.broadcast_to(owner.astype(f32), (8, blocks)), jnp.broadcast_to(slot, (8, blocks))), 0
    )
    both = jnp.dot(both.astype(bf16), widen, preferred_element_type=f32)
    parity = lax.broadcasted_iota(jnp.int32, (1, rows), 1) & 1
    target = both[0:1] * ROWS + (both[8:9] * 2.0 + parity.astype(f32)) * chunks

    row = lax.broadcasted_iota(jnp.int32, (total, rows), 0).astype(f32)
    placed = jnp.zeros((total, LANES), f32)
    taken = jnp.zeros((total, rows), f32)
    for j in range(chunks):
        onto = (row == target + float(j)).astype(f32)
        taken = taken + onto
        placed = placed + jnp.dot(
            onto.astype(bf16), fresh[:, j * LANES : (j + 1) * LANES], preferred_element_type=f32
        )
    filled = jnp.dot(taken.astype(bf16), jnp.ones((rows, LANES), bf16), preferred_element_type=f32)
    rest = jnp.broadcast_to(query_ref[...].astype(f32)[None], (shards, ROWS, LANES))
    out_ref[...] = jnp.where(filled > 0.5, placed, rest.reshape(total, LANES)).astype(bf16)


def place(cls_states, own, across, along, diagonal, owner, query, shards):
    return pl.pallas_call(
        place_kernel,
        out_shape=jax.ShapeDtypeStruct((shards * ROWS, LANES), bf16),
        compiler_params=params(),
        name="place",
    )(cls_states, own, across, along, diagonal, owner, query)


def score_kernel(
    recv_ref, stale_ref, idsg_ref, refreshed_ref, again_ref, packed_ref, recv_s, arrived_s
):
    cache_rows, width = stale_ref.shape
    shards = recv_ref.shape[0] // ROWS
    chunks = width // LANES
    per_shard = cache_rows // shards
    recv_s[...] = recv_ref[...].astype(f32)
    queries = []
    for j in range(chunks):
        for c in range(per_shard):
            arrived_s[j, pl.ds(c, shards, stride=per_shard), :] = recv_s[
                pl.ds(c * chunks + j, shards, stride=ROWS), :
            ]
        queries.append(recv_s[pl.ds(per_shard * chunks + j, shards, stride=ROWS), :])
    queries = jnp.concatenate(queries, 1).astype(bf16)
    arrived = jnp.concatenate([arrived_s[j] for j in range(chunks)], 1)
    refreshed = jnp.where(arrived > 0.5 * EMPTY, stale_ref[...].astype(f32), arrived).astype(bf16)
    refreshed_ref[...] = refreshed
    again_ref[...] = refreshed
    scores = contract_last(queries, refreshed)
    ids = idsg_ref[...]
    lane = lax.broadcasted_iota(jnp.int32, ids.shape, 1)
    low = ids & (LANES - 1)
    picked = jnp.zeros(ids.shape, f32)
    for part in range(cache_rows // LANES):
        here = jnp.take_along_axis(scores[:, part * LANES : (part + 1) * LANES], low, axis=1)
        picked = jnp.where(ids // LANES == part, here, picked)
    packed_ref[...] = jnp.where(lane < LANES // 2, picked, ids.astype(f32))


def score(recv, stale, idsg):
    return pl.pallas_call(
        score_kernel,
        out_shape=(
            jax.ShapeDtypeStruct(stale.shape, bf16),
            jax.ShapeDtypeStruct(stale.shape, bf16),
            jax.ShapeDtypeStruct(idsg.shape, f32),
        ),
        scratch_shapes=[
            pltpu.VMEM(recv.shape, f32),
            pltpu.VMEM((stale.shape[1] // LANES, stale.shape[0], LANES), f32),
        ],
        compiler_params=params(),
        name="score",
    )(recv, stale, idsg)


HALF = LANES // 2


def pair_kernel(
    x_ref, discount_ref, grad_ref, loss_ref, half_s, wide_w, columns, across, spread_s, rows_s, near_q, far_q
):
    x = x_ref[...]
    n_blocks = x.shape[0] // 2
    count = n_blocks * LANES
    top, low = x[:n_blocks], x[n_blocks:]
    lane = lax.broadcasted_iota(jnp.int32, (n_blocks, LANES), 1)
    left = lane < HALF
    scores = jnp.where(left, top, pltpu.roll(low, HALF, 1))
    gains = jnp.exp2(jnp.where(left, pltpu.roll(top, HALF, 1), low))
    position = lax.broadcasted_iota(jnp.int32, (n_blocks, LANES), 0) * LANES + lane

    ordered = jnp.ones((n_blocks, LANES), f32)
    for level in range(1, 5):
        above = jnp.sum((gains > float(2**level) - 0.5).astype(f32))
        ordered = jnp.where(position.astype(f32) < above, float(2**level), ordered)
    ideal = jnp.sum(ordered * discount_ref[...])

    span = n_blocks // 2
    groups = LANES // 8

    def sweep(values, load_or_make):
        columns[...] = jnp.zeros_like(columns)
        values[n_blocks:] = values[:n_blocks]

        def spread(i):
            spread_s[i] = jnp.broadcast_to(values[pl.ds(i, 1), :], (LANES, LANES)).T

        def collect(i):
            across[pl.ds(i, 1), :] = jnp.sum(rows_s[i].T, 0, keepdims=True)

        def block(i, last):
            first = [spread_s[i, pl.ds(8 * g, 8), :] for g in range(groups)]
            collect(i)
            spread(i + 1)
            acc = [jnp.zeros((8, LANES), f32) for _ in range(groups)]
            for d in range(last + 1):
                k = i + d
                kept = near_q.at[i, d] if d < span else far_q.at[i]
                v_k = jnp.broadcast_to(values[pl.ds(k, 1), :], (8, LANES))
                column = [jnp.zeros((8, LANES), f32) for _ in range(4)]
                for g in range(groups):
                    value = load_or_make(first[g], v_k, kept, 8 * g)
                    acc[g] = acc[g] + value
                    column[g % 4] = column[g % 4] + value
                if d > 0:
                    columns[k] = columns[k] + ((column[0] + column[1]) + (column[2] + column[3]))
            for g in range(groups):
                rows_s[i + 1, pl.ds(8 * g, 8), :] = acc[g]
            return 0

        rows_s[0] = jnp.zeros((LANES, LANES), f32)
        spread(0)
        lax.fori_loop(0, span, lambda i, _: block(i, span), 0)
        lax.fori_loop(span, n_blocks, lambda i, _: block(i, span - 1), 0)
        collect(n_blocks)
        folded = jnp.sum(columns[...], 1)
        wrapped = jnp.concatenate((folded[n_blocks:], jnp.zeros((span, LANES), f32)), 0)
        return across[1:] - folded[:n_blocks] - wrapped

    def rank_term(s_i, s_k, kept, at):
        t = jnp.tanh(s_k - s_i)
        kept[pl.ds(at, 8), :] = 1.0 - t * t
        return t

    def cross_term(w_i, w_k, kept, at):
        return (w_k - w_i) * kept[pl.ds(at, 8), :]

    half_s[:n_blocks] = 0.5 * scores
    rank = 0.5 + 0.5 * count + 0.5 * sweep(half_s, rank_term)
    logged = jnp.log2(1.0 + rank)
    weight = gains / (ideal * LOG_TWO * (1.0 + rank) * logged * logged)
    loss_ref[...] = jnp.full((1, LANES), 1.0 - jnp.sum(gains / logged) / ideal, f32)
    wide_w[:n_blocks] = 0.25 * weight
    grad = sweep(wide_w, cross_term).astype(bf16).astype(f32)
    grad_ref[:n_blocks] = grad
    grad_ref[n_blocks:] = pltpu.roll(grad, HALF, 1)


def pair(x, discount):
    n_blocks = x.shape[0] // 2
    span = n_blocks // 2
    return pl.pallas_call(
        pair_kernel,
        out_shape=(
            jax.ShapeDtypeStruct(x.shape, f32),
            jax.ShapeDtypeStruct((1, LANES), f32),
        ),
        scratch_shapes=[
            pltpu.VMEM((2 * n_blocks, LANES), f32),
            pltpu.VMEM((2 * n_blocks, LANES), f32),
            pltpu.VMEM((n_blocks + span, 8, LANES), f32),
            pltpu.VMEM((n_blocks + 1, LANES), f32),
            pltpu.VMEM((n_blocks + 1, LANES, LANES), f32),
            pltpu.VMEM((n_blocks + 1, LANES, LANES), f32),
            pltpu.VMEM((n_blocks, span, LANES, LANES), f32),
            pltpu.VMEM((span, LANES, LANES), f32),
        ],
        compiler_params=params(),
        name="pair",
    )(x, discount)


def share_kernel(grad_ref, idsg_ref, refreshed_ref, out_ref, rows_w):
    lists, cache_rows = rows_w.shape
    for g in range(lists // 8):
        part = slice(8 * g, 8 * g + 8)
        grads = grad_ref[part, :]
        ids = idsg_ref[part, :]
        spots = [
            lax.broadcasted_iota(jnp.int32, (8, LANES), 1) + LANES * p
            for p in range(cache_rows // LANES)
        ]
        acc = [jnp.zeros((8, LANES), f32) for _ in spots]
        for j in range(HALF):
            id_j = jnp.broadcast_to(ids[:, j : j + 1], (8, LANES))
            grad_j = jnp.broadcast_to(grads[:, j : j + 1], (8, LANES))
            acc = [a + jnp.where(id_j == spot, grad_j, 0.0) for a, spot in zip(acc, spots)]
        for p, a in enumerate(acc):
            rows_w[part, p * LANES : (p + 1) * LANES] = a
    weights = rows_w[...]
    high = weights.astype(bf16)
    rest = (weights - high.astype(f32)).astype(bf16)
    refreshed = refreshed_ref[...]
    out_ref[...] = jnp.dot(high, refreshed, preferred_element_type=f32) + jnp.dot(
        rest, refreshed, preferred_element_type=f32
    )


def share(grads, idsg, refreshed):
    return pl.pallas_call(
        share_kernel,
        out_shape=jax.ShapeDtypeStruct((grads.shape[0], refreshed.shape[1]), f32),
        scratch_shapes=[pltpu.VMEM((grads.shape[0], refreshed.shape[0]), f32)],
        compiler_params=params(),
        name="share",
    )(grads, idsg, refreshed)


Y, ZZ, ZL, X = 4, 4, 2, 2


def shard_at(y, zz, zl, x):
    return ((y * ZZ + zz) * ZL + zl) * X + x


def everywhere():
    return [
        (y, zz, zl, x) for y in range(Y) for zz in range(ZZ) for zl in range(ZL) for x in range(X)
    ]


def gather_units(block):
    groups = [
        [shard_at(y, zz, zl, x) for y in range(Y) for x in range(X)]
        for zz in range(ZZ)
        for zl in range(ZL)
    ]
    parts = len(groups[0])
    units, width = block.shape
    gathered = lax.all_to_all(
        jnp.broadcast_to(block[None], (parts, units, width)),
        "shard",
        split_axis=0,
        concat_axis=0,
        tiled=True,
        axis_index_groups=groups,
    )
    return gathered.reshape(parts * units, width)


def per_device(
    cls_states, trainer_in, trainer_out, stale_cache, block_owner, queries, neg_ids, grades
):
    shards = lax.axis_size("shard")
    roles = lax.axis_size("role")
    width = cls_states.shape[1]
    barrier = lax.optimization_barrier

    def to_core(v):
        return lax.ppermute(v, "role", [(0, 1), (1, 0), (2, 3), (3, 2)])

    def to_across(v):
        return lax.ppermute(v, "role", [(0, 2), (1, 3), (2, 0), (3, 1)])

    def to_along(v):
        return lax.ppermute(
            v,
            "shard",
            [
                (shard_at(y, zz, zl, x), shard_at(y, zz, 1 - zl, x))
                for y, zz, zl, x in everywhere()
            ],
        )

    def to_diagonal(v):
        return lax.ppermute(
            v,
            ("role", "shard"),
            [
                (r * shards + shard_at(y, zz, zl, x), (r ^ 2) * shards + shard_at(y, zz, 1 - zl, x))
                for r in range(roles)
                for y, zz, zl, x in everywhere()
            ],
        )

    axes = ("role", "shard")
    mine = jnp.concatenate((trainer_in[0], trainer_out[0]), 1)
    mine = lax.ppermute(
        mine,
        axes,
        [
            ((roles - 1) * shards + shard_at(y, zz, zl, x), zz * shards + shard_at(y, zz, zl, x))
            for y, zz, zl, x in everywhere()
        ],
    )
    mine, cls_after = barrier((mine, cls_states))
    block = mine
    for by in range(1, ZZ):
        turn = [
            (zz * shards + shard_at(y, zz, zl, x), zz * shards + shard_at(y, (zz + by) % ZZ, zl, x))
            for y, zz, zl, x in everywhere()
        ]
        block = block + lax.ppermute(mine, axes, turn)
    x_across = to_across(cls_after)
    block, x_across, cls_after = barrier((block, x_across, cls_after))
    units = gather_units(block)
    xs = (cls_states, x_across, to_along(cls_after), to_along(x_across))
    units, xs = barrier((units, xs))
    other_units = to_core(units)
    so_far = first_half(xs, units)
    (diagonal,) = second_half(xs, other_units, so_far, (3,), bf16)
    from_diagonal = to_diagonal(diagonal)
    other_units, diagonal = barrier((other_units, diagonal))
    across, along = second_half(xs, other_units, so_far, (1, 2), bf16)
    from_across = to_across(across)
    from_along = to_along(along)
    (own,) = second_half(xs, other_units, so_far, (0,), f32)
    chunks = width // LANES
    rest = jnp.concatenate(
        (
            jnp.full((2 * CAP * chunks, LANES), EMPTY, bf16),
            queries.reshape(chunks, LANES),
            jnp.full((ROWS - (2 * CAP + 1) * chunks, LANES), EMPTY, bf16),
        ),
        0,
    )
    idsg = jnp.concatenate((neg_ids, grades), 1)
    outgoing = place(
        cls_states,
        own,
        from_across,
        from_along,
        from_diagonal,
        block_owner.reshape(1, -1),
        rest,
        shards,
    )
    outgoing, idsg = lax.optimization_barrier((outgoing, idsg))
    arrived = lax.all_to_all(
        outgoing.reshape(shards, ROWS, LANES), "shard", split_axis=0, concat_axis=0, tiled=True
    )
    refreshed, again, packed = score(arrived.reshape(-1, LANES), stale_cache, idsg)
    packed = lax.all_to_all(packed, "shard", split_axis=0, concat_axis=0, tiled=True)
    count = shards * neg_ids.shape[1]
    position = np.arange(1, count + 1, dtype=np.float64)
    discount = (1.0 / np.log2(1.0 + position)).astype(np.float32).reshape(-1, LANES)
    grads, loss = pair(packed, jnp.asarray(discount))
    grads = lax.all_to_all(grads, "shard", split_axis=0, concat_axis=0, tiled=True)
    shares = share(grads, idsg, again)
    shares = lax.all_to_all(shares, "shard", split_axis=0, concat_axis=0, tiled=True)
    return refreshed, jnp.sum(shares, 0, keepdims=True), loss[0, :1]


def solution(mesh):
    return jax.shard_map(
        per_device,
        mesh=mesh,
        in_specs=(
            P(("role", "shard"), None),
            P("role", "shard", None),
            P("role", "shard", None),
            P(("role", "shard"), None),
            P(("role", "shard"), None),
            P(("role", "shard"), None),
            P("role", "shard"),
            P("role", "shard"),
        ),
        out_specs=(P(("role", "shard"), None), P(("role", "shard"), None), P(("role", "shard"))),
        check_vma=False,
    )
```

```python
import functools
import math

import jax
import jax.numpy as jnp
import numpy as np
from jax import lax
from jax.experimental import pallas as pl
from jax.experimental.pallas import tpu as pltpu
from jax.sharding import PartitionSpec as P

CAP = 2
EPSILON = 1e-05
LOG_TWO = math.log(2.0)
EMPTY = 1024.0

f32 = jnp.float32
bf16 = jnp.bfloat16
LANES = 128


def params():
    return pltpu.CompilerParams(vmem_limit_bytes=48 * 1024 * 1024)


def contract_last(a, b):
    return lax.dot_general(a, b, (((1,), (1,)), ((), ())), preferred_element_type=f32)


def partial_sums(x, w_ref):
    width = x.shape[1]
    inner = contract_last(x, w_ref[:, :width])
    hidden = 0.5 * inner * (1.0 + lax.erf(inner * math.sqrt(0.5)))
    return jnp.dot(hidden.astype(bf16), w_ref[:, width:], preferred_element_type=f32)


def first_kernel(own_ref, across_ref, along_ref, diagonal_ref, w_ref, out_ref):
    for n, x_ref in enumerate((own_ref, across_ref, along_ref, diagonal_ref)):
        out_ref[n] = partial_sums(x_ref[...], w_ref)


def first_half(xs, units):
    return pl.pallas_call(
        first_kernel,
        out_shape=jax.ShapeDtypeStruct((len(xs),) + xs[0].shape, f32),
        compiler_params=params(),
        name="encode",
    )(*xs, units)


def second_kernel(at, *refs):
    x_refs, (w_ref, so_far_ref), out_refs = refs[: len(at)], refs[len(at) :][:2], refs[-len(at) :]
    for n, x_ref, out_ref in zip(at, x_refs, out_refs):
        part = so_far_ref[n] + partial_sums(x_ref[...], w_ref)
        out_ref[...] = part.astype(out_ref.dtype)


def second_half(xs, units, so_far, at, dtype):
    return pl.pallas_call(
        functools.partial(second_kernel, at),
        out_shape=tuple(jax.ShapeDtypeStruct(xs[n].shape, dtype) for n in at),
        compiler_params=params(),
        name="encode_rest",
    )(*(xs[n] for n in at), units, so_far)


ROWS, SUB = 32, 8


def place_kernel(
    cls_ref, own_ref, across_ref, along_ref, diagonal_ref, owner_ref, query_ref, out_ref
):
    rows, width = cls_ref.shape
    blocks = owner_ref.shape[1]
    shards = out_ref.shape[0] // SUB
    chunks = width // LANES
    resid = cls_ref[...].astype(f32) + own_ref[...]
    for part_ref in (across_ref, along_ref, diagonal_ref):
        resid = resid + part_ref[...].astype(f32)
    centred = resid - jnp.mean(resid, -1, keepdims=True)
    variance = jnp.mean(centred * centred, -1, keepdims=True)
    fresh = (centred * lax.rsqrt(variance + EPSILON)).astype(bf16)

    owner = owner_ref[...]
    shard_of = lax.broadcasted_iota(jnp.int32, (shards, blocks), 0)
    onehot = (shard_of == owner).astype(f32)
    before = lax.broadcasted_iota(jnp.int32, (blocks, blocks), 0) < lax.broadcasted_iota(
        jnp.int32, (blocks, blocks), 1
    )
    earlier = jnp.dot(onehot.astype(bf16), before.astype(bf16), preferred_element_type=f32)
    slot = jnp.sum(earlier * onehot, 0, keepdims=True)
    passage = lax.broadcasted_iota(jnp.int32, (blocks, rows), 1)
    block = lax.broadcasted_iota(jnp.int32, (blocks, rows), 0)
    widen = (passage // 2 == block).astype(bf16)
    both = jnp.concatenate(
        (jnp.broadcast_to(owner.astype(f32), (8, blocks)), jnp.broadcast_to(slot, (8, blocks))), 0
    )
    both = jnp.dot(both.astype(bf16), widen, preferred_element_type=f32)
    parity = lax.broadcasted_iota(jnp.int32, (1, rows), 1) & 1
    target = both[0:1] * (2.0 * CAP * chunks) + (both[8:9] * 2.0 + parity.astype(f32)) * chunks

    passage_rows = 2 * CAP * chunks
    row = lax.broadcasted_iota(jnp.int32, (shards * passage_rows, rows), 0).astype(f32)
    placed = jnp.zeros((shards * passage_rows, LANES), f32)
    taken = jnp.zeros((shards * passage_rows, rows), f32)
    for j in range(chunks):
        onto = (row == target + float(j)).astype(f32)
        taken = taken + onto
        placed = placed + jnp.dot(
            onto.astype(bf16), fresh[:, j * LANES : (j + 1) * LANES], preferred_element_type=f32
        )
    filled = jnp.dot(taken.astype(bf16), jnp.ones((rows, LANES), bf16), preferred_element_type=f32)
    placed = jnp.where(filled > 0.5, placed, EMPTY).reshape(shards, passage_rows, LANES)
    for tile in range(ROWS // SUB):
        if tile < passage_rows // SUB:
            part = placed[:, tile * SUB : (tile + 1) * SUB]
        else:
            part = jnp.broadcast_to(query_ref[...].astype(f32)[None], (shards, SUB, LANES))
        part = part.reshape(shards * SUB, LANES).astype(bf16)
        out_ref[:, tile * LANES : (tile + 1) * LANES] = part


def place(cls_states, own, across, along, diagonal, owner, query, shards):
    return pl.pallas_call(
        place_kernel,
        out_shape=jax.ShapeDtypeStruct((shards * SUB, ROWS // SUB * LANES), bf16),
        compiler_params=params(),
        name="place",
    )(cls_states, own, across, along, diagonal, owner, query)


def score_kernel(
    recv_ref, stale_ref, idsg_ref, refreshed_ref, again_ref, packed_ref, recv_s, arrived_s
):
    cache_rows, width = stale_ref.shape
    shards = recv_ref.shape[0] // SUB
    chunks = width // LANES
    per_shard = cache_rows // shards
    for tile in range(ROWS // SUB):
        recv_s[tile] = recv_ref[:, tile * LANES : (tile + 1) * LANES].astype(f32)

    def arrived_row(r):
        return recv_s[r // SUB, pl.ds(r % SUB, shards, stride=SUB), :]

    queries = []
    for j in range(chunks):
        for c in range(per_shard):
            arrived_s[j, pl.ds(c, shards, stride=per_shard), :] = arrived_row(c * chunks + j)
        queries.append(arrived_row(per_shard * chunks + j))
    queries = jnp.concatenate(queries, 1).astype(bf16)
    arrived = jnp.concatenate([arrived_s[j] for j in range(chunks)], 1)
    refreshed = jnp.where(arrived > 0.5 * EMPTY, stale_ref[...].astype(f32), arrived).astype(bf16)
    refreshed_ref[...] = refreshed
    again_ref[...] = refreshed
    scores = contract_last(queries, refreshed)
    ids = idsg_ref[...]
    lane = lax.broadcasted_iota(jnp.int32, ids.shape, 1)
    low = ids & (LANES - 1)
    picked = jnp.zeros(ids.shape, f32)
    for part in range(cache_rows // LANES):
        here = jnp.take_along_axis(scores[:, part * LANES : (part + 1) * LANES], low, axis=1)
        picked = jnp.where(ids // LANES == part, here, picked)
    packed_ref[...] = jnp.where(lane < LANES // 2, picked, ids.astype(f32))


def score(recv, stale, idsg):
    return pl.pallas_call(
        score_kernel,
        out_shape=(
            jax.ShapeDtypeStruct(stale.shape, bf16),
            jax.ShapeDtypeStruct(stale.shape, bf16),
            jax.ShapeDtypeStruct(idsg.shape, f32),
        ),
        scratch_shapes=[
            pltpu.VMEM((ROWS // SUB, recv.shape[0], LANES), f32),
            pltpu.VMEM((stale.shape[1] // LANES, stale.shape[0], LANES), f32),
        ],
        compiler_params=params(),
        name="score",
    )(recv, stale, idsg)


HALF = LANES // 2


def pair_kernel(
    x_ref, discount_ref, grad_ref, loss_ref, half_s, wide_w, columns, across, spread_s, rows_s, near_q, far_q
):
    x = x_ref[...]
    n_blocks = x.shape[0] // 2
    count = n_blocks * LANES
    top, low = x[:n_blocks], x[n_blocks:]
    lane = lax.broadcasted_iota(jnp.int32, (n_blocks, LANES), 1)
    left = lane < HALF
    scores = jnp.where(left, top, pltpu.roll(low, HALF, 1))
    gains = jnp.exp2(jnp.where(left, pltpu.roll(top, HALF, 1), low))
    position = lax.broadcasted_iota(jnp.int32, (n_blocks, LANES), 0) * LANES + lane

    ordered = jnp.ones((n_blocks, LANES), f32)
    for level in range(1, 5):
        above = jnp.sum((gains > float(2**level) - 0.5).astype(f32))
        ordered = jnp.where(position.astype(f32) < above, float(2**level), ordered)
    ideal = jnp.sum(ordered * discount_ref[...])

    span = n_blocks // 2
    groups = LANES // 8

    def sweep(values, load_or_make):
        columns[...] = jnp.zeros_like(columns)
        values[n_blocks:] = values[:n_blocks]

        def spread(i):
            spread_s[i] = jnp.broadcast_to(values[pl.ds(i, 1), :], (LANES, LANES)).T

        def collect(i):
            across[pl.ds(i, 1), :] = jnp.sum(rows_s[i].T, 0, keepdims=True)

        def block(i, last):
            first = [spread_s[i, pl.ds(8 * g, 8), :] for g in range(groups)]
            collect(i)
            spread(i + 1)
            acc = [jnp.zeros((8, LANES), f32) for _ in range(groups)]
            for d in range(last + 1):
                k = i + d
                kept = near_q.at[i, d] if d < span else far_q.at[i]
                v_k = jnp.broadcast_to(values[pl.ds(k, 1), :], (8, LANES))
                column = [jnp.zeros((8, LANES), f32) for _ in range(4)]
                for g in range(groups):
                    value = load_or_make(first[g], v_k, kept, 8 * g)
                    acc[g] = acc[g] + value
                    column[g % 4] = column[g % 4] + value
                if d > 0:
                    columns[k] = columns[k] + ((column[0] + column[1]) + (column[2] + column[3]))
            for g in range(groups):
                rows_s[i + 1, pl.ds(8 * g, 8), :] = acc[g]
            return 0

        rows_s[0] = jnp.zeros((LANES, LANES), f32)
        spread(0)
        lax.fori_loop(0, span, lambda i, _: block(i, span), 0)
        lax.fori_loop(span, n_blocks, lambda i, _: block(i, span - 1), 0)
        collect(n_blocks)
        folded = jnp.sum(columns[...], 1)
        wrapped = jnp.concatenate((folded[n_blocks:], jnp.zeros((span, LANES), f32)), 0)
        return across[1:] - folded[:n_blocks] - wrapped

    def rank_term(s_i, s_k, kept, at):
        t = jnp.tanh(s_k - s_i)
        kept[pl.ds(at, 8), :] = 1.0 - t * t
        return t

    def cross_term(w_i, w_k, kept, at):
        return (w_k - w_i) * kept[pl.ds(at, 8), :]

    half_s[:n_blocks] = 0.5 * scores
    rank = 0.5 + 0.5 * count + 0.5 * sweep(half_s, rank_term)
    logged = jnp.log2(1.0 + rank)
    weight = gains / (ideal * LOG_TWO * (1.0 + rank) * logged * logged)
    loss_ref[...] = jnp.full((1, LANES), 1.0 - jnp.sum(gains / logged) / ideal, f32)
    wide_w[:n_blocks] = 0.25 * weight
    grad = sweep(wide_w, cross_term).astype(bf16).astype(f32)
    grad_ref[:n_blocks] = grad
    grad_ref[n_blocks:] = pltpu.roll(grad, HALF, 1)


def pair(x, discount):
    n_blocks = x.shape[0] // 2
    span = n_blocks // 2
    return pl.pallas_call(
        pair_kernel,
        out_shape=(
            jax.ShapeDtypeStruct(x.shape, f32),
            jax.ShapeDtypeStruct((1, LANES), f32),
        ),
        scratch_shapes=[
            pltpu.VMEM((2 * n_blocks, LANES), f32),
            pltpu.VMEM((2 * n_blocks, LANES), f32),
            pltpu.VMEM((n_blocks + span, 8, LANES), f32),
            pltpu.VMEM((n_blocks + 1, LANES), f32),
            pltpu.VMEM((n_blocks + 1, LANES, LANES), f32),
            pltpu.VMEM((n_blocks + 1, LANES, LANES), f32),
            pltpu.VMEM((n_blocks, span, LANES, LANES), f32),
            pltpu.VMEM((span, LANES, LANES), f32),
        ],
        compiler_params=params(),
        name="pair",
    )(x, discount)


def share_kernel(grad_ref, idsg_ref, refreshed_ref, out_ref, rows_w):
    lists, cache_rows = rows_w.shape
    for g in range(lists // 8):
        part = slice(8 * g, 8 * g + 8)
        grads = grad_ref[part, :]
        ids = idsg_ref[part, :]
        spots = [
            lax.broadcasted_iota(jnp.int32, (8, LANES), 1) + LANES * p
            for p in range(cache_rows // LANES)
        ]
        acc = [jnp.zeros((8, LANES), f32) for _ in spots]
        for j in range(HALF):
            id_j = jnp.broadcast_to(ids[:, j : j + 1], (8, LANES))
            grad_j = jnp.broadcast_to(grads[:, j : j + 1], (8, LANES))
            acc = [a + jnp.where(id_j == spot, grad_j, 0.0) for a, spot in zip(acc, spots)]
        for p, a in enumerate(acc):
            rows_w[part, p * LANES : (p + 1) * LANES] = a
    weights = rows_w[...]
    high = weights.astype(bf16)
    rest = (weights - high.astype(f32)).astype(bf16)
    refreshed = refreshed_ref[...]
    out_ref[...] = jnp.dot(high, refreshed, preferred_element_type=f32) + jnp.dot(
        rest, refreshed, preferred_element_type=f32
    )


def share(grads, idsg, refreshed):
    return pl.pallas_call(
        share_kernel,
        out_shape=jax.ShapeDtypeStruct((grads.shape[0], refreshed.shape[1]), f32),
        scratch_shapes=[pltpu.VMEM((grads.shape[0], refreshed.shape[0]), f32)],
        compiler_params=params(),
        name="share",
    )(grads, idsg, refreshed)


Y, ZZ, ZL, X = 4, 4, 2, 2


def shard_at(y, zz, zl, x):
    return ((y * ZZ + zz) * ZL + zl) * X + x


def everywhere():
    return [
        (y, zz, zl, x) for y in range(Y) for zz in range(ZZ) for zl in range(ZL) for x in range(X)
    ]


def gather_units(block):
    groups = [
        [shard_at(y, zz, zl, x) for y in range(Y) for x in range(X)]
        for zz in range(ZZ)
        for zl in range(ZL)
    ]
    parts = len(groups[0])
    units, width = block.shape
    gathered = lax.all_to_all(
        jnp.broadcast_to(block[None], (parts, units, width)),
        "shard",
        split_axis=0,
        concat_axis=0,
        tiled=True,
        axis_index_groups=groups,
    )
    return gathered.reshape(parts * units, width)


def per_device(
    cls_states, trainer_in, trainer_out, stale_cache, block_owner, queries, neg_ids, grades
):
    shards = lax.axis_size("shard")
    roles = lax.axis_size("role")
    width = cls_states.shape[1]
    barrier = lax.optimization_barrier

    def to_core(v):
        return lax.ppermute(v, "role", [(0, 1), (1, 0), (2, 3), (3, 2)])

    def to_across(v):
        return lax.ppermute(v, "role", [(0, 2), (1, 3), (2, 0), (3, 1)])

    def to_along(v):
        return lax.ppermute(
            v,
            "shard",
            [
                (shard_at(y, zz, zl, x), shard_at(y, zz, 1 - zl, x))
                for y, zz, zl, x in everywhere()
            ],
        )

    def to_diagonal(v):
        return lax.ppermute(
            v,
            ("role", "shard"),
            [
                (r * shards + shard_at(y, zz, zl, x), (r ^ 2) * shards + shard_at(y, zz, 1 - zl, x))
                for r in range(roles)
                for y, zz, zl, x in everywhere()
            ],
        )

    role_of = (0, 2, 1, 3)
    axes = ("role", "shard")
    mine = jnp.concatenate((trainer_in[0], trainer_out[0]), 1)
    mine = lax.ppermute(
        mine,
        axes,
        [
            (
                (roles - 1) * shards + shard_at(y, zz, zl, x),
                role_of[zz] * shards + shard_at(y, zz, zl, x),
            )
            for y, zz, zl, x in everywhere()
        ],
    )
    mine, cls_after = barrier((mine, cls_states))
    block = mine
    for by in range(1, ZZ):
        turn = [
            (
                role_of[zz] * shards + shard_at(y, zz, zl, x),
                role_of[zz] * shards + shard_at(y, (zz + by) % ZZ, zl, x),
            )
            for y, zz, zl, x in everywhere()
        ]
        block = block + lax.ppermute(mine, axes, turn)
    x_across = to_across(cls_after)
    block, x_across, cls_after = barrier((block, x_across, cls_after))
    units = gather_units(block)
    xs = (cls_states, x_across, to_along(cls_after), to_along(x_across))
    units, xs = barrier((units, xs))
    other_units = to_core(units)
    so_far = first_half(xs, units)
    (diagonal,) = second_half(xs, other_units, so_far, (3,), bf16)
    from_diagonal = to_diagonal(diagonal)
    other_units, diagonal = barrier((other_units, diagonal))
    across, along = second_half(xs, other_units, so_far, (1, 2), bf16)
    from_across = to_across(across)
    from_along = to_along(along)
    (own,) = second_half(xs, other_units, so_far, (0,), f32)
    query = jnp.pad(queries.reshape(-1, LANES), ((0, SUB - width // LANES), (0, 0)))
    idsg = jnp.concatenate((neg_ids, grades), 1)
    outgoing = place(
        cls_states,
        own,
        from_across,
        from_along,
        from_diagonal,
        block_owner.reshape(1, -1),
        query,
        shards,
    )
    outgoing, idsg = barrier((outgoing, idsg))
    arrived = lax.all_to_all(
        outgoing.reshape(shards, SUB, -1), "shard", split_axis=0, concat_axis=0, tiled=True
    )
    refreshed, again, packed = score(arrived.reshape(shards * SUB, -1), stale_cache, idsg)
    packed = lax.all_to_all(packed, "shard", split_axis=0, concat_axis=0, tiled=True)
    count = shards * neg_ids.shape[1]
    position = np.arange(1, count + 1, dtype=np.float64)
    discount = (1.0 / np.log2(1.0 + position)).astype(np.float32).reshape(-1, LANES)
    grads, loss = pair(packed, jnp.asarray(discount))
    grads = lax.all_to_all(grads, "shard", split_axis=0, concat_axis=0, tiled=True)
    shares = share(grads, idsg, again)
    shares = lax.all_to_all(shares, "shard", split_axis=0, concat_axis=0, tiled=True)
    return refreshed, jnp.sum(shares, 0, keepdims=True), loss[0, :1]


def solution(mesh):
    return jax.shard_map(
        per_device,
        mesh=mesh,
        in_specs=(
            P(("role", "shard"), None),
            P("role", "shard", None),
            P("role", "shard", None),
            P(("role", "shard"), None),
            P(("role", "shard"), None),
            P(("role", "shard"), None),
            P("role", "shard"),
            P("role", "shard"),
        ),
        out_specs=(P(("role", "shard"), None), P(("role", "shard"), None), P(("role", "shard"))),
        check_vma=False,
    )
```

```python
import functools
import math

import jax
import jax.numpy as jnp
import numpy as np
from jax import lax
from jax.experimental import pallas as pl
from jax.experimental.pallas import tpu as pltpu
from jax.sharding import PartitionSpec as P

CAP = 2
EPSILON = 1e-05
LOG_TWO = math.log(2.0)
EMPTY = 1024.0

f32 = jnp.float32
bf16 = jnp.bfloat16
LANES = 128


def params(mebibytes=16):
    return pltpu.CompilerParams(vmem_limit_bytes=mebibytes * 1024 * 1024)


def contract_last(a, b):
    return lax.dot_general(a, b, (((1,), (1,)), ((), ())), preferred_element_type=f32)


def partial_sums(x, w_ref):
    width = x.shape[1]
    inner = contract_last(x, w_ref[:, :width])
    hidden = 0.5 * inner * (1.0 + lax.erf(inner * math.sqrt(0.5)))
    return jnp.dot(hidden.astype(bf16), w_ref[:, width:], preferred_element_type=f32)


def first_kernel(own_ref, across_ref, along_ref, diagonal_ref, w_ref, out_ref):
    for n, x_ref in enumerate((own_ref, across_ref, along_ref, diagonal_ref)):
        out_ref[n] = partial_sums(x_ref[...], w_ref)


def first_half(xs, units):
    return pl.pallas_call(
        first_kernel,
        out_shape=jax.ShapeDtypeStruct((len(xs),) + xs[0].shape, f32),
        compiler_params=params(),
        name="encode",
    )(*xs, units)


def second_kernel(at, *refs):
    x_refs, (w_ref, so_far_ref), out_refs = refs[: len(at)], refs[len(at) :][:2], refs[-len(at) :]
    for n, x_ref, out_ref in zip(at, x_refs, out_refs):
        part = so_far_ref[n] + partial_sums(x_ref[...], w_ref)
        out_ref[...] = part.astype(out_ref.dtype)


def second_half(xs, units, so_far, at, dtype):
    return pl.pallas_call(
        functools.partial(second_kernel, at),
        out_shape=tuple(jax.ShapeDtypeStruct(xs[n].shape, dtype) for n in at),
        compiler_params=params(),
        name="encode_rest",
    )(*(xs[n] for n in at), units, so_far)


ROWS, SUB = 32, 8


def place_kernel(
    cls_ref, own_ref, across_ref, along_ref, diagonal_ref, owner_ref, query_ref, out_ref
):
    rows, width = cls_ref.shape
    blocks = owner_ref.shape[1]
    shards = out_ref.shape[0] // SUB
    chunks = width // LANES
    resid = cls_ref[...].astype(f32) + own_ref[...]
    for part_ref in (across_ref, along_ref, diagonal_ref):
        resid = resid + part_ref[...].astype(f32)
    centred = resid - jnp.mean(resid, -1, keepdims=True)
    variance = jnp.mean(centred * centred, -1, keepdims=True)
    fresh = (centred * lax.rsqrt(variance + EPSILON)).astype(bf16)

    owner = owner_ref[...]
    shard_of = lax.broadcasted_iota(jnp.int32, (shards, blocks), 0)
    onehot = (shard_of == owner).astype(f32)
    before = lax.broadcasted_iota(jnp.int32, (blocks, blocks), 0) < lax.broadcasted_iota(
        jnp.int32, (blocks, blocks), 1
    )
    earlier = jnp.dot(onehot.astype(bf16), before.astype(bf16), preferred_element_type=f32)
    slot = jnp.sum(earlier * onehot, 0, keepdims=True)
    passage = lax.broadcasted_iota(jnp.int32, (blocks, rows), 1)
    block = lax.broadcasted_iota(jnp.int32, (blocks, rows), 0)
    widen = (passage // 2 == block).astype(bf16)
    both = jnp.concatenate(
        (jnp.broadcast_to(owner.astype(f32), (8, blocks)), jnp.broadcast_to(slot, (8, blocks))), 0
    )
    both = jnp.dot(both.astype(bf16), widen, preferred_element_type=f32)
    parity = lax.broadcasted_iota(jnp.int32, (1, rows), 1) & 1
    target = both[0:1] * (2.0 * CAP * chunks) + (both[8:9] * 2.0 + parity.astype(f32)) * chunks

    passage_rows = 2 * CAP * chunks
    row = lax.broadcasted_iota(jnp.int32, (shards * passage_rows, rows), 0).astype(f32)
    placed = jnp.zeros((shards * passage_rows, LANES), f32)
    taken = jnp.zeros((shards * passage_rows, rows), f32)
    for j in range(chunks):
        onto = (row == target + float(j)).astype(f32)
        taken = taken + onto
        placed = placed + jnp.dot(
            onto.astype(bf16), fresh[:, j * LANES : (j + 1) * LANES], preferred_element_type=f32
        )
    filled = jnp.dot(taken.astype(bf16), jnp.ones((rows, LANES), bf16), preferred_element_type=f32)
    placed = jnp.where(filled > 0.5, placed, EMPTY).reshape(shards, passage_rows, LANES)
    for tile in range(ROWS // SUB):
        if tile < passage_rows // SUB:
            part = placed[:, tile * SUB : (tile + 1) * SUB]
        else:
            part = jnp.broadcast_to(query_ref[...].astype(f32)[None], (shards, SUB, LANES))
        part = part.reshape(shards * SUB, LANES).astype(bf16)
        out_ref[:, tile * LANES : (tile + 1) * LANES] = part


def place(cls_states, own, across, along, diagonal, owner, query, shards):
    return pl.pallas_call(
        place_kernel,
        out_shape=jax.ShapeDtypeStruct((shards * SUB, ROWS // SUB * LANES), bf16),
        compiler_params=params(),
        name="place",
    )(cls_states, own, across, along, diagonal, owner, query)


def score_kernel(
    recv_ref, stale_ref, idsg_ref, refreshed_ref, again_ref, packed_ref, recv_s, arrived_s
):
    cache_rows, width = stale_ref.shape
    shards = recv_ref.shape[0] // SUB
    chunks = width // LANES
    per_shard = cache_rows // shards
    for tile in range(ROWS // SUB):
        recv_s[tile] = recv_ref[:, tile * LANES : (tile + 1) * LANES].astype(f32)

    def arrived_row(r):
        return recv_s[r // SUB, pl.ds(r % SUB, shards, stride=SUB), :]

    queries = []
    for j in range(chunks):
        for c in range(per_shard):
            arrived_s[j, pl.ds(c, shards, stride=per_shard), :] = arrived_row(c * chunks + j)
        queries.append(arrived_row(per_shard * chunks + j))
    queries = jnp.concatenate(queries, 1).astype(bf16)
    arrived = jnp.concatenate([arrived_s[j] for j in range(chunks)], 1)
    refreshed = jnp.where(arrived > 0.5 * EMPTY, stale_ref[...].astype(f32), arrived).astype(bf16)
    refreshed_ref[...] = refreshed
    again_ref[...] = refreshed
    scores = contract_last(queries, refreshed)
    ids = idsg_ref[...]
    lane = lax.broadcasted_iota(jnp.int32, ids.shape, 1)
    low = ids & (LANES - 1)
    picked = jnp.zeros(ids.shape, f32)
    for part in range(cache_rows // LANES):
        here = jnp.take_along_axis(scores[:, part * LANES : (part + 1) * LANES], low, axis=1)
        picked = jnp.where(ids // LANES == part, here, picked)
    packed_ref[...] = jnp.where(lane < LANES // 2, picked, ids.astype(f32))


def score(recv, stale, idsg):
    return pl.pallas_call(
        score_kernel,
        out_shape=(
            jax.ShapeDtypeStruct(stale.shape, bf16),
            jax.ShapeDtypeStruct(stale.shape, bf16),
            jax.ShapeDtypeStruct(idsg.shape, f32),
        ),
        scratch_shapes=[
            pltpu.VMEM((ROWS // SUB, recv.shape[0], LANES), f32),
            pltpu.VMEM((stale.shape[1] // LANES, stale.shape[0], LANES), f32),
        ],
        compiler_params=params(),
        name="score",
    )(recv, stale, idsg)


HALF = LANES // 2


def pair_kernel(
    x_ref, discount_ref, grad_ref, loss_ref, half_s, wide_w, columns, across, spread_s, rows_s, near_q, far_q
):
    x = x_ref[...]
    n_blocks = x.shape[0] // 2
    count = n_blocks * LANES
    top, low = x[:n_blocks], x[n_blocks:]
    lane = lax.broadcasted_iota(jnp.int32, (n_blocks, LANES), 1)
    left = lane < HALF
    scores = jnp.where(left, top, pltpu.roll(low, HALF, 1))
    gains = jnp.exp2(jnp.where(left, pltpu.roll(top, HALF, 1), low))
    position = lax.broadcasted_iota(jnp.int32, (n_blocks, LANES), 0) * LANES + lane

    ordered = jnp.ones((n_blocks, LANES), f32)
    for level in range(1, 5):
        above = jnp.sum((gains > float(2**level) - 0.5).astype(f32))
        ordered = jnp.where(position.astype(f32) < above, float(2**level), ordered)
    ideal = jnp.sum(ordered * discount_ref[...])

    span = n_blocks // 2
    groups = LANES // 8

    def sweep(values, load_or_make):
        columns[...] = jnp.zeros_like(columns)
        values[n_blocks:] = values[:n_blocks]

        def spread(i):
            spread_s[i] = jnp.broadcast_to(values[pl.ds(i, 1), :], (LANES, LANES)).T

        def collect(i):
            across[pl.ds(i, 1), :] = jnp.sum(rows_s[i].T, 0, keepdims=True)

        def block(i, last):
            first = [spread_s[i, pl.ds(8 * g, 8), :] for g in range(groups)]
            collect(i)
            spread(i + 1)
            acc = [jnp.zeros((8, LANES), f32) for _ in range(groups)]
            for d in range(last + 1):
                k = i + d
                kept = near_q.at[i, d] if d < span else far_q.at[i]
                v_k = jnp.broadcast_to(values[pl.ds(k, 1), :], (8, LANES))
                column = [jnp.zeros((8, LANES), f32) for _ in range(4)]
                for g in range(groups):
                    value = load_or_make(first[g], v_k, kept, 8 * g)
                    acc[g] = acc[g] + value
                    column[g % 4] = column[g % 4] + value
                if d > 0:
                    columns[k] = columns[k] + ((column[0] + column[1]) + (column[2] + column[3]))
            for g in range(groups):
                rows_s[i + 1, pl.ds(8 * g, 8), :] = acc[g]
            return 0

        rows_s[0] = jnp.zeros((LANES, LANES), f32)
        spread(0)
        lax.fori_loop(0, span, lambda i, _: block(i, span), 0)
        lax.fori_loop(span, n_blocks, lambda i, _: block(i, span - 1), 0)
        collect(n_blocks)
        folded = jnp.sum(columns[...], 1)
        wrapped = jnp.concatenate((folded[n_blocks:], jnp.zeros((span, LANES), f32)), 0)
        return across[1:] - folded[:n_blocks] - wrapped

    def rank_term(s_i, s_k, kept, at):
        t = jnp.tanh(s_k - s_i)
        kept[pl.ds(at, 8), :] = 1.0 - t * t
        return t

    def cross_term(w_i, w_k, kept, at):
        return (w_k - w_i) * kept[pl.ds(at, 8), :]

    half_s[:n_blocks] = 0.5 * scores
    rank = 0.5 + 0.5 * count + 0.5 * sweep(half_s, rank_term)
    logged = jnp.log2(1.0 + rank)
    weight = gains / (ideal * LOG_TWO * (1.0 + rank) * logged * logged)
    loss_ref[...] = jnp.full((1, LANES), 1.0 - jnp.sum(gains / logged) / ideal, f32)
    wide_w[:n_blocks] = 0.25 * weight
    grad = sweep(wide_w, cross_term).astype(bf16).astype(f32)
    grad_ref[:n_blocks] = grad
    grad_ref[n_blocks:] = pltpu.roll(grad, HALF, 1)


def pair(x, discount):
    n_blocks = x.shape[0] // 2
    span = n_blocks // 2
    return pl.pallas_call(
        pair_kernel,
        out_shape=(
            jax.ShapeDtypeStruct(x.shape, f32),
            jax.ShapeDtypeStruct((1, LANES), f32),
        ),
        scratch_shapes=[
            pltpu.VMEM((2 * n_blocks, LANES), f32),
            pltpu.VMEM((2 * n_blocks, LANES), f32),
            pltpu.VMEM((n_blocks + span, 8, LANES), f32),
            pltpu.VMEM((n_blocks + 1, LANES), f32),
            pltpu.VMEM((n_blocks + 1, LANES, LANES), f32),
            pltpu.VMEM((n_blocks + 1, LANES, LANES), f32),
            pltpu.VMEM((n_blocks, span, LANES, LANES), f32),
            pltpu.VMEM((span, LANES, LANES), f32),
        ],
        compiler_params=params(44),
        name="pair",
    )(x, discount)


def share_kernel(grad_ref, idsg_ref, refreshed_ref, out_ref, rows_w):
    lists, cache_rows = rows_w.shape
    for g in range(lists // 8):
        part = slice(8 * g, 8 * g + 8)
        grads = grad_ref[part, :]
        ids = idsg_ref[part, :]
        spots = [
            lax.broadcasted_iota(jnp.int32, (8, LANES), 1) + LANES * p
            for p in range(cache_rows // LANES)
        ]
        acc = [jnp.zeros((8, LANES), f32) for _ in spots]
        for j in range(HALF):
            id_j = jnp.broadcast_to(ids[:, j : j + 1], (8, LANES))
            grad_j = jnp.broadcast_to(grads[:, j : j + 1], (8, LANES))
            acc = [a + jnp.where(id_j == spot, grad_j, 0.0) for a, spot in zip(acc, spots)]
        for p, a in enumerate(acc):
            rows_w[part, p * LANES : (p + 1) * LANES] = a
    weights = rows_w[...]
    high = weights.astype(bf16)
    rest = (weights - high.astype(f32)).astype(bf16)
    refreshed = refreshed_ref[...]
    out_ref[...] = jnp.dot(high, refreshed, preferred_element_type=f32) + jnp.dot(
        rest, refreshed, preferred_element_type=f32
    )


def share(grads, idsg, refreshed):
    return pl.pallas_call(
        share_kernel,
        out_shape=jax.ShapeDtypeStruct((grads.shape[0], refreshed.shape[1]), f32),
        scratch_shapes=[pltpu.VMEM((grads.shape[0], refreshed.shape[0]), f32)],
        compiler_params=params(),
        name="share",
    )(grads, idsg, refreshed)


Y, ZZ, ZL, X = 4, 4, 2, 2


def shard_at(y, zz, zl, x):
    return ((y * ZZ + zz) * ZL + zl) * X + x


def everywhere():
    return [
        (y, zz, zl, x) for y in range(Y) for zz in range(ZZ) for zl in range(ZL) for x in range(X)
    ]


def gather_units(block):
    groups = [
        [shard_at(y, zz, zl, x) for y in range(Y) for x in range(X)]
        for zz in range(ZZ)
        for zl in range(ZL)
    ]
    parts = len(groups[0])
    units, width = block.shape
    gathered = lax.all_to_all(
        jnp.broadcast_to(block[None], (parts, units, width)),
        "shard",
        split_axis=0,
        concat_axis=0,
        tiled=True,
        axis_index_groups=groups,
    )
    return gathered.reshape(parts * units, width)


def per_device(
    cls_states, trainer_in, trainer_out, stale_cache, block_owner, queries, neg_ids, grades
):
    shards = lax.axis_size("shard")
    roles = lax.axis_size("role")
    width = cls_states.shape[1]
    barrier = lax.optimization_barrier

    def to_core(v):
        return lax.ppermute(v, "role", [(0, 1), (1, 0), (2, 3), (3, 2)])

    def to_across(v):
        return lax.ppermute(v, "role", [(0, 2), (1, 3), (2, 0), (3, 1)])

    def to_along(v):
        return lax.ppermute(
            v,
            "shard",
            [
                (shard_at(y, zz, zl, x), shard_at(y, zz, 1 - zl, x))
                for y, zz, zl, x in everywhere()
            ],
        )

    def to_diagonal(v):
        return lax.ppermute(
            v,
            ("role", "shard"),
            [
                (r * shards + shard_at(y, zz, zl, x), (r ^ 2) * shards + shard_at(y, zz, 1 - zl, x))
                for r in range(roles)
                for y, zz, zl, x in everywhere()
            ],
        )

    role_of = (0, 2, 1, 3)
    axes = ("role", "shard")
    mine = jnp.concatenate((trainer_in[0], trainer_out[0]), 1)
    mine = lax.ppermute(
        mine,
        axes,
        [
            (
                (roles - 1) * shards + shard_at(y, zz, zl, x),
                role_of[zz] * shards + shard_at(y, zz, zl, x),
            )
            for y, zz, zl, x in everywhere()
        ],
    )
    mine, cls_after = barrier((mine, cls_states))
    block = mine
    for by in range(1, ZZ):
        turn = [
            (
                role_of[zz] * shards + shard_at(y, zz, zl, x),
                role_of[zz] * shards + shard_at(y, (zz + by) % ZZ, zl, x),
            )
            for y, zz, zl, x in everywhere()
        ]
        block = block + lax.ppermute(mine, axes, turn)
    x_across = to_across(cls_after)
    block, x_across, cls_after = barrier((block, x_across, cls_after))
    units = gather_units(block)
    xs = (cls_states, x_across, to_along(cls_after), to_along(x_across))
    query = jnp.pad(queries.reshape(-1, LANES), ((0, SUB - width // LANES), (0, 0)))
    idsg = jnp.concatenate((neg_ids, grades), 1)
    units, xs, query, idsg = barrier((units, xs, query, idsg))
    other_units = to_core(units)
    so_far = first_half(xs, units)
    (diagonal,) = second_half(xs, other_units, so_far, (3,), bf16)
    from_diagonal = to_diagonal(diagonal)
    other_units, diagonal = barrier((other_units, diagonal))
    across, along = second_half(xs, other_units, so_far, (1, 2), bf16)
    from_across = to_across(across)
    from_along = to_along(along)
    (own,) = second_half(xs, other_units, so_far, (0,), f32)
    outgoing = place(
        cls_states,
        own,
        from_across,
        from_along,
        from_diagonal,
        block_owner.reshape(1, -1),
        query,
        shards,
    )
    outgoing, idsg = barrier((outgoing, idsg))
    arrived = lax.all_to_all(
        outgoing.reshape(shards, SUB, -1), "shard", split_axis=0, concat_axis=0, tiled=True
    )
    refreshed, again, packed = score(arrived.reshape(shards * SUB, -1), stale_cache, idsg)
    packed = lax.all_to_all(packed, "shard", split_axis=0, concat_axis=0, tiled=True)
    count = shards * neg_ids.shape[1]
    position = np.arange(1, count + 1, dtype=np.float64)
    discount = (1.0 / np.log2(1.0 + position)).astype(np.float32).reshape(-1, LANES)
    grads, loss = pair(packed, jnp.asarray(discount))
    grads = lax.all_to_all(grads, "shard", split_axis=0, concat_axis=0, tiled=True)
    shares = share(grads, idsg, again)
    shares = lax.all_to_all(shares, "shard", split_axis=0, concat_axis=0, tiled=True)
    return refreshed, jnp.sum(shares, 0, keepdims=True), loss[0, :1]


def solution(mesh):
    return jax.shard_map(
        per_device,
        mesh=mesh,
        in_specs=(
            P(("role", "shard"), None),
            P("role", "shard", None),
            P("role", "shard", None),
            P(("role", "shard"), None),
            P(("role", "shard"), None),
            P(("role", "shard"), None),
            P("role", "shard"),
            P("role", "shard"),
        ),
        out_specs=(P(("role", "shard"), None), P(("role", "shard"), None), P(("role", "shard"))),
        check_vma=False,
    )
```

```python
import functools
import math

import jax
import jax.numpy as jnp
import numpy as np
from jax import lax
from jax.experimental import pallas as pl
from jax.experimental.pallas import tpu as pltpu
from jax.sharding import PartitionSpec as P

CAP = 2
EPSILON = 1e-05
LOG_TWO = math.log(2.0)
EMPTY = 1024.0

f32 = jnp.float32
bf16 = jnp.bfloat16
LANES = 128


def params(mebibytes=16):
    return pltpu.CompilerParams(vmem_limit_bytes=mebibytes * 1024 * 1024)


def contract_last(a, b):
    return lax.dot_general(a, b, (((1,), (1,)), ((), ())), preferred_element_type=f32)


def partial_sums(x, w_ref):
    width = x.shape[1]
    inner = contract_last(x, w_ref[:, :width])
    hidden = 0.5 * inner * (1.0 + lax.erf(inner * math.sqrt(0.5)))
    return jnp.dot(hidden.astype(bf16), w_ref[:, width:], preferred_element_type=f32)


def first_kernel(own_ref, across_ref, along_ref, diagonal_ref, w_ref, out_ref):
    for n, x_ref in enumerate((own_ref, across_ref, along_ref, diagonal_ref)):
        out_ref[n] = partial_sums(x_ref[...], w_ref)


def first_half(xs, units):
    return pl.pallas_call(
        first_kernel,
        out_shape=jax.ShapeDtypeStruct((len(xs),) + xs[0].shape, f32),
        compiler_params=params(),
        name="encode",
    )(*xs, units)


def second_kernel(at, *refs):
    x_refs, (w_ref, so_far_ref), out_refs = refs[: len(at)], refs[len(at) :][:2], refs[-len(at) :]
    for n, x_ref, out_ref in zip(at, x_refs, out_refs):
        part = so_far_ref[n] + partial_sums(x_ref[...], w_ref)
        out_ref[...] = part.astype(out_ref.dtype)


def second_half(xs, units, so_far, at, dtype):
    return pl.pallas_call(
        functools.partial(second_kernel, at),
        out_shape=tuple(jax.ShapeDtypeStruct(xs[n].shape, dtype) for n in at),
        compiler_params=params(),
        name="encode_rest",
    )(*(xs[n] for n in at), units, so_far)


ROWS, SUB = 32, 8


def place_kernel(
    cls_ref, own_ref, across_ref, along_ref, diagonal_ref, owner_ref, query_ref, out_ref
):
    rows, width = cls_ref.shape
    blocks = owner_ref.shape[1]
    shards = out_ref.shape[0] // SUB
    chunks = width // LANES
    resid = cls_ref[...].astype(f32) + own_ref[...]
    for part_ref in (across_ref, along_ref, diagonal_ref):
        resid = resid + part_ref[...].astype(f32)
    centred = resid - jnp.mean(resid, -1, keepdims=True)
    variance = jnp.mean(centred * centred, -1, keepdims=True)
    fresh = (centred * lax.rsqrt(variance + EPSILON)).astype(bf16)

    owner = owner_ref[...]
    shard_of = lax.broadcasted_iota(jnp.int32, (shards, blocks), 0)
    onehot = (shard_of == owner).astype(f32)
    before = lax.broadcasted_iota(jnp.int32, (blocks, blocks), 0) < lax.broadcasted_iota(
        jnp.int32, (blocks, blocks), 1
    )
    earlier = jnp.dot(onehot.astype(bf16), before.astype(bf16), preferred_element_type=f32)
    slot = jnp.sum(earlier * onehot, 0, keepdims=True)
    passage = lax.broadcasted_iota(jnp.int32, (blocks, rows), 1)
    block = lax.broadcasted_iota(jnp.int32, (blocks, rows), 0)
    widen = (passage // 2 == block).astype(bf16)
    both = jnp.concatenate(
        (jnp.broadcast_to(owner.astype(f32), (8, blocks)), jnp.broadcast_to(slot, (8, blocks))), 0
    )
    both = jnp.dot(both.astype(bf16), widen, preferred_element_type=f32)
    parity = lax.broadcasted_iota(jnp.int32, (1, rows), 1) & 1
    target = both[0:1] * (2.0 * CAP * chunks) + (both[8:9] * 2.0 + parity.astype(f32)) * chunks

    passage_rows = 2 * CAP * chunks
    row = lax.broadcasted_iota(jnp.int32, (shards * passage_rows, rows), 0).astype(f32)
    placed = jnp.zeros((shards * passage_rows, LANES), f32)
    taken = jnp.zeros((shards * passage_rows, rows), f32)
    for j in range(chunks):
        onto = (row == target + float(j)).astype(f32)
        taken = taken + onto
        placed = placed + jnp.dot(
            onto.astype(bf16), fresh[:, j * LANES : (j + 1) * LANES], preferred_element_type=f32
        )
    filled = jnp.dot(taken.astype(bf16), jnp.ones((rows, LANES), bf16), preferred_element_type=f32)
    placed = jnp.where(filled > 0.5, placed, EMPTY).reshape(shards, passage_rows, LANES)
    for tile in range(ROWS // SUB):
        if tile < passage_rows // SUB:
            part = placed[:, tile * SUB : (tile + 1) * SUB]
        else:
            part = jnp.broadcast_to(query_ref[...].astype(f32)[None], (shards, SUB, LANES))
        part = part.reshape(shards * SUB, LANES).astype(bf16)
        out_ref[:, tile * LANES : (tile + 1) * LANES] = part


def place(cls_states, own, across, along, diagonal, owner, query, shards):
    return pl.pallas_call(
        place_kernel,
        out_shape=jax.ShapeDtypeStruct((shards * SUB, ROWS // SUB * LANES), bf16),
        compiler_params=params(),
        name="place",
    )(cls_states, own, across, along, diagonal, owner, query)


def score_kernel(
    recv_ref, stale_ref, idsg_ref, refreshed_ref, again_ref, packed_ref, recv_s, arrived_s
):
    cache_rows, width = stale_ref.shape
    shards = recv_ref.shape[0] // SUB
    chunks = width // LANES
    per_shard = cache_rows // shards
    for tile in range(ROWS // SUB):
        recv_s[tile] = recv_ref[:, tile * LANES : (tile + 1) * LANES].astype(f32)

    def arrived_row(r):
        return recv_s[r // SUB, pl.ds(r % SUB, shards, stride=SUB), :]

    queries = []
    for j in range(chunks):
        for c in range(per_shard):
            arrived_s[j, pl.ds(c, shards, stride=per_shard), :] = arrived_row(c * chunks + j)
        queries.append(arrived_row(per_shard * chunks + j))
    queries = jnp.concatenate(queries, 1).astype(bf16)
    arrived = jnp.concatenate([arrived_s[j] for j in range(chunks)], 1)
    refreshed = jnp.where(arrived > 0.5 * EMPTY, stale_ref[...].astype(f32), arrived).astype(bf16)
    refreshed_ref[...] = refreshed
    again_ref[...] = refreshed
    scores = contract_last(queries, refreshed)
    ids = idsg_ref[...]
    lane = lax.broadcasted_iota(jnp.int32, ids.shape, 1)
    low = ids & (LANES - 1)
    picked = jnp.zeros(ids.shape, f32)
    for part in range(cache_rows // LANES):
        here = jnp.take_along_axis(scores[:, part * LANES : (part + 1) * LANES], low, axis=1)
        picked = jnp.where(ids // LANES == part, here, picked)
    packed_ref[...] = jnp.where(lane < LANES // 2, picked, ids.astype(f32))


def score(recv, stale, idsg):
    return pl.pallas_call(
        score_kernel,
        out_shape=(
            jax.ShapeDtypeStruct(stale.shape, bf16),
            jax.ShapeDtypeStruct(stale.shape, bf16),
            jax.ShapeDtypeStruct(idsg.shape, f32),
        ),
        scratch_shapes=[
            pltpu.VMEM((ROWS // SUB, recv.shape[0], LANES), f32),
            pltpu.VMEM((stale.shape[1] // LANES, stale.shape[0], LANES), f32),
        ],
        compiler_params=params(),
        name="score",
    )(recv, stale, idsg)


HALF = LANES // 2


def pair_kernel(
    x_ref, discount_ref, grad_ref, loss_ref, half_s, wide_w, columns, across, spread_s, rows_s, near_q, far_q
):
    x = x_ref[...]
    n_blocks = x.shape[0] // 2
    count = n_blocks * LANES
    top, low = x[:n_blocks], x[n_blocks:]
    lane = lax.broadcasted_iota(jnp.int32, (n_blocks, LANES), 1)
    left = lane < HALF
    scores = jnp.where(left, top, pltpu.roll(low, HALF, 1))
    gains = jnp.exp2(jnp.where(left, pltpu.roll(top, HALF, 1), low))
    position = lax.broadcasted_iota(jnp.int32, (n_blocks, LANES), 0) * LANES + lane

    ordered = jnp.ones((n_blocks, LANES), f32)
    for level in range(1, 5):
        above = jnp.sum((gains > float(2**level) - 0.5).astype(f32))
        ordered = jnp.where(position.astype(f32) < above, float(2**level), ordered)
    ideal = jnp.sum(ordered * discount_ref[...])

    span = n_blocks // 2
    groups = LANES // 8

    def sweep(values, load_or_make):
        columns[...] = jnp.zeros_like(columns)
        values[n_blocks:] = values[:n_blocks]

        def spread(i):
            spread_s[i] = jnp.broadcast_to(values[pl.ds(i, 1), :], (LANES, LANES)).T

        def collect(i):
            across[pl.ds(i, 1), :] = jnp.sum(rows_s[i].T, 0, keepdims=True)

        def block(i, last):
            first = [spread_s[i, pl.ds(8 * g, 8), :] for g in range(groups)]
            collect(i)
            spread(i + 1)
            acc = [jnp.zeros((8, LANES), f32) for _ in range(groups)]
            for d in range(last + 1):
                k = i + d
                kept = near_q.at[i, d] if d < span else far_q.at[i]
                v_k = jnp.broadcast_to(values[pl.ds(k, 1), :], (8, LANES))
                column = [jnp.zeros((8, LANES), f32) for _ in range(4)]
                for g in range(groups):
                    value = load_or_make(first[g], v_k, kept, 8 * g)
                    acc[g] = acc[g] + value
                    column[g % 4] = column[g % 4] + value
                if d > 0:
                    columns[k] = columns[k] + ((column[0] + column[1]) + (column[2] + column[3]))
            for g in range(groups):
                rows_s[i + 1, pl.ds(8 * g, 8), :] = acc[g]
            return 0

        rows_s[0] = jnp.zeros((LANES, LANES), f32)
        spread(0)
        lax.fori_loop(0, span, lambda i, _: block(i, span), 0, unroll=2)
        lax.fori_loop(span, n_blocks, lambda i, _: block(i, span - 1), 0, unroll=2)
        collect(n_blocks)
        folded = jnp.sum(columns[...], 1)
        wrapped = jnp.concatenate((folded[n_blocks:], jnp.zeros((span, LANES), f32)), 0)
        return across[1:] - folded[:n_blocks] - wrapped

    def rank_term(s_i, s_k, kept, at):
        t = jnp.tanh(s_k - s_i)
        kept[pl.ds(at, 8), :] = 1.0 - t * t
        return t

    def cross_term(w_i, w_k, kept, at):
        return (w_k - w_i) * kept[pl.ds(at, 8), :]

    half_s[:n_blocks] = 0.5 * scores
    rank = 0.5 + 0.5 * count + 0.5 * sweep(half_s, rank_term)
    logged = jnp.log2(1.0 + rank)
    weight = gains / (ideal * LOG_TWO * (1.0 + rank) * logged * logged)
    loss_ref[...] = jnp.full((1, LANES), 1.0 - jnp.sum(gains / logged) / ideal, f32)
    wide_w[:n_blocks] = 0.25 * weight
    grad = sweep(wide_w, cross_term).astype(bf16).astype(f32)
    grad_ref[:n_blocks] = grad
    grad_ref[n_blocks:] = pltpu.roll(grad, HALF, 1)


def pair(x, discount):
    n_blocks = x.shape[0] // 2
    span = n_blocks // 2
    return pl.pallas_call(
        pair_kernel,
        out_shape=(
            jax.ShapeDtypeStruct(x.shape, f32),
            jax.ShapeDtypeStruct((1, LANES), f32),
        ),
        scratch_shapes=[
            pltpu.VMEM((2 * n_blocks, LANES), f32),
            pltpu.VMEM((2 * n_blocks, LANES), f32),
            pltpu.VMEM((n_blocks + span, 8, LANES), f32),
            pltpu.VMEM((n_blocks + 1, LANES), f32),
            pltpu.VMEM((n_blocks + 1, LANES, LANES), f32),
            pltpu.VMEM((n_blocks + 1, LANES, LANES), f32),
            pltpu.VMEM((n_blocks, span, LANES, LANES), f32),
            pltpu.VMEM((span, LANES, LANES), f32),
        ],
        compiler_params=params(44),
        name="pair",
    )(x, discount)


def share_kernel(grad_ref, idsg_ref, refreshed_ref, out_ref, rows_w):
    lists, cache_rows = rows_w.shape
    for g in range(lists // 8):
        part = slice(8 * g, 8 * g + 8)
        grads = grad_ref[part, :]
        ids = idsg_ref[part, :]
        spots = [
            lax.broadcasted_iota(jnp.int32, (8, LANES), 1) + LANES * p
            for p in range(cache_rows // LANES)
        ]
        acc = [jnp.zeros((8, LANES), f32) for _ in spots]
        for j in range(HALF):
            id_j = jnp.broadcast_to(ids[:, j : j + 1], (8, LANES))
            grad_j = jnp.broadcast_to(grads[:, j : j + 1], (8, LANES))
            acc = [a + jnp.where(id_j == spot, grad_j, 0.0) for a, spot in zip(acc, spots)]
        for p, a in enumerate(acc):
            rows_w[part, p * LANES : (p + 1) * LANES] = a
    weights = rows_w[...]
    high = weights.astype(bf16)
    rest = (weights - high.astype(f32)).astype(bf16)
    refreshed = refreshed_ref[...]
    out_ref[...] = jnp.dot(high, refreshed, preferred_element_type=f32) + jnp.dot(
        rest, refreshed, preferred_element_type=f32
    )


def share(grads, idsg, refreshed):
    return pl.pallas_call(
        share_kernel,
        out_shape=jax.ShapeDtypeStruct((grads.shape[0], refreshed.shape[1]), f32),
        scratch_shapes=[pltpu.VMEM((grads.shape[0], refreshed.shape[0]), f32)],
        compiler_params=params(),
        name="share",
    )(grads, idsg, refreshed)


def total_kernel(x_ref, out_ref):
    out_ref[...] = jnp.sum(x_ref[...], 0)


def total(x):
    return pl.pallas_call(
        total_kernel,
        out_shape=jax.ShapeDtypeStruct(x.shape[1:], f32),
        compiler_params=params(),
        name="total",
    )(x)


Y, ZZ, ZL, X = 4, 4, 2, 2


def shard_at(y, zz, zl, x):
    return ((y * ZZ + zz) * ZL + zl) * X + x


def everywhere():
    return [
        (y, zz, zl, x) for y in range(Y) for zz in range(ZZ) for zl in range(ZL) for x in range(X)
    ]


def gather_units(block):
    groups = [
        [shard_at(y, zz, zl, x) for y in range(Y) for x in range(X)]
        for zz in range(ZZ)
        for zl in range(ZL)
    ]
    parts = len(groups[0])
    units, width = block.shape
    gathered = lax.all_to_all(
        jnp.broadcast_to(block[None], (parts, units, width)),
        "shard",
        split_axis=0,
        concat_axis=0,
        tiled=True,
        axis_index_groups=groups,
    )
    return gathered.reshape(parts * units, width)


def per_device(
    cls_states, trainer_in, trainer_out, stale_cache, block_owner, queries, neg_ids, grades
):
    shards = lax.axis_size("shard")
    roles = lax.axis_size("role")
    width = cls_states.shape[1]
    barrier = lax.optimization_barrier

    def to_core(v):
        return lax.ppermute(v, "role", [(0, 1), (1, 0), (2, 3), (3, 2)])

    def to_across(v):
        return lax.ppermute(v, "role", [(0, 2), (1, 3), (2, 0), (3, 1)])

    def to_along(v):
        return lax.ppermute(
            v,
            "shard",
            [
                (shard_at(y, zz, zl, x), shard_at(y, zz, 1 - zl, x))
                for y, zz, zl, x in everywhere()
            ],
        )

    def to_diagonal(v):
        return lax.ppermute(
            v,
            ("role", "shard"),
            [
                (r * shards + shard_at(y, zz, zl, x), (r ^ 2) * shards + shard_at(y, zz, 1 - zl, x))
                for r in range(roles)
                for y, zz, zl, x in everywhere()
            ],
        )

    role_of = (0, 2, 1, 3)
    axes = ("role", "shard")
    mine = jnp.concatenate((trainer_in[0], trainer_out[0]), 1)
    mine = lax.ppermute(
        mine,
        axes,
        [
            (
                (roles - 1) * shards + shard_at(y, zz, zl, x),
                role_of[zz] * shards + shard_at(y, zz, zl, x),
            )
            for y, zz, zl, x in everywhere()
        ],
    )
    mine, cls_after = barrier((mine, cls_states))
    block = mine
    for by in range(1, ZZ):
        turn = [
            (
                role_of[zz] * shards + shard_at(y, zz, zl, x),
                role_of[zz] * shards + shard_at(y, (zz + by) % ZZ, zl, x),
            )
            for y, zz, zl, x in everywhere()
        ]
        block = block + lax.ppermute(mine, axes, turn)
    x_across = to_across(cls_after)
    block, x_across, cls_after = barrier((block, x_across, cls_after))
    units = gather_units(block)
    xs = (cls_states, x_across, to_along(cls_after), to_along(x_across))
    query = jnp.pad(queries.reshape(-1, LANES), ((0, SUB - width // LANES), (0, 0)))
    idsg = jnp.concatenate((neg_ids, grades), 1)
    units, xs, query, idsg = barrier((units, xs, query, idsg))
    other_units = to_core(units)
    so_far = first_half(xs, units)
    (diagonal,) = second_half(xs, other_units, so_far, (3,), bf16)
    from_diagonal = to_diagonal(diagonal)
    other_units, diagonal = barrier((other_units, diagonal))
    across, along = second_half(xs, other_units, so_far, (1, 2), bf16)
    from_across = to_across(across)
    from_along = to_along(along)
    (own,) = second_half(xs, other_units, so_far, (0,), f32)
    outgoing = place(
        cls_states,
        own,
        from_across,
        from_along,
        from_diagonal,
        block_owner.reshape(1, -1),
        query,
        shards,
    )
    outgoing, idsg = barrier((outgoing, idsg))
    arrived = lax.all_to_all(
        outgoing.reshape(shards, SUB, -1), "shard", split_axis=0, concat_axis=0, tiled=True
    )
    refreshed, again, packed = score(arrived.reshape(shards * SUB, -1), stale_cache, idsg)
    packed = lax.all_to_all(packed, "shard", split_axis=0, concat_axis=0, tiled=True)
    count = shards * neg_ids.shape[1]
    position = np.arange(1, count + 1, dtype=np.float64)
    discount = (1.0 / np.log2(1.0 + position)).astype(np.float32).reshape(-1, LANES)
    grads, loss = pair(packed, jnp.asarray(discount))
    grads = lax.all_to_all(grads, "shard", split_axis=0, concat_axis=0, tiled=True)
    shares = share(grads, idsg, again).reshape(shards, 1, width)
    shares = lax.all_to_all(shares, "shard", split_axis=0, concat_axis=0, tiled=True)
    return refreshed, total(shares), loss[0, :1]


def solution(mesh):
    return jax.shard_map(
        per_device,
        mesh=mesh,
        in_specs=(
            P(("role", "shard"), None),
            P("role", "shard", None),
            P("role", "shard", None),
            P(("role", "shard"), None),
            P(("role", "shard"), None),
            P(("role", "shard"), None),
            P("role", "shard"),
            P("role", "shard"),
        ),
        out_specs=(P(("role", "shard"), None), P(("role", "shard"), None), P(("role", "shard"))),
        check_vma=False,
    )
```

```python
import functools
import math

import jax
import jax.numpy as jnp
import numpy as np
from jax import lax
from jax.experimental import pallas as pl
from jax.experimental.pallas import tpu as pltpu
from jax.sharding import PartitionSpec as P

CAP = 2
EPSILON = 1e-05
LOG_TWO = math.log(2.0)
EMPTY = 1024.0

f32 = jnp.float32
bf16 = jnp.bfloat16
LANES = 128


def params(mebibytes=16):
    return pltpu.CompilerParams(vmem_limit_bytes=mebibytes * 1024 * 1024)


def contract_last(a, b):
    return lax.dot_general(a, b, (((1,), (1,)), ((), ())), preferred_element_type=f32)


def partial_sums(x, w_ref):
    width = x.shape[1]
    inner = contract_last(x, w_ref[:, :width])
    hidden = 0.5 * inner * (1.0 + lax.erf(inner * math.sqrt(0.5)))
    return jnp.dot(hidden.astype(bf16), w_ref[:, width:], preferred_element_type=f32)


def first_kernel(own_ref, across_ref, along_ref, diagonal_ref, w_ref, out_ref):
    for n, x_ref in enumerate((own_ref, across_ref, along_ref, diagonal_ref)):
        out_ref[n] = partial_sums(x_ref[...], w_ref)


def first_half(xs, units):
    return pl.pallas_call(
        first_kernel,
        out_shape=jax.ShapeDtypeStruct((len(xs),) + xs[0].shape, f32),
        compiler_params=params(),
        name="encode",
    )(*xs, units)


def second_kernel(at, *refs):
    x_refs, (w_ref, so_far_ref), out_refs = refs[: len(at)], refs[len(at) :][:2], refs[-len(at) :]
    for n, x_ref, out_ref in zip(at, x_refs, out_refs):
        part = so_far_ref[n] + partial_sums(x_ref[...], w_ref)
        out_ref[...] = part.astype(out_ref.dtype)


def second_half(xs, units, so_far, at, dtype):
    return pl.pallas_call(
        functools.partial(second_kernel, at),
        out_shape=tuple(jax.ShapeDtypeStruct(xs[n].shape, dtype) for n in at),
        compiler_params=params(),
        name="encode_rest",
    )(*(xs[n] for n in at), units, so_far)


ROWS, SUB = 32, 8


def place_kernel(
    cls_ref, own_ref, across_ref, along_ref, diagonal_ref, owner_ref, query_ref, out_ref
):
    rows, width = cls_ref.shape
    blocks = owner_ref.shape[1]
    shards = out_ref.shape[0] // SUB
    chunks = width // LANES
    resid = cls_ref[...].astype(f32) + own_ref[...]
    for part_ref in (across_ref, along_ref, diagonal_ref):
        resid = resid + part_ref[...].astype(f32)
    centred = resid - jnp.mean(resid, -1, keepdims=True)
    variance = jnp.mean(centred * centred, -1, keepdims=True)
    fresh = (centred * lax.rsqrt(variance + EPSILON)).astype(bf16)

    owner = owner_ref[...]
    shard_of = lax.broadcasted_iota(jnp.int32, (shards, blocks), 0)
    onehot = (shard_of == owner).astype(f32)
    before = lax.broadcasted_iota(jnp.int32, (blocks, blocks), 0) < lax.broadcasted_iota(
        jnp.int32, (blocks, blocks), 1
    )
    earlier = jnp.dot(onehot.astype(bf16), before.astype(bf16), preferred_element_type=f32)
    slot = jnp.sum(earlier * onehot, 0, keepdims=True)
    passage = lax.broadcasted_iota(jnp.int32, (blocks, rows), 1)
    block = lax.broadcasted_iota(jnp.int32, (blocks, rows), 0)
    widen = (passage // 2 == block).astype(bf16)
    both = jnp.concatenate(
        (jnp.broadcast_to(owner.astype(f32), (8, blocks)), jnp.broadcast_to(slot, (8, blocks))), 0
    )
    both = jnp.dot(both.astype(bf16), widen, preferred_element_type=f32)
    parity = lax.broadcasted_iota(jnp.int32, (1, rows), 1) & 1
    target = both[0:1] * (2.0 * CAP * chunks) + (both[8:9] * 2.0 + parity.astype(f32)) * chunks

    passage_rows = 2 * CAP * chunks
    row = lax.broadcasted_iota(jnp.int32, (shards * passage_rows, rows), 0).astype(f32)
    placed = jnp.zeros((shards * passage_rows, LANES), f32)
    taken = jnp.zeros((shards * passage_rows, rows), f32)
    for j in range(chunks):
        onto = (row == target + float(j)).astype(f32)
        taken = taken + onto
        placed = placed + jnp.dot(
            onto.astype(bf16), fresh[:, j * LANES : (j + 1) * LANES], preferred_element_type=f32
        )
    filled = jnp.dot(taken.astype(bf16), jnp.ones((rows, LANES), bf16), preferred_element_type=f32)
    placed = jnp.where(filled > 0.5, placed, EMPTY).reshape(shards, passage_rows, LANES)
    for tile in range(ROWS // SUB):
        if tile < passage_rows // SUB:
            part = placed[:, tile * SUB : (tile + 1) * SUB]
        else:
            part = jnp.broadcast_to(query_ref[...].astype(f32)[None], (shards, SUB, LANES))
        part = part.reshape(shards * SUB, LANES).astype(bf16)
        out_ref[:, tile * LANES : (tile + 1) * LANES] = part


def place(cls_states, own, across, along, diagonal, owner, query, shards):
    return pl.pallas_call(
        place_kernel,
        out_shape=jax.ShapeDtypeStruct((shards * SUB, ROWS // SUB * LANES), bf16),
        compiler_params=params(),
        name="place",
    )(cls_states, own, across, along, diagonal, owner, query)


def score_kernel(
    recv_ref, stale_ref, idsg_ref, refreshed_ref, again_ref, packed_ref, recv_s, arrived_s
):
    cache_rows, width = stale_ref.shape
    shards = recv_ref.shape[0] // SUB
    chunks = width // LANES
    per_shard = cache_rows // shards
    for tile in range(ROWS // SUB):
        recv_s[tile] = recv_ref[:, tile * LANES : (tile + 1) * LANES].astype(f32)

    def arrived_row(r):
        return recv_s[r // SUB, pl.ds(r % SUB, shards, stride=SUB), :]

    queries = []
    for j in range(chunks):
        for c in range(per_shard):
            arrived_s[j, pl.ds(c, shards, stride=per_shard), :] = arrived_row(c * chunks + j)
        queries.append(arrived_row(per_shard * chunks + j))
    queries = jnp.concatenate(queries, 1).astype(bf16)
    arrived = jnp.concatenate([arrived_s[j] for j in range(chunks)], 1)
    refreshed = jnp.where(arrived > 0.5 * EMPTY, stale_ref[...].astype(f32), arrived).astype(bf16)
    refreshed_ref[...] = refreshed
    again_ref[...] = refreshed
    scores = contract_last(queries, refreshed)
    ids = idsg_ref[...]
    lane = lax.broadcasted_iota(jnp.int32, ids.shape, 1)
    low = ids & (LANES - 1)
    picked = jnp.zeros(ids.shape, f32)
    for part in range(cache_rows // LANES):
        here = jnp.take_along_axis(scores[:, part * LANES : (part + 1) * LANES], low, axis=1)
        picked = jnp.where(ids // LANES == part, here, picked)
    packed_ref[...] = jnp.where(lane < LANES // 2, picked, ids.astype(f32))


def score(recv, stale, idsg):
    return pl.pallas_call(
        score_kernel,
        out_shape=(
            jax.ShapeDtypeStruct(stale.shape, bf16),
            jax.ShapeDtypeStruct(stale.shape, bf16),
            jax.ShapeDtypeStruct(idsg.shape, f32),
        ),
        scratch_shapes=[
            pltpu.VMEM((ROWS // SUB, recv.shape[0], LANES), f32),
            pltpu.VMEM((stale.shape[1] // LANES, stale.shape[0], LANES), f32),
        ],
        compiler_params=params(),
        name="score",
    )(recv, stale, idsg)


HALF = LANES // 2


def pair_kernel(
    x_ref, discount_ref, grad_ref, loss_ref, half_s, wide_w, columns, across, spread_s, rows_s, near_q, far_q
):
    x = x_ref[...]
    n_blocks = x.shape[0] // 2
    count = n_blocks * LANES
    top, low = x[:n_blocks], x[n_blocks:]
    lane = lax.broadcasted_iota(jnp.int32, (n_blocks, LANES), 1)
    left = lane < HALF
    scores = jnp.where(left, top, pltpu.roll(low, HALF, 1))
    gains = jnp.exp2(jnp.where(left, pltpu.roll(top, HALF, 1), low))
    position = lax.broadcasted_iota(jnp.int32, (n_blocks, LANES), 0) * LANES + lane

    ordered = jnp.ones((n_blocks, LANES), f32)
    for level in range(1, 5):
        above = jnp.sum((gains > float(2**level) - 0.5).astype(f32))
        ordered = jnp.where(position.astype(f32) < above, float(2**level), ordered)
    ideal = jnp.sum(ordered * discount_ref[...])

    span = n_blocks // 2
    groups = LANES // 8

    def sweep(values, load_or_make):
        columns[...] = jnp.zeros_like(columns)
        values[n_blocks:] = values[:n_blocks]

        def spread(i):
            spread_s[i] = jnp.broadcast_to(values[pl.ds(i, 1), :], (LANES, LANES)).T

        def collect(i):
            across[pl.ds(i, 1), :] = jnp.sum(rows_s[i].T, 0, keepdims=True)

        def block(i, last):
            first = [spread_s[i, pl.ds(8 * g, 8), :] for g in range(groups)]
            collect(i)
            spread(i + 1)
            acc = [jnp.zeros((8, LANES), f32) for _ in range(groups)]
            for d in range(last + 1):
                k = i + d
                kept = near_q.at[i, d] if d < span else far_q.at[i]
                v_k = jnp.broadcast_to(values[pl.ds(k, 1), :], (8, LANES))
                column = [jnp.zeros((8, LANES), f32) for _ in range(4)]
                for g in range(groups):
                    value = load_or_make(first[g], v_k, kept, 8 * g)
                    acc[g] = acc[g] + value
                    column[g % 4] = column[g % 4] + value
                if d > 0:
                    columns[k] = columns[k] + ((column[0] + column[1]) + (column[2] + column[3]))
            for g in range(groups):
                rows_s[i + 1, pl.ds(8 * g, 8), :] = acc[g]
            return 0

        rows_s[0] = jnp.zeros((LANES, LANES), f32)
        spread(0)
        lax.fori_loop(0, span, lambda i, _: block(i, span), 0, unroll=2)
        lax.fori_loop(span, n_blocks, lambda i, _: block(i, span - 1), 0, unroll=2)
        collect(n_blocks)
        folded = jnp.sum(columns[...], 1)
        wrapped = jnp.concatenate((folded[n_blocks:], jnp.zeros((span, LANES), f32)), 0)
        return across[1:] - folded[:n_blocks] - wrapped

    def rank_term(s_i, s_k, kept, at):
        t = jnp.tanh(s_k - s_i)
        kept[pl.ds(at, 8), :] = 1.0 - t * t
        return t

    def cross_term(w_i, w_k, kept, at):
        return (w_k - w_i) * kept[pl.ds(at, 8), :]

    half_s[:n_blocks] = 0.5 * scores
    rank = 0.5 + 0.5 * count + 0.5 * sweep(half_s, rank_term)
    logged = jnp.log2(1.0 + rank)
    weight = gains / (ideal * LOG_TWO * (1.0 + rank) * logged * logged)
    loss_ref[...] = jnp.full((1, LANES), 1.0 - jnp.sum(gains / logged) / ideal, f32)
    wide_w[:n_blocks] = 0.25 * weight
    grad = sweep(wide_w, cross_term).astype(bf16).astype(f32)
    grad_ref[:n_blocks] = grad
    grad_ref[n_blocks:] = pltpu.roll(grad, HALF, 1)


def pair(x, discount):
    n_blocks = x.shape[0] // 2
    span = n_blocks // 2
    return pl.pallas_call(
        pair_kernel,
        out_shape=(
            jax.ShapeDtypeStruct(x.shape, f32),
            jax.ShapeDtypeStruct((1, LANES), f32),
        ),
        scratch_shapes=[
            pltpu.VMEM((2 * n_blocks, LANES), f32),
            pltpu.VMEM((2 * n_blocks, LANES), f32),
            pltpu.VMEM((n_blocks + span, 8, LANES), f32),
            pltpu.VMEM((n_blocks + 1, LANES), f32),
            pltpu.VMEM((n_blocks + 1, LANES, LANES), f32),
            pltpu.VMEM((n_blocks + 1, LANES, LANES), f32),
            pltpu.VMEM((n_blocks, span, LANES, LANES), f32),
            pltpu.VMEM((span, LANES, LANES), f32),
        ],
        compiler_params=params(44),
        name="pair",
    )(x, discount)


def share_kernel(grad_ref, idsg_ref, refreshed_ref, out_ref, rows_w):
    lists, cache_rows = rows_w.shape
    for g in range(lists // 8):
        part = slice(8 * g, 8 * g + 8)
        grads = grad_ref[part, :]
        ids = idsg_ref[part, :]
        spots = [
            lax.broadcasted_iota(jnp.int32, (8, LANES), 1) + LANES * p
            for p in range(cache_rows // LANES)
        ]
        acc = [jnp.zeros((8, LANES), f32) for _ in spots]
        for j in range(HALF):
            id_j = jnp.broadcast_to(ids[:, j : j + 1], (8, LANES))
            grad_j = jnp.broadcast_to(grads[:, j : j + 1], (8, LANES))
            acc = [a + jnp.where(id_j == spot, grad_j, 0.0) for a, spot in zip(acc, spots)]
        for p, a in enumerate(acc):
            rows_w[part, p * LANES : (p + 1) * LANES] = a
    weights = rows_w[...]
    high = weights.astype(bf16)
    rest = (weights - high.astype(f32)).astype(bf16)
    refreshed = refreshed_ref[...]
    out_ref[...] = jnp.dot(high, refreshed, preferred_element_type=f32) + jnp.dot(
        rest, refreshed, preferred_element_type=f32
    )


def share(grads, idsg, refreshed):
    return pl.pallas_call(
        share_kernel,
        out_shape=jax.ShapeDtypeStruct((grads.shape[0], refreshed.shape[1]), f32),
        scratch_shapes=[pltpu.VMEM((grads.shape[0], refreshed.shape[0]), f32)],
        compiler_params=params(),
        name="share",
    )(grads, idsg, refreshed)


def total_kernel(x_ref, out_ref):
    out_ref[...] = jnp.sum(x_ref[...], 0)


def total(x):
    return pl.pallas_call(
        total_kernel,
        out_shape=jax.ShapeDtypeStruct(x.shape[1:], f32),
        compiler_params=params(),
        name="total",
    )(x)


Y, ZZ, ZL, X = 4, 4, 2, 2


def shard_at(y, zz, zl, x):
    return ((y * ZZ + zz) * ZL + zl) * X + x


def everywhere():
    return [
        (y, zz, zl, x) for y in range(Y) for zz in range(ZZ) for zl in range(ZL) for x in range(X)
    ]


def gather_units(block):
    groups = [
        [shard_at(y, zz, zl, x) for y in range(Y) for x in range(X)]
        for zz in range(ZZ)
        for zl in range(ZL)
    ]
    parts = len(groups[0])
    units, width = block.shape
    gathered = lax.all_to_all(
        jnp.broadcast_to(block[None], (parts, units, width)),
        "shard",
        split_axis=0,
        concat_axis=0,
        tiled=True,
        axis_index_groups=groups,
    )
    return gathered.reshape(parts * units, width)


def per_device(
    cls_states, trainer_in, trainer_out, stale_cache, block_owner, queries, neg_ids, grades
):
    shards = lax.axis_size("shard")
    roles = lax.axis_size("role")
    width = cls_states.shape[1]
    barrier = lax.optimization_barrier

    def to_core(v):
        return lax.ppermute(v, "role", [(0, 1), (1, 0), (2, 3), (3, 2)])

    def to_across(v):
        return lax.ppermute(v, "role", [(0, 2), (1, 3), (2, 0), (3, 1)])

    def to_along(v):
        return lax.ppermute(
            v,
            "shard",
            [
                (shard_at(y, zz, zl, x), shard_at(y, zz, 1 - zl, x))
                for y, zz, zl, x in everywhere()
            ],
        )

    def to_diagonal(v):
        return lax.ppermute(
            v,
            ("role", "shard"),
            [
                (r * shards + shard_at(y, zz, zl, x), (r ^ 2) * shards + shard_at(y, zz, 1 - zl, x))
                for r in range(roles)
                for y, zz, zl, x in everywhere()
            ],
        )

    role_of = (0, 2, 1, 3)
    axes = ("role", "shard")
    mine = jnp.concatenate((trainer_in[0], trainer_out[0]), 1)
    mine = lax.ppermute(
        mine,
        axes,
        [
            (
                (roles - 1) * shards + shard_at(y, zz, zl, x),
                role_of[zz] * shards + shard_at(y, zz, zl, x),
            )
            for y, zz, zl, x in everywhere()
        ],
    )
    mine, cls_after = barrier((mine, cls_states))
    block = mine
    for by in range(1, ZZ):
        turn = [
            (
                role_of[zz] * shards + shard_at(y, zz, zl, x),
                role_of[zz] * shards + shard_at(y, (zz + by) % ZZ, zl, x),
            )
            for y, zz, zl, x in everywhere()
        ]
        block = block + lax.ppermute(mine, axes, turn)
    x_across = to_across(cls_after)
    block, x_across, cls_after = barrier((block, x_across, cls_after))
    units = gather_units(block)
    xs = (cls_states, x_across, to_along(cls_after), to_along(x_across))
    query = jnp.pad(queries.reshape(-1, LANES), ((0, SUB - width // LANES), (0, 0)))
    idsg = jnp.concatenate((neg_ids, grades), 1)
    units, xs, query, idsg = barrier((units, xs, query, idsg))
    other_units = to_core(units)
    so_far = first_half(xs, units)
    across, along = second_half(xs, other_units, so_far, (1, 2), bf16)
    from_across = to_across(across)
    from_along = to_along(along)
    (diagonal,) = second_half(xs, other_units, so_far, (3,), bf16)
    from_diagonal = to_diagonal(diagonal)
    (own,) = second_half(xs, other_units, so_far, (0,), f32)
    outgoing = place(
        cls_states,
        own,
        from_across,
        from_along,
        from_diagonal,
        block_owner.reshape(1, -1),
        query,
        shards,
    )
    outgoing, idsg = barrier((outgoing, idsg))
    arrived = lax.all_to_all(
        outgoing.reshape(shards, SUB, -1), "shard", split_axis=0, concat_axis=0, tiled=True
    )
    refreshed, again, packed = score(arrived.reshape(shards * SUB, -1), stale_cache, idsg)
    packed = lax.all_to_all(packed, "shard", split_axis=0, concat_axis=0, tiled=True)
    count = shards * neg_ids.shape[1]
    position = np.arange(1, count + 1, dtype=np.float64)
    discount = (1.0 / np.log2(1.0 + position)).astype(np.float32).reshape(-1, LANES)
    grads, loss = pair(packed, jnp.asarray(discount))
    grads = lax.all_to_all(grads, "shard", split_axis=0, concat_axis=0, tiled=True)
    shares = share(grads, idsg, again).reshape(shards, 1, width)
    shares = lax.all_to_all(shares, "shard", split_axis=0, concat_axis=0, tiled=True)
    return refreshed, total(shares), loss[0, :1]


def solution(mesh):
    return jax.shard_map(
        per_device,
        mesh=mesh,
        in_specs=(
            P(("role", "shard"), None),
            P("role", "shard", None),
            P("role", "shard", None),
            P(("role", "shard"), None),
            P(("role", "shard"), None),
            P(("role", "shard"), None),
            P("role", "shard"),
            P("role", "shard"),
        ),
        out_specs=(P(("role", "shard"), None), P(("role", "shard"), None), P(("role", "shard"))),
        check_vma=False,
    )
```

```python
import functools
import math

import jax
import jax.numpy as jnp
import numpy as np
from jax import lax
from jax.experimental import pallas as pl
from jax.experimental.pallas import tpu as pltpu
from jax.sharding import PartitionSpec as P

CAP = 2
EPSILON = 1e-05
LOG_TWO = math.log(2.0)
EMPTY = 1024.0

f32 = jnp.float32
bf16 = jnp.bfloat16
LANES = 128


def params(mebibytes=16):
    return pltpu.CompilerParams(vmem_limit_bytes=mebibytes * 1024 * 1024)


def contract_last(a, b):
    return lax.dot_general(a, b, (((1,), (1,)), ((), ())), preferred_element_type=f32)


def partial_sums(x, w_ref):
    width = x.shape[1]
    inner = contract_last(x, w_ref[:, :width])
    hidden = 0.5 * inner * (1.0 + lax.erf(inner * math.sqrt(0.5)))
    return jnp.dot(hidden.astype(bf16), w_ref[:, width:], preferred_element_type=f32)


def first_kernel(own_ref, across_ref, along_ref, diagonal_ref, w_ref, out_ref):
    for n, x_ref in enumerate((own_ref, across_ref, along_ref, diagonal_ref)):
        out_ref[n] = partial_sums(x_ref[...], w_ref)


def first_half(xs, units):
    return pl.pallas_call(
        first_kernel,
        out_shape=jax.ShapeDtypeStruct((len(xs),) + xs[0].shape, f32),
        compiler_params=params(),
        name="encode",
    )(*xs, units)


def second_kernel(at, *refs):
    x_refs, (w_ref, so_far_ref), out_refs = refs[: len(at)], refs[len(at) :][:2], refs[-len(at) :]
    for n, x_ref, out_ref in zip(at, x_refs, out_refs):
        part = so_far_ref[n] + partial_sums(x_ref[...], w_ref)
        out_ref[...] = part.astype(out_ref.dtype)


def second_half(xs, units, so_far, at, dtype):
    return pl.pallas_call(
        functools.partial(second_kernel, at),
        out_shape=tuple(jax.ShapeDtypeStruct(xs[n].shape, dtype) for n in at),
        compiler_params=params(),
        name="encode_rest",
    )(*(xs[n] for n in at), units, so_far)


ROWS, SUB = 32, 8


def place_kernel(
    cls_ref, own_ref, across_ref, along_ref, diagonal_ref, owner_ref, query_ref, out_ref, placed_s, tiles_s
):
    rows, width = cls_ref.shape
    blocks = owner_ref.shape[1]
    shards = out_ref.shape[0] // SUB
    chunks = width // LANES
    resid = cls_ref[...].astype(f32) + own_ref[...]
    for part_ref in (across_ref, along_ref, diagonal_ref):
        resid = resid + part_ref[...].astype(f32)
    centred = resid - jnp.mean(resid, -1, keepdims=True)
    variance = jnp.mean(centred * centred, -1, keepdims=True)
    fresh = (centred * lax.rsqrt(variance + EPSILON)).astype(bf16)

    owner = owner_ref[...]
    shard_of = lax.broadcasted_iota(jnp.int32, (shards, blocks), 0)
    onehot = (shard_of == owner).astype(f32)
    before = lax.broadcasted_iota(jnp.int32, (blocks, blocks), 0) < lax.broadcasted_iota(
        jnp.int32, (blocks, blocks), 1
    )
    earlier = jnp.dot(onehot.astype(bf16), before.astype(bf16), preferred_element_type=f32)
    slot = jnp.sum(earlier * onehot, 0, keepdims=True)
    passage = lax.broadcasted_iota(jnp.int32, (blocks, rows), 1)
    block = lax.broadcasted_iota(jnp.int32, (blocks, rows), 0)
    widen = (passage // 2 == block).astype(bf16)
    both = jnp.concatenate(
        (jnp.broadcast_to(owner.astype(f32), (8, blocks)), jnp.broadcast_to(slot, (8, blocks))), 0
    )
    both = jnp.dot(both.astype(bf16), widen, preferred_element_type=f32)
    parity = lax.broadcasted_iota(jnp.int32, (1, rows), 1) & 1
    target = both[0:1] * (2.0 * CAP) + both[8:9] * 2.0 + parity.astype(f32)

    row = lax.broadcasted_iota(jnp.int32, (shards * 2 * CAP, rows), 0).astype(f32)
    onto = (row == target).astype(f32)
    filled = jnp.sum(onto, 1, keepdims=True) > 0.5
    placed = jnp.dot(onto.astype(bf16), fresh, preferred_element_type=f32)
    placed = jnp.where(filled, placed, EMPTY)
    for j in range(chunks):
        placed_s[j] = placed[:, j * LANES : (j + 1) * LANES]
        for c in range(2 * CAP):
            r = c * chunks + j
            tiles_s[r // SUB, pl.ds(r % SUB, shards, stride=SUB), :] = placed_s[
                j, pl.ds(c, shards, stride=2 * CAP), :
            ]
    for tile in range(ROWS // SUB):
        if tile < 2 * CAP * chunks // SUB:
            part = tiles_s[tile]
        else:
            part = jnp.broadcast_to(query_ref[...].astype(f32)[None], (shards, SUB, LANES))
            part = part.reshape(shards * SUB, LANES)
        out_ref[:, tile * LANES : (tile + 1) * LANES] = part.astype(bf16)


def place(cls_states, own, across, along, diagonal, owner, query, shards):
    return pl.pallas_call(
        place_kernel,
        out_shape=jax.ShapeDtypeStruct((shards * SUB, ROWS // SUB * LANES), bf16),
        scratch_shapes=[
            pltpu.VMEM((cls_states.shape[1] // LANES, shards * 2 * CAP, LANES), f32),
            pltpu.VMEM((ROWS // SUB - 1, shards * SUB, LANES), f32),
        ],
        compiler_params=params(),
        name="place",
    )(cls_states, own, across, along, diagonal, owner, query)


def score_kernel(
    recv_ref, stale_ref, idsg_ref, refreshed_ref, again_ref, packed_ref, recv_s, arrived_s
):
    cache_rows, width = stale_ref.shape
    shards = recv_ref.shape[0] // SUB
    chunks = width // LANES
    per_shard = cache_rows // shards
    for tile in range(ROWS // SUB):
        recv_s[tile] = recv_ref[:, tile * LANES : (tile + 1) * LANES].astype(f32)

    def arrived_row(r):
        return recv_s[r // SUB, pl.ds(r % SUB, shards, stride=SUB), :]

    queries = []
    for j in range(chunks):
        for c in range(per_shard):
            arrived_s[j, pl.ds(c, shards, stride=per_shard), :] = arrived_row(c * chunks + j)
        queries.append(arrived_row(per_shard * chunks + j))
    queries = jnp.concatenate(queries, 1).astype(bf16)
    arrived = jnp.concatenate([arrived_s[j] for j in range(chunks)], 1)
    refreshed = jnp.where(arrived > 0.5 * EMPTY, stale_ref[...].astype(f32), arrived).astype(bf16)
    refreshed_ref[...] = refreshed
    again_ref[...] = refreshed
    scores = contract_last(queries, refreshed)
    ids = idsg_ref[...]
    lane = lax.broadcasted_iota(jnp.int32, ids.shape, 1)
    low = ids & (LANES - 1)
    picked = jnp.zeros(ids.shape, f32)
    for part in range(cache_rows // LANES):
        here = jnp.take_along_axis(scores[:, part * LANES : (part + 1) * LANES], low, axis=1)
        picked = jnp.where(ids // LANES == part, here, picked)
    packed_ref[...] = jnp.where(lane < LANES // 2, picked, ids.astype(f32))


def score(recv, stale, idsg):
    return pl.pallas_call(
        score_kernel,
        out_shape=(
            jax.ShapeDtypeStruct(stale.shape, bf16),
            jax.ShapeDtypeStruct(stale.shape, bf16),
            jax.ShapeDtypeStruct(idsg.shape, f32),
        ),
        scratch_shapes=[
            pltpu.VMEM((ROWS // SUB, recv.shape[0], LANES), f32),
            pltpu.VMEM((stale.shape[1] // LANES, stale.shape[0], LANES), f32),
        ],
        compiler_params=params(),
        name="score",
    )(recv, stale, idsg)


HALF = LANES // 2


def pair_kernel(
    x_ref, discount_ref, grad_ref, loss_ref, half_s, wide_w, columns, across, spread_s, rows_s, near_q, far_q
):
    x = x_ref[...]
    n_blocks = x.shape[0] // 2
    count = n_blocks * LANES
    top, low = x[:n_blocks], x[n_blocks:]
    lane = lax.broadcasted_iota(jnp.int32, (n_blocks, LANES), 1)
    left = lane < HALF
    scores = jnp.where(left, top, pltpu.roll(low, HALF, 1))
    gains = jnp.exp2(jnp.where(left, pltpu.roll(top, HALF, 1), low))
    position = lax.broadcasted_iota(jnp.int32, (n_blocks, LANES), 0) * LANES + lane

    ordered = jnp.ones((n_blocks, LANES), f32)
    for level in range(1, 5):
        above = jnp.sum((gains > float(2**level) - 0.5).astype(f32))
        ordered = jnp.where(position.astype(f32) < above, float(2**level), ordered)
    ideal = jnp.sum(ordered * discount_ref[...])

    span = n_blocks // 2
    groups = LANES // 8

    def sweep(values, load_or_make):
        columns[...] = jnp.zeros_like(columns)
        values[n_blocks:] = values[:n_blocks]

        def spread(i):
            spread_s[i] = jnp.broadcast_to(values[pl.ds(i, 1), :], (LANES, LANES)).T

        def collect(i):
            across[pl.ds(i, 1), :] = jnp.sum(rows_s[i].T, 0, keepdims=True)

        def block(i, last):
            first = [spread_s[i, pl.ds(8 * g, 8), :] for g in range(groups)]
            collect(i)
            spread(i + 1)
            acc = [jnp.zeros((8, LANES), f32) for _ in range(groups)]
            for d in range(last + 1):
                k = i + d
                kept = near_q.at[i, d] if d < span else far_q.at[i]
                v_k = jnp.broadcast_to(values[pl.ds(k, 1), :], (8, LANES))
                column = [jnp.zeros((8, LANES), f32) for _ in range(4)]
                for g in range(groups):
                    value = load_or_make(first[g], v_k, kept, 8 * g)
                    acc[g] = acc[g] + value
                    column[g % 4] = column[g % 4] + value
                if d > 0:
                    columns[k] = columns[k] + ((column[0] + column[1]) + (column[2] + column[3]))
            for g in range(groups):
                rows_s[i + 1, pl.ds(8 * g, 8), :] = acc[g]
            return 0

        rows_s[0] = jnp.zeros((LANES, LANES), f32)
        spread(0)
        lax.fori_loop(0, span, lambda i, _: block(i, span), 0, unroll=2)
        lax.fori_loop(span, n_blocks, lambda i, _: block(i, span - 1), 0, unroll=2)
        collect(n_blocks)
        folded = jnp.sum(columns[...], 1)
        wrapped = jnp.concatenate((folded[n_blocks:], jnp.zeros((span, LANES), f32)), 0)
        return across[1:] - folded[:n_blocks] - wrapped

    def rank_term(s_i, s_k, kept, at):
        t = jnp.tanh(s_k - s_i)
        kept[pl.ds(at, 8), :] = 1.0 - t * t
        return t

    def cross_term(w_i, w_k, kept, at):
        return (w_k - w_i) * kept[pl.ds(at, 8), :]

    half_s[:n_blocks] = 0.5 * scores
    rank = 0.5 + 0.5 * count + 0.5 * sweep(half_s, rank_term)
    logged = jnp.log2(1.0 + rank)
    weight = gains / (ideal * LOG_TWO * (1.0 + rank) * logged * logged)
    loss_ref[...] = jnp.full((1, LANES), 1.0 - jnp.sum(gains / logged) / ideal, f32)
    wide_w[:n_blocks] = 0.25 * weight
    grad = sweep(wide_w, cross_term).astype(bf16).astype(f32)
    grad_ref[:n_blocks] = grad
    grad_ref[n_blocks:] = pltpu.roll(grad, HALF, 1)


def pair(x, discount):
    n_blocks = x.shape[0] // 2
    span = n_blocks // 2
    return pl.pallas_call(
        pair_kernel,
        out_shape=(
            jax.ShapeDtypeStruct(x.shape, f32),
            jax.ShapeDtypeStruct((1, LANES), f32),
        ),
        scratch_shapes=[
            pltpu.VMEM((2 * n_blocks, LANES), f32),
            pltpu.VMEM((2 * n_blocks, LANES), f32),
            pltpu.VMEM((n_blocks + span, 8, LANES), f32),
            pltpu.VMEM((n_blocks + 1, LANES), f32),
            pltpu.VMEM((n_blocks + 1, LANES, LANES), f32),
            pltpu.VMEM((n_blocks + 1, LANES, LANES), f32),
            pltpu.VMEM((n_blocks, span, LANES, LANES), f32),
            pltpu.VMEM((span, LANES, LANES), f32),
        ],
        compiler_params=params(44),
        name="pair",
    )(x, discount)


def share_kernel(grad_ref, idsg_ref, refreshed_ref, out_ref, rows_w):
    lists, cache_rows = rows_w.shape
    for g in range(lists // 8):
        part = slice(8 * g, 8 * g + 8)
        grads = grad_ref[part, :]
        ids = idsg_ref[part, :]
        spots = [
            lax.broadcasted_iota(jnp.int32, (8, LANES), 1) + LANES * p
            for p in range(cache_rows // LANES)
        ]
        acc = [jnp.zeros((8, LANES), f32) for _ in spots]
        for j in range(HALF):
            id_j = jnp.broadcast_to(ids[:, j : j + 1], (8, LANES))
            grad_j = jnp.broadcast_to(grads[:, j : j + 1], (8, LANES))
            acc = [a + jnp.where(id_j == spot, grad_j, 0.0) for a, spot in zip(acc, spots)]
        for p, a in enumerate(acc):
            rows_w[part, p * LANES : (p + 1) * LANES] = a
    weights = rows_w[...]
    high = weights.astype(bf16)
    rest = (weights - high.astype(f32)).astype(bf16)
    refreshed = refreshed_ref[...]
    out_ref[...] = jnp.dot(high, refreshed, preferred_element_type=f32) + jnp.dot(
        rest, refreshed, preferred_element_type=f32
    )


def share(grads, idsg, refreshed):
    return pl.pallas_call(
        share_kernel,
        out_shape=jax.ShapeDtypeStruct((grads.shape[0], refreshed.shape[1]), f32),
        scratch_shapes=[pltpu.VMEM((grads.shape[0], refreshed.shape[0]), f32)],
        compiler_params=params(),
        name="share",
    )(grads, idsg, refreshed)


def total_kernel(x_ref, out_ref):
    out_ref[...] = jnp.sum(x_ref[...].astype(f32), 0)


def total(x):
    return pl.pallas_call(
        total_kernel,
        out_shape=jax.ShapeDtypeStruct(x.shape[1:], f32),
        compiler_params=params(),
        name="total",
    )(x)


Y, ZZ, ZL, X = 4, 4, 2, 2


def shard_at(y, zz, zl, x):
    return ((y * ZZ + zz) * ZL + zl) * X + x


def everywhere():
    return [
        (y, zz, zl, x) for y in range(Y) for zz in range(ZZ) for zl in range(ZL) for x in range(X)
    ]


def gather_units(block):
    groups = [
        [shard_at(y, zz, zl, x) for y in range(Y) for x in range(X)]
        for zz in range(ZZ)
        for zl in range(ZL)
    ]
    parts = len(groups[0])
    units, width = block.shape
    gathered = lax.all_to_all(
        jnp.broadcast_to(block[None], (parts, units, width)),
        "shard",
        split_axis=0,
        concat_axis=0,
        tiled=True,
        axis_index_groups=groups,
    )
    return gathered.reshape(parts * units, width)


def per_device(
    cls_states, trainer_in, trainer_out, stale_cache, block_owner, queries, neg_ids, grades
):
    shards = lax.axis_size("shard")
    roles = lax.axis_size("role")
    width = cls_states.shape[1]
    barrier = lax.optimization_barrier

    def to_core(v):
        return lax.ppermute(v, "role", [(0, 1), (1, 0), (2, 3), (3, 2)])

    def to_across(v):
        return lax.ppermute(v, "role", [(0, 2), (1, 3), (2, 0), (3, 1)])

    def to_along(v):
        return lax.ppermute(
            v,
            "shard",
            [
                (shard_at(y, zz, zl, x), shard_at(y, zz, 1 - zl, x))
                for y, zz, zl, x in everywhere()
            ],
        )

    def to_diagonal(v):
        return lax.ppermute(
            v,
            ("role", "shard"),
            [
                (r * shards + shard_at(y, zz, zl, x), (r ^ 2) * shards + shard_at(y, zz, 1 - zl, x))
                for r in range(roles)
                for y, zz, zl, x in everywhere()
            ],
        )

    role_of = (0, 2, 1, 3)
    axes = ("role", "shard")
    mine = jnp.concatenate((trainer_in[0], trainer_out[0]), 1)
    mine = lax.ppermute(
        mine,
        axes,
        [
            (
                (roles - 1) * shards + shard_at(y, zz, zl, x),
                role_of[zz] * shards + shard_at(y, zz, zl, x),
            )
            for y, zz, zl, x in everywhere()
        ],
    )
    mine, cls_after = barrier((mine, cls_states))
    block = mine
    for by in range(1, ZZ):
        turn = [
            (
                role_of[zz] * shards + shard_at(y, zz, zl, x),
                role_of[zz] * shards + shard_at(y, (zz + by) % ZZ, zl, x),
            )
            for y, zz, zl, x in everywhere()
        ]
        block = block + lax.ppermute(mine, axes, turn)
    x_across = to_across(cls_after)
    block, x_across, cls_after = barrier((block, x_across, cls_after))
    units = gather_units(block)
    xs = (cls_states, x_across, to_along(cls_after), to_along(x_across))
    query = jnp.pad(queries.reshape(-1, LANES), ((0, SUB - width // LANES), (0, 0)))
    idsg = jnp.concatenate((neg_ids, grades), 1)
    units, xs, query, idsg = barrier((units, xs, query, idsg))
    other_units = to_core(units)
    so_far = first_half(xs, units)
    across, along = second_half(xs, other_units, so_far, (1, 2), bf16)
    from_across = to_across(across)
    from_along = to_along(along)
    (diagonal,) = second_half(xs, other_units, so_far, (3,), bf16)
    from_diagonal = to_diagonal(diagonal)
    (own,) = second_half(xs, other_units, so_far, (0,), f32)
    outgoing = place(
        cls_states,
        own,
        from_across,
        from_along,
        from_diagonal,
        block_owner.reshape(1, -1),
        query,
        shards,
    )
    outgoing, idsg = barrier((outgoing, idsg))
    arrived = lax.all_to_all(
        outgoing.reshape(shards, SUB, -1), "shard", split_axis=0, concat_axis=0, tiled=True
    )
    refreshed, again, packed = score(arrived.reshape(shards * SUB, -1), stale_cache, idsg)
    packed = lax.all_to_all(packed, "shard", split_axis=0, concat_axis=0, tiled=True)
    count = shards * neg_ids.shape[1]
    position = np.arange(1, count + 1, dtype=np.float64)
    discount = (1.0 / np.log2(1.0 + position)).astype(np.float32).reshape(-1, LANES)
    grads, loss = pair(packed, jnp.asarray(discount))
    grads = lax.all_to_all(grads, "shard", split_axis=0, concat_axis=0, tiled=True)
    shares = share(grads, idsg, again).reshape(shards, 1, width)
    shares = lax.all_to_all(shares, "shard", split_axis=0, concat_axis=0, tiled=True)
    return refreshed, total(shares), loss[0, :1]


def solution(mesh):
    return jax.shard_map(
        per_device,
        mesh=mesh,
        in_specs=(
            P(("role", "shard"), None),
            P("role", "shard", None),
            P("role", "shard", None),
            P(("role", "shard"), None),
            P(("role", "shard"), None),
            P(("role", "shard"), None),
            P("role", "shard"),
            P("role", "shard"),
        ),
        out_specs=(P(("role", "shard"), None), P(("role", "shard"), None), P(("role", "shard"))),
        check_vma=False,
    )
```
